128 devices in a mesh: seq: 2 (over x_hi), ctx: 16 (over x_lo, y, core), head: 4 (over z).
Axes of the slice: x: 4 (x_hi: 2, x_lo: 2; x = x_hi * 2 + x_lo), y: 4, z: 4, core: 2. Of those that a mesh axis runs over, the one named last changes fastest.
Arguments:
- block_input: bfloat16 [2, 2, 2048, 1024], P(None, 'seq', 'ctx'), may hold values from -6 to 6
- first_gain: float32 [1024], replicated, may hold values from 0.1 to 1.9
- first_shift: float32 [1024], replicated, may hold values from -3 to 3
- query_weight: bfloat16 [1024, 1024], P(('seq', 'ctx'), 'head'), may hold values from -0.1875 to 0.1875
- query_bias: float32 [1024], P('head'), may hold values from -3 to 3
- key_weight: bfloat16 [1024, 1024], P(('seq', 'ctx'), 'head'), may hold values from -1 to 1
- value_weight: bfloat16 [1024, 1024], P(('seq', 'ctx'), 'head'), may hold values from -0.1875 to 0.1875
- value_bias: float32 [1024], P('head'), may hold values from -3 to 3
- output_weight: bfloat16 [1024, 1024], P(('seq', 'ctx'), 'head'), may hold values from -0.5 to 0.5
- output_bias: float32 [1024], replicated, may hold values from -3 to 3
- second_gain: float32 [1024], replicated, may hold values from 0.1 to 1.9
- second_shift: float32 [1024], replicated, may hold values from -3 to 3
- up_weight: bfloat16 [1024, 4096], P(('seq', 'ctx'), 'head'), may hold values from -0.1875 to 0.1875
- up_bias: float32 [4096], P('head'), may hold values from -3 to 3
- down_weight: bfloat16 [1024, 4096], P(('seq', 'ctx'), 'head'), may hold values from -0.09375 to 0.09375
- down_bias: float32 [1024], replicated, may hold values from -3 to 3
- segments: int32 [2, 2, 2048], P(None, 'seq', 'ctx'), may hold values from 0 to 3, as said below
- out_cotangent: bfloat16 [2, 2, 2048, 1024], P(None, 'seq', 'ctx'), may hold values from -6 to 6
Outputs:
- block_output: float32 [2, 2, 2048, 1024], P(None, 'seq', 'ctx')
- input_grad: float32 [2, 2, 2048, 1024], P(None, 'seq', 'ctx')
- first_gain_grad: float32 [1024], replicated
- first_shift_grad: float32 [1024], replicated
- query_weight_grad: float32 [1024, 1024], P(('seq', 'ctx'), 'head')
- query_bias_grad: float32 [1024], P('head')
- key_weight_grad: float32 [1024, 1024], P(('seq', 'ctx'), 'head')
- value_weight_grad: float32 [1024, 1024], P(('seq', 'ctx'), 'head')
- value_bias_grad: float32 [1024], P('head')
- output_weight_grad: float32 [1024, 1024], P(('seq', 'ctx'), 'head')
- output_bias_grad: float32 [1024], replicated
- second_gain_grad: float32 [1024], replicated
- second_shift_grad: float32 [1024], replicated
- up_weight_grad: float32 [1024, 4096], P(('seq', 'ctx'), 'head')
- up_bias_grad: float32 [4096], P('head')
- down_weight_grad: float32 [1024, 4096], P(('seq', 'ctx'), 'head')
- down_bias_grad: float32 [1024], replicated
The draws below stay inside these ranges and needn't reach their ends.
Inputs may be any that keep to these rules, and one draw needn't show every extreme that they name: `segments`: along each sequence the numbers never fall. For each of the 2 sequence slots, one of the 2 micro-batches, chosen at random, holds a single document (all zeros); the others hold up to four documents of random lengths and end with number 3.
All inputs are finite; a program needn't handle non-finite values.
Results may differ from the reference program's by a relative error of at most 0.012.
The reference program's roundings to bfloat16 on the way count: a program that leaves them out, or rounds other values in their place, can miss the bound.
Values may be sent and summed in bfloat16 or wider, within the bound.
A program may use at most 128 MiB of HBM per device.

```python
import math
import jax
import jax.numpy as jnp
from jax import lax

D = 1024
FF = 4096
HEADS = 16
HEAD_DIM = 64
MB = 2
SEQS = 2
LEN = 2048


def shared_plan(key):
    sign_key, offset_key = jax.random.split(key)
    direction = jnp.where(jax.random.bernoulli(sign_key, 0.5, (D,)), 1.0, -1.0).astype(jnp.float32)
    offsets = jnp.clip(0.5 * jax.random.normal(offset_key, (D,), jnp.float32), -3.0, 3.0)
    return (direction, offsets)


def draw_query_bias(key, part):
    direction, offsets = shared_plan(key)
    return offsets


def draw_key_weight(key, part):
    direction, offsets = shared_plan(key)
    key = jax.random.fold_in(key, 11)
    random_part = jnp.clip(jax.random.normal(key, (D, D), jnp.float32), -6.0, 6.0) / math.sqrt(D)
    columns = jnp.arange(D)
    slow_heads = (columns // HEAD_DIM >= HEADS - HEADS // 4).astype(jnp.float32)
    signs = jnp.where(offsets >= 0.0, 1.0, -1.0).astype(jnp.float32)
    strength = 50.0 / (D * math.sqrt(HEAD_DIM))
    planted = strength * direction[:, None] * (signs * slow_heads)[None, :]
    return jnp.clip(random_part + planted, -1.0, 1.0).astype(jnp.bfloat16)


def draw_block_input(key, part):
    direction, offsets = shared_plan(key)
    key = jax.random.fold_in(key, 5)
    normal_key, place_key = jax.random.split(key)
    normal_part = jnp.clip(jax.random.normal(normal_key, (MB, SEQS, LEN, D), jnp.float32), -6.0, 6.0)
    chosen = jax.random.randint(place_key, (MB, SEQS, 2), LEN // 16, LEN // 2)
    places = jnp.arange(LEN)
    marked = jnp.any(places[None, None, :, None] == chosen[:, :, None, :], axis=-1)
    planted = direction[None, None, None, :] + 0.3 * normal_part
    return jnp.clip(jnp.where(marked[:, :, :, None], planted, normal_part), -6.0, 6.0).astype(jnp.bfloat16)


def draw_segments(key, part):
    key = jax.random.fold_in(key, 7)
    pick_key, cut_key = jax.random.split(key)
    whole = jax.random.randint(pick_key, (SEQS,), 0, MB)
    cuts = jax.random.randint(cut_key, (MB, SEQS, 3), 1, LEN)
    places = jnp.arange(LEN)
    numbers = jnp.sum((places[None, None, :, None] >= cuts[:, :, None, :]).astype(jnp.int32), axis=-1)
    single = jnp.arange(MB)[:, None] == whole[None, :]
    return jnp.where(single[:, :, None], 0, numbers).astype(jnp.int32)


def block_levels(key, shape, cuts, smallest, top_value):
    def one(position, parts):
        draws = jax.random.uniform(jax.random.fold_in(jax.random.fold_in(key, 6), position), (parts,), jnp.float32, smallest / len(cuts), top_value / len(cuts))
        return jnp.repeat(jnp.exp(draws), shape[position] // parts).reshape((-1,) + (1,) * (len(shape) - position - 1))

    factor_of = one(*cuts[0])
    for cut in cuts[1:]:
        factor_of = factor_of * one(*cut)
    return factor_of


def scatter_about(own_key, extent, scale, limit, shards=(), kind=jnp.bfloat16):
    values = scale * jax.random.normal(own_key, extent, jnp.float32)
    if shards:
        values = values * block_levels(own_key, extent, shards, -0.22, 0.18)
    return jnp.clip(values, -limit, limit).astype(kind)


def setup_inputs(seed: int = 0) -> dict:
    seeds = jax.random.split(jax.random.key(seed), 19)
    block_input = draw_block_input(jax.random.fold_in(seeds[18], 71), 0)
    first_gain = jnp.clip(1.0 + 0.18 * jax.random.normal(seeds[1], (D,), jnp.float32), 0.1, 1.9)
    first_shift = scatter_about(seeds[2], (D,), 0.5, 3.0, (), jnp.float32)
    query_weight = scatter_about(seeds[3], (D, D), D ** -0.5, 0.1875, ((0, 32), (1, 4)))
    query_bias = draw_query_bias(jax.random.fold_in(seeds[18], 71), 0)
    key_weight = draw_key_weight(jax.random.fold_in(seeds[18], 71), 0)
    value_weight = scatter_about(seeds[6], (D, D), D ** -0.5, 0.1875, ((0, 32), (1, 4)))
    value_bias = scatter_about(seeds[7], (D,), 0.5, 3.0, ((0, 4),), jnp.float32)
    output_weight = scatter_about(seeds[8], (D, D), (D // 8) ** -0.5, 0.5, ((0, 32), (1, 4)))
    output_bias = scatter_about(seeds[9], (D,), 0.5, 3.0, (), jnp.float32)
    second_gain = jnp.clip(1.0 + 0.18 * jax.random.normal(seeds[10], (D,), jnp.float32), 0.1, 1.9)
    second_shift = scatter_about(seeds[11], (D,), 0.5, 3.0, (), jnp.float32)
    up_weight = scatter_about(seeds[12], (D, FF), D ** -0.5, 0.1875, ((0, 32), (1, 4)))
    up_bias = scatter_about(seeds[13], (FF,), 0.5, 3.0, ((0, 4),), jnp.float32)
    down_weight = scatter_about(seeds[14], (D, FF), FF ** -0.5, 0.09375, ((0, 32), (1, 4)))
    down_bias = scatter_about(seeds[15], (D,), 0.5, 3.0, (), jnp.float32)
    segments = draw_segments(jax.random.fold_in(seeds[18], 71), 0)
    out_cotangent = scatter_about(seeds[17], (MB, SEQS, LEN, D), 1.0, 6.0, ((1, 2), (2, 16)))
    return {"block_input": block_input, "first_gain": first_gain, "first_shift": first_shift, "query_weight": query_weight, "query_bias": query_bias, "key_weight": key_weight, "value_weight": value_weight, "value_bias": value_bias, "output_weight": output_weight, "output_bias": output_bias, "second_gain": second_gain, "second_shift": second_shift, "up_weight": up_weight, "up_bias": up_bias, "down_weight": down_weight, "down_bias": down_bias, "segments": segments, "out_cotangent": out_cotangent}


@jax.custom_vjp
def low(v):
    return lax.optimization_barrier(v.astype(jnp.bfloat16)).astype(jnp.float32)

@jax.custom_vjp
def low_back(v):
    return v

def low_keep(v):
    return (low(v), None)

def low_pass(kept, grad):
    return (grad,)

def back_keep(v):
    return (v, None)

def back_low(kept, grad):
    return (low(grad),)
low.defvjp(low_keep, low_pass)
low_back.defvjp(back_keep, back_low)
HIGH = lax.Precision.HIGHEST

def layer_norm(value, gain, shift):
    center = value - lax.optimization_barrier(jnp.mean(value, axis=-1, keepdims=True))
    spread = lax.optimization_barrier(jnp.mean(center * center, axis=-1, keepdims=True))
    return center * lax.rsqrt(spread + 1e-05) * gain + shift

def gelu_tanh(value):
    return 0.5 * value * (1.0 + jnp.tanh(0.7978845608028654 * (value + 0.044715 * value * value * value)))

def matmul(left, right):
    return jnp.dot(left, right, precision=HIGH)

def attend(query, keys, values, seg):
    heads_q = query.reshape(LEN, HEADS, HEAD_DIM)
    heads_k = keys.reshape(LEN, HEADS, HEAD_DIM)
    heads_v = values.reshape(LEN, HEADS, HEAD_DIM)
    block = math.gcd(LEN, 512)
    scale = 1.0 / math.sqrt(HEAD_DIM)
    slopes = jnp.exp2(-8.0 * (jnp.arange(HEADS) + 1).astype(jnp.float32) / HEADS)
    places = jnp.arange(LEN).astype(jnp.int32)

    def one_block(start):
        rows_q = lax.dynamic_slice_in_dim(heads_q, start, block, 0)
        seg_q = lax.dynamic_slice_in_dim(seg, start, block, 0)
        index = start + jnp.arange(block).astype(jnp.int32)
        raw = jnp.einsum('qhd,khd->hqk', rows_q, heads_k, precision=HIGH) * scale
        dist = (index[:, None] - places[None, :]).astype(jnp.float32)
        raw = low_back(raw - slopes[:, None, None] * dist[None])
        allowed = (seg_q[:, None] == seg[None, :]) & (places[None, :] <= index[:, None])
        raw = jnp.where(allowed[None], raw, -1000000000.0)
        top = lax.optimization_barrier(jnp.max(raw, axis=-1, keepdims=True))
        expo = jnp.exp(raw - top)
        probs = expo / lax.optimization_barrier(jnp.sum(expo, axis=-1, keepdims=True))
        out = jnp.einsum('hqk,khd->qhd', low(probs), heads_v, precision=HIGH)
        return out.reshape(block, HEADS * HEAD_DIM)
    starts = (jnp.arange(LEN // block) * block).astype(jnp.int32)
    return lax.map(jax.checkpoint(one_block), starts).reshape(LEN, HEADS * HEAD_DIM)

def forward(params, inputs, seg):
    first_gain, first_shift, query_weight, query_bias, key_weight, value_weight, value_bias, output_weight, output_bias, second_gain, second_shift, up_weight, up_bias, down_weight, down_bias = params
    normed = low(layer_norm(inputs, first_gain, first_shift))
    query = low(low_back(matmul(normed, query_weight) + query_bias))
    keys = low(low_back(matmul(normed, key_weight)))
    values = low(low_back(matmul(normed, value_weight) + value_bias))
    mixed = low(low_back(attend(query, keys, values, seg)))
    middle = inputs + low_back(matmul(mixed, output_weight.T)) + output_bias
    second = low(layer_norm(middle, second_gain, second_shift))
    hidden = low_back(matmul(second, up_weight) + up_bias)
    active = low(gelu_tanh(hidden))
    return middle + low_back(matmul(active, down_weight.T)) + down_bias

def reference(block_input, first_gain, first_shift, query_weight, query_bias, key_weight, value_weight, value_bias, output_weight, output_bias, second_gain, second_shift, up_weight, up_bias, down_weight, down_bias, segments, out_cotangent):
    params = tuple((p.astype(jnp.float32) for p in (first_gain, first_shift, query_weight, query_bias, key_weight, value_weight, value_bias, output_weight, output_bias, second_gain, second_shift, up_weight, up_bias, down_weight, down_bias)))
    count = MB * SEQS
    inputs = block_input.astype(jnp.float32).reshape(count, LEN, D)
    cotan = out_cotangent.astype(jnp.float32).reshape(count, LEN, D)
    segs = segments.reshape(count, LEN).astype(jnp.int32)

    def one_sequence(totals, item):
        xs, seg, dy = item
        result, pull = jax.vjp(lambda p, v: forward(p, v, seg), params, xs)
        grads, dx = pull(dy)
        return (jax.tree.map(lambda a, b: a + b, totals, grads), (result, dx))
    zeros = jax.tree.map(jnp.zeros_like, params)
    totals, (outputs, dxs) = lax.scan(one_sequence, zeros, (inputs, segs, cotan))
    shape = (MB, SEQS, LEN, D)
    return (outputs.reshape(shape), dxs.reshape(shape)) + tuple(totals)
```

```python
import functools

import jax
import jax.numpy as jnp
from jax import lax
from jax.experimental import pallas as pl
from jax.experimental.pallas import tpu as pltpu
from jax.sharding import PartitionSpec as P

F32 = jnp.float32
BF16 = jnp.bfloat16
MESH = pl.DeviceIdType.MESH
VMEM_BYTES = 56 * 1024 * 1024
KEYS = 512


def dot(left, right, dim_left, dim_right):
    return lax.dot_general(
        left, right, (((dim_left,), (dim_right,)), ((), ())), preferred_element_type=F32
    )


def turn(index, by):
    return lax.rem(index + by, 4)


class Place:
    def __init__(self):
        self.seq = lax.axis_index("seq")
        self.ctx = lax.axis_index("ctx")
        self.z = lax.axis_index("head")
        self.core = lax.rem(self.ctx, 2)
        self.y = lax.rem(lax.div(self.ctx, 2), 4)
        self.low = lax.div(self.ctx, 8)
        self.x = self.seq * 2 + self.low
        self.x_plus = self.at(turn(self.x, 1), self.y, self.core, self.z)
        self.x_minus = self.at(turn(self.x, 3), self.y, self.core, self.z)
        self.y_plus = self.at(self.x, turn(self.y, 1), self.core, self.z)
        self.y_minus = self.at(self.x, turn(self.y, 3), self.core, self.z)
        self.z_plus = self.at(self.x, self.y, self.core, turn(self.z, 1))
        self.z_minus = self.at(self.x, self.y, self.core, turn(self.z, 3))
        self.sibling = self.at(self.x, self.y, 1 - self.core, self.z)
        self.pair = self.at(self.seq * 2 + 1 - self.low, self.y, self.core, self.z)

    def at(self, x, y, core, z):
        return (lax.div(x, 2), (lax.rem(x, 2) * 4 + y) * 2 + core, z)

    def greet(self, partners):
        barrier = pltpu.get_barrier_semaphore()
        for partner in partners:
            pl.semaphore_signal(barrier, inc=1, device_id=partner, device_id_type=MESH)
        pl.semaphore_wait(barrier, len(partners))


class Net:
    def __init__(self, send, recv):
        self.send, self.recv, self.used = send, recv, 0

    def copy(self, src, dst, device):
        index = self.used
        self.used += 1
        made = pltpu.make_async_remote_copy(
            src_ref=src,
            dst_ref=dst,
            send_sem=self.send.at[index],
            recv_sem=self.recv.at[index],
            device_id=device,
            device_id_type=MESH,
        )
        made.start()
        return made


def run(steps):
    for _ in steps:
        pass


def gather4(net, region, here, plus, minus, halves=True):
    own = region(here, None)
    one = net.copy(own, own, plus)
    two = net.copy(own, own, minus)
    yield
    first = 0 if halves else None
    one.wait_recv()
    far = region(turn(here, 3), first)
    done = [one, two, net.copy(far, far, plus)]
    two.wait_recv()
    if halves:
        far = region(turn(here, 1), 1)
        done.append(net.copy(far, far, minus))
    yield
    for copy in done[2:]:
        copy.wait_recv()
    for copy in done:
        copy.wait_send()


def add_into(view, other):
    view[...] = (view[...].astype(F32) + other[...].astype(F32)).astype(BF16)


def scatter4(net, part, relay, from_minus, from_plus, here, plus, minus):
    after, before, across = turn(here, 1), turn(here, 3), turn(here, 2)
    out = net.copy(part(across, 0), relay(0), plus)
    back = net.copy(part(across, 1), relay(1), minus)
    early_out = net.copy(part(after, 1), from_minus(1), plus)
    early_back = net.copy(part(before, 0), from_plus(0), minus)
    yield
    out.wait_recv()
    add_into(part(after, 0), relay(0))
    late_out = net.copy(part(after, 0), from_minus(0), plus)
    back.wait_recv()
    add_into(part(before, 1), relay(1))
    late_back = net.copy(part(before, 1), from_plus(1), minus)
    yield
    for copy in (early_out, early_back, late_out, late_back):
        copy.wait_recv()
    for copy in (out, back, early_out, early_back, late_out, late_back):
        copy.wait_send()


def gather_plane(net, at, full):
    half = full.shape[4] // 2

    def cut(index):
        return slice(None) if index is None else slice(index * half, (index + 1) * half)

    def two(index):
        return slice(None) if index is None else slice(index * 2, index * 2 + 2)

    top, low = slice(0, 16), slice(16, 32)
    x, y, core = at.x, at.y, at.core
    done = []

    def share(view):
        done.append(net.copy(view, view, at.sibling))

    a = gather4(net, lambda j, h: full.at[j, y, core, top, cut(h)], x, at.x_plus, at.x_minus)
    b = gather4(net, lambda j, h: full.at[x, j, core, low, cut(h)], y, at.y_plus, at.y_minus)
    next(a)
    next(b)
    yield
    next(a)
    next(b)
    yield
    run(a)
    a = gather4(net, lambda j, h: full.at[two(h), j, core, top, :], y, at.y_plus, at.y_minus)
    next(a)
    share(full.at[:, y, core, top, :])
    run(b)
    b = gather4(net, lambda j, h: full.at[j, two(h), core, low, :], x, at.x_plus, at.x_minus)
    next(b)
    share(full.at[x, :, core, low, :])
    yield
    next(a)
    share(full.at[:, turn(y, 1), core, top, :])
    share(full.at[:, turn(y, 3), core, top, :])
    next(b)
    share(full.at[turn(x, 1), :, core, low, :])
    share(full.at[turn(x, 3), :, core, low, :])
    yield
    run(a)
    share(full.at[:, turn(y, 2), core, top, :])
    run(b)
    share(full.at[turn(x, 2), :, core, low, :])
    for copy in done:
        copy.wait()


def scatter_plane(net, at, partial, other, total, rings, result):
    half = total.shape[3] // 2

    def cut(index):
        return slice(index * half, (index + 1) * half)

    def two(index):
        return slice(index * 2, index * 2 + 2)

    top, low = slice(0, 16), slice(16, 32)
    x, y, core = at.x, at.y, at.core
    shared = net.copy(partial.at[:, :, 1 - core], other, at.sibling)
    yield
    shared.wait()

    def add(index, carry):
        i, j = lax.div(index, 4), lax.rem(index, 4)
        total[i, j] = (partial[i, j, core].astype(F32) + other[i, j].astype(F32)).astype(BF16)
        return carry

    lax.fori_loop(0, 16, add, 0)
    wide_a, wide_b, thin_a, thin_b = rings

    def slots(buffer, kind):
        return lambda h: buffer.at[kind, h]

    a = scatter4(
        net, lambda j, h: total.at[two(h), j, top, :],
        slots(wide_a, 0), slots(wide_a, 1), slots(wide_a, 2), y, at.y_plus, at.y_minus,
    )
    b = scatter4(
        net, lambda j, h: total.at[j, two(h), low, :],
        slots(wide_b, 0), slots(wide_b, 1), slots(wide_b, 2), x, at.x_plus, at.x_minus,
    )
    next(a)
    next(b)
    yield
    next(a)
    next(b)
    yield
    run(a)
    for h in range(2):
        view = total.at[two(h), y, top, :]
        view[...] = (
            view[...].astype(F32) + wide_a[1, h].astype(F32) + wide_a[2, h].astype(F32)
        ).astype(BF16)
    a = scatter4(
        net, lambda j, h: total.at[j, y, top, cut(h)],
        slots(thin_a, 0), slots(thin_a, 1), slots(thin_a, 2), x, at.x_plus, at.x_minus,
    )
    next(a)
    run(b)
    for h in range(2):
        view = total.at[x, two(h), low, :]
        view[...] = (
            view[...].astype(F32) + wide_b[1, h].astype(F32) + wide_b[2, h].astype(F32)
        ).astype(BF16)
    b = scatter4(
        net, lambda j, h: total.at[x, j, low, cut(h)],
        slots(thin_b, 0), slots(thin_b, 1), slots(thin_b, 2), y, at.y_plus, at.y_minus,
    )
    next(b)
    yield
    next(a)
    next(b)
    yield
    for steps, rows, thin in ((a, top, thin_a), (b, low, thin_b)):
        run(steps)
        extra = thin[1].astype(F32) + thin[2].astype(F32)
        extra = jnp.concatenate([extra[0], extra[1]], axis=1)
        result(rows, total[x, y, rows, :].astype(F32) + extra)


def plane_scratch(width):
    return [
        pltpu.VMEM((4, 4, 32, width), BF16),
        pltpu.VMEM((4, 4, 32, width), BF16),
        pltpu.VMEM((3, 2, 2, 16, width), BF16),
        pltpu.VMEM((3, 2, 2, 16, width), BF16),
        pltpu.VMEM((3, 2, 16, width // 2), BF16),
        pltpu.VMEM((3, 2, 16, width // 2), BF16),
    ]


def norm_parts(value):
    center = value - jnp.mean(value, axis=-1, keepdims=True)
    rate = lax.rsqrt(jnp.mean(center * center, axis=-1, keepdims=True) + 1e-05)
    return center * rate, rate


def norm_back(grad, unit, rate, gain):
    inner = grad * gain
    even = jnp.mean(inner, axis=-1, keepdims=True)
    along = jnp.mean(inner * unit, axis=-1, keepdims=True)
    return rate * (inner - even - unit * along)


def column_sum(value):
    return jnp.sum(value, axis=0, keepdims=True)


def split_heads(pair):
    wide = pair.astype(F32)
    lane = lax.broadcasted_iota(jnp.int32, wide.shape, 1)
    both = [jnp.where(lane < 64, wide, 0.0), jnp.where(lane >= 64, wide, 0.0)]
    return jnp.concatenate(both, axis=0).astype(BF16)


def join_heads(wide):
    return jnp.concatenate([wide[0:64, 0:128], wide[64:128, 128:256]], axis=0).T


def slope_row(at, pair):
    first = jnp.where(
        at.z == 0, 1.0, jnp.where(at.z == 1, 0.25, jnp.where(at.z == 2, 0.0625, 0.015625))
    ).astype(F32)
    lane = lax.broadcasted_iota(jnp.int32, (1, 256), 1)
    even = 2.0 ** (-(2 * pair + 1) / 2.0)
    odd = 2.0 ** (-(2 * pair + 2) / 2.0)
    return first * jnp.where(lane < 128, even, odd).astype(F32)


def fill_distance(at, dist, start):
    def fill(block, carry):
        first = block * 256
        lane = lax.broadcasted_iota(jnp.int32, (256, 128), 1)
        query = (lane + at.ctx * 128).astype(F32)
        key = (lax.broadcasted_iota(jnp.int32, (256, 128), 0) + first).astype(F32)
        apart = query - key
        value = jnp.where((key >= start) & (apart >= 0.0), apart, -1.0)
        dist[pl.ds(pl.multiple_of(first, 256), 256), 0:128] = value
        dist[pl.ds(pl.multiple_of(first, 256), 256), 128:256] = value
        return carry

    lax.fori_loop(0, 8, fill, 0)


def masked_scores(keys, queries, dist, slope):
    raw = dot(keys, queries, 1, 1) * 0.125
    return jnp.where(dist >= 0.0, raw - slope * dist, -1000000000.0)


def key_block(kv, micro, block, first):
    low, y = block // 2, (block % 2) * 2
    return kv[micro, low, y : y + 2, :, :, first : first + 128].reshape(KEYS, 128)


def first_kernel(
    x_ref, gain_ref, shift_ref, wq_ref, wk_ref, wv_ref, wo_ref, wu_ref, wd_ref, qb_ref, vb_ref, seg_ref,
    h1_ref, q_ref, kv_ref, w1_ref, w2_ref, o_ref, lse_ref, start_ref,
    seg_all, dist, score, send, recv,
):
    at = Place()
    net = Net(send, recv)
    at.greet((at.x_plus, at.x_minus, at.y_plus, at.y_minus, at.sibling))
    x, y, core, low = at.x, at.y, at.core, at.low
    mine = w1_ref.at[x, y, core]
    mine[:, 0:256] = wq_ref[...]
    mine[:, 256:512] = wk_ref[...]
    mine[:, 512:768] = wv_ref[...]
    w1 = gather_plane(net, at, w1_ref)
    next(w1)
    mine = w2_ref.at[x, y, core]
    mine[:, 0:256] = wo_ref[...]
    mine[:, 256:1280] = wu_ref[...]
    mine[:, 1280:2304] = wd_ref[...]
    seg_all[low, y, core] = jnp.concatenate([seg_ref[...], seg_ref[...], seg_ref[...], seg_ref[...]], axis=0)
    seg = gather4(
        net, lambda j, h: seg_all.at[low, j, core], y, at.y_plus, at.y_minus, halves=False
    )
    next(seg)
    unit, _ = norm_parts(x_ref[...].astype(F32))
    h1_ref[...] = (unit * gain_ref[...] + shift_ref[...]).astype(BF16)
    next(w1)
    next(seg)
    next(w1)
    run(seg)
    view = seg_all.at[low, :, core]
    seg_pair = net.copy(view, view, at.pair)
    next(w1)
    seg_pair.wait()
    view = seg_all.at[:, :, core]
    seg_share = net.copy(view, view, at.sibling)
    run(w1)
    w2 = gather_plane(net, at, w2_ref)
    next(w2)
    h1 = h1_ref[...]
    kv_wide = dot(h1, w1_ref[:, :, :, :, 256:768].reshape(1024, 512), 1, 0)
    kv_ref[0, low, y, core, :, 0:256] = kv_wide[0:128, 0:256].astype(BF16)
    kv_ref[1, low, y, core, :, 0:256] = kv_wide[128:256, 0:256].astype(BF16)
    values = (kv_wide[:, 256:512] + vb_ref[...]).astype(BF16)
    kv_ref[0, low, y, core, :, 256:512] = values[0:128]
    kv_ref[1, low, y, core, :, 256:512] = values[128:256]
    own = kv_ref.at[0, low, y, core]
    a_pair = net.copy(own, own, at.pair)
    b = gather4(
        net,
        lambda j, h: kv_ref.at[
            1, low, j, core, slice(None) if h is None else slice(h * 64, h * 64 + 64)
        ],
        y, at.y_plus, at.y_minus,
    )
    next(b)
    q_ref[...] = (dot(h1, w1_ref[:, :, :, :, 0:256].reshape(1024, 256), 1, 0) + qb_ref[...]).astype(BF16)
    a_pair.wait()
    a = gather4(
        net,
        lambda j, h: kv_ref.at[0, slice(None) if h is None else h, j, core],
        y, at.y_plus, at.y_minus,
    )
    next(a)
    done = []

    def share(view):
        done.append(net.copy(view, view, at.sibling))

    share(kv_ref.at[0, :, y, core])
    next(b)
    seg_share.wait()
    row = lax.broadcasted_iota(jnp.int32, (2, 128), 0)
    found = jnp.zeros((2, 128), F32)
    for number in range(1, 4):
        below = (seg_all[:, :, :, 0:2, :] < number).astype(F32)
        below = jnp.sum(below.reshape(16, 2, 128), axis=0)
        below = jnp.sum(below, axis=-1, keepdims=True)
        found = jnp.where(seg_ref[...] == number, below, found)
    start_ref[...] = found
    fill_distance(at, dist, found[0:1])
    next(a)
    share(kv_ref.at[0, :, turn(y, 1), core])
    share(kv_ref.at[0, :, turn(y, 3), core])
    run(b)
    b_view = kv_ref.at[1, low, :, core]
    b_pair = net.copy(b_view, b_view, at.pair)
    share(b_view)
    next(w2)
    run(a)
    share(kv_ref.at[0, :, turn(y, 2), core])
    next(w2)
    for index in (0, 1, 2, 4):
        done[index].wait()
    b_done = done[3]
    for micro in range(2):
        if micro == 1:
            fill_distance(at, dist, found[1:2])
            b_pair.wait()
            view = kv_ref.at[1, 1 - low, :, core]
            last = net.copy(view, view, at.sibling)
            b_done.wait()
            last.wait()
        for pair in range(2):
            lanes = slice(pair * 128, pair * 128 + 128)
            queries = split_heads(q_ref[micro * 128 : micro * 128 + 128, lanes])
            slope = slope_row(at, pair)
            top = jnp.full((1, 256), -3.0e38, F32)
            for block in range(2048 // KEYS):
                rows = slice(block * KEYS, block * KEYS + KEYS)
                part = masked_scores(
                    key_block(kv_ref, micro, block, pair * 128), queries, dist[rows, :], slope
                )
                score[rows, :] = part
                top = jnp.maximum(top, jnp.max(part, axis=0, keepdims=True))
            summed = jnp.zeros((1, 256), F32)
            for block in range(2048 // KEYS):
                rows = slice(block * KEYS, block * KEYS + KEYS)
                part = jnp.exp(score[rows, :] - top)
                score[rows, :] = part
                summed = summed + column_sum(part)
            scale = 1.0 / summed
            mixed = jnp.zeros((128, 256), F32)
            for block in range(2048 // KEYS):
                rows = slice(block * KEYS, block * KEYS + KEYS)
                probs = (score[rows, :] * scale).astype(BF16)
                mixed = mixed + dot(key_block(kv_ref, micro, block, 256 + pair * 128), probs, 0, 0)
            o_ref[micro * 128 : micro * 128 + 128, lanes] = join_heads(mixed).astype(BF16)
            lse_ref[micro * 2 + pair : micro * 2 + pair + 1, :] = top + jnp.log(summed)
            if micro == 0:
                next(w2, None)
    run(w2)


def second_kernel(
    x_ref, dy_ref, o_ref, w2_ref, ob_ref, gain_ref, shift_ref, ub_ref, db_ref,
    bo_ref, dx1_ref, do_ref, dw_ref, small_ref, dub_ref,
    part, relay, minus, plus, gathered, slope, dg, g_ref, send, recv,
):
    at = Place()
    net = Net(send, recv)
    z = at.z
    at.greet((at.z_plus, at.z_minus))

    def scatter(index, value):
        part[index] = value.astype(BF16).reshape(4, 64, 1024)
        return scatter4(
            net,
            lambda j, h: part.at[index, j, h * 32 : h * 32 + 32, :],
            lambda h: relay.at[index, h],
            lambda h: minus.at[index, h],
            lambda h: plus.at[index, h],
            z, at.z_plus, at.z_minus,
        )

    def gather(buffer):
        return gather4(
            net,
            lambda j, h: buffer.at[j] if h is None else buffer.at[j, h * 32 : h * 32 + 32, :],
            z, at.z_plus, at.z_minus,
        )

    def owned(index):
        extra = minus[index].astype(F32) + plus[index].astype(F32)
        return part[index, z].astype(F32) + extra.reshape(64, 1024)

    def weight(first, width):
        return w2_ref[:, :, :, :, first : first + width].reshape(1024, width)

    def put_grad(first, width, left, right):
        for i in range(4):
            value = dot(left(i), right, 0, 0).astype(BF16)
            dw_ref[i, :, :, :, first : first + width] = value.reshape(4, 2, 32, width)

    mixed = o_ref[...]
    steps = scatter(0, dot(mixed, weight(0, 256), 1, 1))
    next(steps)
    dyl = dy_ref[...].reshape(256, 1024)
    dg[:, 0:512] = dot(dyl, weight(1280, 512), 1, 0)
    next(steps)
    dg[:, 512:1024] = dot(dyl, weight(1792, 512), 1, 0)
    run(steps)
    x1 = x_ref[z].astype(F32) + owned(0) + ob_ref[...]
    unit, rate = norm_parts(x1)
    gathered[0, z] = (unit * gain_ref[...] + shift_ref[...]).astype(BF16)
    steps = gather(gathered.at[0])
    next(steps)
    upstream = dy_ref[z].astype(F32)
    small_ref[...] = jnp.zeros((8, 1024), F32)
    small_ref[5:6, :] = column_sum(upstream)
    next(steps)
    run(steps)
    h2 = gathered[0].reshape(256, 1024)
    for i in range(2):
        cols = slice(i * 512, i * 512 + 512)
        u = dot(h2, weight(256 + i * 512, 512), 1, 0) + ub_ref[:, cols]
        tanh = jnp.tanh(0.7978845608028654 * (u + 0.044715 * u * u * u))
        g_ref[:, cols] = (0.5 * u * (1.0 + tanh)).astype(BF16)
        turned = 0.5 * u * (1.0 - tanh * tanh) * 0.7978845608028654 * (1.0 + 3 * 0.044715 * u * u)
        slope[:, cols] = (dg[:, cols] * (0.5 * (1.0 + tanh) + turned)).astype(BF16)
    du = slope[...]
    back = scatter(2, dot(du, weight(256, 1024), 1, 1))
    next(back)
    front = scatter(1, dot(g_ref[...], weight(1280, 1024), 1, 1))
    next(front)
    dub_ref[...] = column_sum(du.astype(F32))
    next(back)
    put_grad(1280, 1024, lambda i: dy_ref[:, :, i * 256 : i * 256 + 256].reshape(256, 256), g_ref[...])
    run(back)
    dh2 = owned(2)
    small_ref[3:4, :] = column_sum(dh2 * unit)
    small_ref[4:5, :] = column_sum(dh2)
    dx1 = upstream + norm_back(dh2, unit, rate, gain_ref[...])
    dx1_ref[...] = dx1
    small_ref[2:3, :] = column_sum(dx1)
    gathered[1, z] = dx1.astype(BF16)
    steps = gather(gathered.at[1])
    next(steps)
    next(front)
    run(front)
    bo_ref[z] = (x1 + owned(1) + db_ref[...]).astype(BF16)
    outs = gather(bo_ref)
    next(outs)
    put_grad(256, 1024, lambda i: gathered[0, :, :, i * 256 : i * 256 + 256].reshape(256, 256), du)
    next(steps)
    run(steps)
    next(outs)
    do_ref[...] = dot(gathered[1].reshape(256, 1024), weight(0, 256), 1, 0).astype(BF16)
    put_grad(0, 256, lambda i: gathered[1, :, :, i * 256 : i * 256 + 256].reshape(256, 256), mixed)
    run(outs)


def third_kernel(
    x_ref, h1_ref, q_ref, kv_ref, w1_ref, start_ref, lse_ref, do_ref, dx1_ref, dw2_ref, small_ref, dub_ref, gain_ref,
    dxin_ref, dwq_ref, dwk_ref, dwv_ref, dwo_ref, dwu_ref, dwd_ref, sums_ref,
    dist, p_ref, dp_ref, dkv, kv_other, kv_pair0, kv_pair1, ring0, ring1, dq_ref,
    part, relay, minus, plus, dw1, gx, gy, gc, gz,
    other2, total2, wide2a, wide2b, thin2a, thin2b,
    other1, total1, wide1a, wide1b, thin1a, thin1b,
    send, recv,
):
    at = Place()
    net = Net(send, recv)
    x, y, z, core, low = at.x, at.y, at.z, at.core, at.low
    at.greet(
        (at.x_plus, at.x_minus, at.y_plus, at.y_minus, at.sibling, at.z_plus, at.z_minus)
    )

    def put2(rows, value):
        dwo_ref[rows, :] = value[:, 0:256]
        dwu_ref[rows, :] = value[:, 256:1280]
        dwd_ref[rows, :] = value[:, 1280:2304]

    grads2 = scatter_plane(
        net, at, dw2_ref, other2, total2, (wide2a, wide2b, thin2a, thin2b), put2
    )
    next(grads2)
    shared = [None, None]
    for micro in range(2):
        fill_distance(at, dist, start_ref[micro : micro + 1, :])
        for pair in range(2):
            lanes = slice(pair * 128, pair * 128 + 128)
            here = slice(micro * 128, micro * 128 + 128)
            queries = split_heads(q_ref[here, lanes])
            grads = split_heads(do_ref[here, lanes])
            slope = slope_row(at, pair)
            lse = lse_ref[micro * 2 + pair : micro * 2 + pair + 1, :]
            inner = jnp.zeros((1, 256), F32)
            for block in range(2048 // KEYS):
                rows = slice(block * KEYS, block * KEYS + KEYS)
                a, b = block // 2, (block % 2) * 2
                part_s = masked_scores(
                    key_block(kv_ref, micro, block, pair * 128), queries, dist[rows, :], slope
                )
                probs = jnp.exp(part_s - lse)
                prob_grad = dot(key_block(kv_ref, micro, block, 256 + pair * 128), grads, 1, 1)
                p_ref[rows, :] = probs
                dp_ref[rows, :] = prob_grad
                inner = inner + column_sum(probs * prob_grad)
                dkv[micro, a, b : b + 2, :, :, 256 + pair * 128 : 384 + pair * 128] = (
                    dot(probs.astype(BF16), grads, 1, 0).astype(BF16).reshape(2, 2, 128, 128)
                )
            query_grad = jnp.zeros((128, 256), F32)
            for block in range(2048 // KEYS):
                rows = slice(block * KEYS, block * KEYS + KEYS)
                a, b = block // 2, (block % 2) * 2
                score_grad = (p_ref[rows, :] * (dp_ref[rows, :] - inner)).astype(BF16)
                dkv[micro, a, b : b + 2, :, :, lanes] = (
                    (dot(score_grad, queries, 1, 0) * 0.125).astype(BF16).reshape(2, 2, 128, 128)
                )
                query_grad = query_grad + dot(
                    key_block(kv_ref, micro, block, pair * 128), score_grad, 0, 0
                )
            dq_ref[here, lanes] = (join_heads(query_grad) * 0.125).astype(BF16)
            next(grads2, None)
        shared[micro] = net.copy(dkv.at[micro, :, :, 1 - core], kv_other.at[micro], at.sibling)
        if micro == 0:
            continue

    def add_other(micro):
        def add(index, carry):
            i, j = lax.div(index, 4), lax.rem(index, 4)
            add_into(dkv.at[micro, i, j, core], kv_other.at[micro, i, j])
            return carry

        shared[micro].wait()
        lax.fori_loop(0, 8, add, 0)

    add_other(0)
    a = scatter4(
        net, lambda j, h: dkv.at[0, h, j, core],
        lambda h: ring0.at[0, h], lambda h: ring0.at[1, h], lambda h: ring0.at[2, h],
        y, at.y_plus, at.y_minus,
    )
    next(a)
    add_other(1)
    b_pair = net.copy(dkv.at[1, 1 - low, :, core], kv_pair1, at.pair)
    next(a)
    h1 = h1_ref[...]
    dq = dq_ref[...]

    def put_grad(first, width, right):
        for i in range(4):
            value = dot(h1[:, i * 256 : i * 256 + 256], right, 0, 0).astype(BF16)
            dw1[i, :, :, :, first : first + width] = value.reshape(4, 2, 32, width)

    put_grad(0, 256, dq)
    b_pair.wait()

    def add(index, carry):
        add_into(dkv.at[1, low, index, core], kv_pair1.at[index])
        return carry

    lax.fori_loop(0, 4, add, 0)
    b = scatter4(
        net, lambda j, h: dkv.at[1, low, j, core, h * 64 : h * 64 + 64],
        lambda h: ring1.at[0, h], lambda h: ring1.at[1, h], lambda h: ring1.at[2, h],
        y, at.y_plus, at.y_minus,
    )
    next(b)
    run(a)
    for h in range(2):
        view = dkv.at[0, h, y, core]
        view[...] = (
            view[...].astype(F32) + ring0[1, h].astype(F32) + ring0[2, h].astype(F32)
        ).astype(BF16)
    a_pair = net.copy(dkv.at[0, 1 - low, y, core], kv_pair0, at.pair)
    next(b)
    back = dot(dq, w1_ref[:, :, :, :, 0:256].reshape(1024, 256), 1, 1)
    a_pair.wait()
    top = dkv[0, low, y, core].astype(F32) + kv_pair0[...].astype(F32)
    run(b)
    extra = ring1[1].astype(F32) + ring1[2].astype(F32)
    bottom = dkv[1, low, y, core].astype(F32) + extra.reshape(128, 512)
    owned = jnp.concatenate([top, bottom], axis=0).astype(BF16)
    back = back + dot(owned, w1_ref[:, :, :, :, 256:768].reshape(1024, 512), 1, 1)
    part[...] = back.astype(BF16).reshape(4, 64, 1024)
    steps = scatter4(
        net, lambda j, h: part.at[j, h * 32 : h * 32 + 32, :],
        lambda h: relay.at[h], lambda h: minus.at[h], lambda h: plus.at[h],
        z, at.z_plus, at.z_minus,
    )
    next(steps)
    put_grad(256, 512, owned)

    def put1(rows, value):
        dwq_ref[rows, :] = value[:, 0:256]
        dwk_ref[rows, :] = value[:, 256:512]
        dwv_ref[rows, :] = value[:, 512:768]

    grads1 = scatter_plane(
        net, at, dw1, other1, total1, (wide1a, wide1b, thin1a, thin1b), put1
    )
    next(grads1)
    next(steps)
    next(grads1)
    run(steps)
    dh1 = part[z].astype(F32) + (minus[...].astype(F32) + plus[...].astype(F32)).reshape(64, 1024)
    unit, rate = norm_parts(x_ref[z].astype(F32))
    dxin_ref[z] = (dx1_ref[...] + norm_back(dh1, unit, rate, gain_ref[...])).astype(BF16)
    outs = gather4(
        net, lambda j, h: dxin_ref.at[j] if h is None else dxin_ref.at[j, h * 32 : h * 32 + 32, :],
        z, at.z_plus, at.z_minus,
    )
    next(outs)
    gx[x] = small_ref[...]
    gx[x, 0:1, :] = column_sum(dh1 * unit)
    gx[x, 1:2, :] = column_sum(dh1)
    gx[x, 6:7, :] = dub_ref[...]
    gx[x, 7:8, 0:256] = column_sum(dq.astype(F32))
    gx[x, 7:8, 256:512] = column_sum(owned[:, 256:512].astype(F32))

    def ring(buffer, here, plus_device, minus_device):
        return gather4(
            net,
            lambda j, h: buffer.at[j] if h is None else buffer.at[j, :, h * 512 : h * 512 + 512],
            here, plus_device, minus_device,
        )

    small = ring(gx, x, at.x_plus, at.x_minus)
    next(small)
    next(grads1)
    next(small)
    run(small)
    gy[y] = gx[0] + gx[1] + gx[2] + gx[3]
    small = ring(gy, y, at.y_plus, at.y_minus)
    next(small)
    next(grads1)
    next(outs)
    next(small)
    run(small)
    gc[core] = gy[0] + gy[1] + gy[2] + gy[3]
    small = net.copy(gc.at[core], gc.at[core], at.sibling)
    next(grads1)
    small.wait()
    gz[z] = gc[0] + gc[1]
    small = ring(gz, z, at.z_plus, at.z_minus)
    next(small)
    run(grads1)
    next(small)
    run(small)
    sums_ref[0:6, :] = gz[0, 0:6, :] + gz[1, 0:6, :] + gz[2, 0:6, :] + gz[3, 0:6, :]
    sums_ref[6:8, :] = gz[z, 6:8, :]
    run(outs)
    run(grads2)


def call(kernel, name, collective, count, outs, scratch, args, flops):
    vmem = pl.BlockSpec(memory_space=pltpu.VMEM)
    sems = [pltpu.SemaphoreType.DMA((count,)), pltpu.SemaphoreType.DMA((count,))]
    return pl.pallas_call(
        kernel,
        out_shape=[jax.ShapeDtypeStruct(shape, kind) for shape, kind in outs],
        in_specs=[vmem] * len(args),
        out_specs=[vmem] * len(outs),
        scratch_shapes=list(scratch) + sems,
        compiler_params=pltpu.CompilerParams(
            collective_id=collective, has_side_effects=True, vmem_limit_bytes=VMEM_BYTES
        ),
        cost_estimate=pl.CostEstimate(flops=flops, bytes_accessed=16000000, transcendentals=0),
        name=name,
    )(*args)


def on_device(
    block_input, first_gain, first_shift, query_weight, query_bias, key_weight, value_weight, value_bias,
    output_weight, output_bias, second_gain, second_shift, up_weight, up_bias, down_weight, down_bias,
    segments, out_cotangent,
):
    rows = block_input.reshape(256, 1024)
    fourths = block_input.reshape(4, 64, 1024)
    upstream = out_cotangent.reshape(4, 64, 1024)

    def row(value):
        return value.reshape(1, -1)

    h1, q, kv, w1, w2, o, lse, start = call(
        first_kernel, "first", 1, 80,
        [
            ((256, 1024), BF16),
            ((256, 256), BF16),
            ((2, 2, 4, 2, 128, 512), BF16),
            ((4, 4, 2, 32, 768), BF16),
            ((4, 4, 2, 32, 2304), BF16),
            ((256, 256), BF16),
            ((4, 256), F32),
            ((2, 128), F32),
        ],
        [
            pltpu.VMEM((2, 4, 2, 8, 128), jnp.int32),
            pltpu.VMEM((2048, 256), F32),
            pltpu.VMEM((2048, 256), F32),
        ],
        (
            rows, row(first_gain), row(first_shift), query_weight, key_weight, value_weight,
            output_weight, up_weight, down_weight, row(query_bias), row(value_bias),
            segments.reshape(2, 128),
        ),
        2_000_000_000,
    )
    block, dx1, do, dw2, small, dub = call(
        second_kernel, "second", 2, 40,
        [
            ((4, 64, 1024), BF16),
            ((64, 1024), F32),
            ((256, 256), BF16),
            ((4, 4, 2, 32, 2304), BF16),
            ((8, 1024), F32),
            ((1, 1024), F32),
        ],
        [
            pltpu.VMEM((3, 4, 64, 1024), BF16),
            pltpu.VMEM((3, 2, 32, 1024), BF16),
            pltpu.VMEM((3, 2, 32, 1024), BF16),
            pltpu.VMEM((3, 2, 32, 1024), BF16),
            pltpu.VMEM((2, 4, 64, 1024), BF16),
            pltpu.VMEM((256, 1024), BF16),
            pltpu.VMEM((256, 1024), F32),
            pltpu.VMEM((256, 1024), BF16),
        ],
        (
            fourths, upstream, o, w2, row(output_bias), row(second_gain), row(second_shift),
            row(up_bias), row(down_bias),
        ),
        4_000_000_000,
    )
    dxin, dwq, dwk, dwv, dwo, dwu, dwd, sums = call(
        third_kernel, "third", 3, 90,
        [
            ((4, 64, 1024), BF16),
            ((32, 256), F32),
            ((32, 256), F32),
            ((32, 256), F32),
            ((32, 256), F32),
            ((32, 1024), F32),
            ((32, 1024), F32),
            ((8, 1024), F32),
        ],
        [
            pltpu.VMEM((2048, 256), F32),
            pltpu.VMEM((2048, 256), F32),
            pltpu.VMEM((2048, 256), F32),
            pltpu.VMEM((2, 2, 4, 2, 128, 512), BF16),
            pltpu.VMEM((2, 2, 4, 128, 512), BF16),
            pltpu.VMEM((128, 512), BF16),
            pltpu.VMEM((4, 128, 512), BF16),
            pltpu.VMEM((3, 2, 128, 512), BF16),
            pltpu.VMEM((3, 2, 64, 512), BF16),
            pltpu.VMEM((256, 256), BF16),
            pltpu.VMEM((4, 64, 1024), BF16),
            pltpu.VMEM((2, 32, 1024), BF16),
            pltpu.VMEM((2, 32, 1024), BF16),
            pltpu.VMEM((2, 32, 1024), BF16),
            pltpu.VMEM((4, 4, 2, 32, 768), BF16),
            pltpu.VMEM((4, 8, 1024), F32),
            pltpu.VMEM((4, 8, 1024), F32),
            pltpu.VMEM((2, 8, 1024), F32),
            pltpu.VMEM((4, 8, 1024), F32),
        ]
        + plane_scratch(2304)
        + plane_scratch(768),
        (
            fourths, h1, q, kv, w1, start, lse, do, dx1, dw2, small, dub, row(first_gain),
        ),
        4_000_000_000,
    )
    shape = (2, 1, 128, 1024)
    return (
        block.astype(F32).reshape(shape),
        dxin.astype(F32).reshape(shape),
        sums[0],
        sums[1],
        dwq,
        sums[7, 0:256],
        dwk,
        dwv,
        sums[7, 256:512],
        dwo,
        sums[2],
        sums[3],
        sums[4],
        dwu,
        sums[6],
        dwd,
        sums[5],
    )


def solution(mesh):
    tokens = P(None, "seq", "ctx", None)
    matrix = P(("seq", "ctx"), "head")
    return jax.shard_map(
        on_device,
        mesh=mesh,
        in_specs=(
            tokens, P(), P(), matrix, P("head"), matrix, matrix, P("head"), matrix, P(), P(), P(),
            matrix, P("head"), matrix, P(), P(None, "seq", "ctx"), tokens,
        ),
        out_specs=(
            tokens, tokens, P(), P(), matrix, P("head"), matrix, matrix, P("head"), matrix, P(), P(),
            P(), matrix, P("head"), matrix, P(),
        ),
        check_vma=False,
    )
```

```python
import jax
import jax.numpy as jnp
from jax import lax
from jax.experimental import pallas as pl
from jax.experimental.pallas import tpu as pltpu
from jax.sharding import PartitionSpec as P

F32 = jnp.float32
BF16 = jnp.bfloat16
MESH = pl.DeviceIdType.MESH
VMEM_BYTES = 56 * 1024 * 1024
KEYS = 512
COPIES = 168


def dot(left, right, dim_left, dim_right):
    return lax.dot_general(
        left, right, (((dim_left,), (dim_right,)), ((), ())), preferred_element_type=F32
    )


def turn(index, by):
    return lax.rem(index + by, 4)


class Place:
    def __init__(self):
        self.seq = lax.axis_index("seq")
        self.ctx = lax.axis_index("ctx")
        self.z = lax.axis_index("head")
        self.core = lax.rem(self.ctx, 2)
        self.y = lax.rem(lax.div(self.ctx, 2), 4)
        self.low = lax.div(self.ctx, 8)
        self.x = self.seq * 2 + self.low
        self.x_plus = self.at(turn(self.x, 1), self.y, self.core, self.z)
        self.x_minus = self.at(turn(self.x, 3), self.y, self.core, self.z)
        self.y_plus = self.at(self.x, turn(self.y, 1), self.core, self.z)
        self.y_minus = self.at(self.x, turn(self.y, 3), self.core, self.z)
        self.z_plus = self.at(self.x, self.y, self.core, turn(self.z, 1))
        self.z_minus = self.at(self.x, self.y, self.core, turn(self.z, 3))
        self.x_across = self.at(turn(self.x, 2), self.y, self.core, self.z)
        self.y_across = self.at(self.x, turn(self.y, 2), self.core, self.z)
        self.z_across = self.at(self.x, self.y, self.core, turn(self.z, 2))
        self.x_ring = (self.x, (self.x_plus, self.x_minus, self.x_across))
        self.y_ring = (self.y, (self.y_plus, self.y_minus, self.y_across))
        self.z_ring = (self.z, (self.z_plus, self.z_minus, self.z_across))
        self.sibling = self.at(self.x, self.y, 1 - self.core, self.z)
        self.pair = self.at(self.seq * 2 + 1 - self.low, self.y, self.core, self.z)

    def at(self, x, y, core, z):
        return (lax.div(x, 2), (lax.rem(x, 2) * 4 + y) * 2 + core, z)

    def greet(self, partners):
        barrier = pltpu.get_barrier_semaphore()
        for partner in partners:
            pl.semaphore_signal(barrier, inc=1, device_id=partner, device_id_type=MESH)
        pl.semaphore_wait(barrier, len(partners))


class Net:
    def __init__(self, send, recv):
        self.send, self.recv, self.used = send, recv, 0

    def copy(self, src, dst, device):
        index = self.used
        self.used += 1
        made = pltpu.make_async_remote_copy(
            src_ref=src,
            dst_ref=dst,
            send_sem=self.send.at[index],
            recv_sem=self.recv.at[index],
            device_id=device,
            device_id_type=MESH,
        )
        made.start()
        return made


def run(steps):
    for _ in steps:
        pass


FROM = (3, 1, 2)
TO = (1, 3, 2)


def add_into(view, *others):
    value = view[...].astype(F32)
    for other in others:
        value = value + other[...].astype(F32)
    view[...] = value.astype(BF16)


class Gather:
    def __init__(self, net, region, ring):
        self.here, others = ring
        own = region(self.here)
        self.region = region
        self.copies = [net.copy(own, own, device) for device in others]

    def arrivals(self):
        for copy, step in zip(self.copies, FROM):
            copy.wait_recv()
            yield self.region(turn(self.here, step))

    def sent(self):
        for copy in self.copies:
            copy.wait_send()

    def finish(self):
        for _ in self.arrivals():
            pass
        self.sent()


class Scatter:
    def __init__(self, net, part, slots, ring):
        here, others = ring
        self.copies = [
            net.copy(part(turn(here, step)), slots.at[index], device)
            for index, (step, device) in enumerate(zip(TO, others))
        ]

    def finish(self):
        for copy in self.copies:
            copy.wait()


TOP, LOW = slice(0, 16), slice(16, 32)


def gather_plane(net, at, full):
    x, y, core = at.x, at.y, at.core
    done = []

    def share(view):
        done.append(net.copy(view, view, at.sibling))

    a = Gather(net, lambda j: full.at[j, y, core, TOP, :], at.x_ring)
    b = Gather(net, lambda j: full.at[x, j, core, LOW, :], at.y_ring)
    yield
    a.finish()
    a = Gather(net, lambda j: full.at[:, j, core, TOP, :], at.y_ring)
    b.finish()
    b = Gather(net, lambda j: full.at[j, :, core, LOW, :], at.x_ring)
    share(full.at[:, y, core, TOP, :])
    share(full.at[x, :, core, LOW, :])
    yield
    for one, two in zip(a.arrivals(), b.arrivals()):
        share(one)
        share(two)
    a.sent()
    b.sent()
    yield
    for copy in done:
        copy.wait()


def scatter_plane(net, at, partial, other, total, wide, thin, result):
    x, y, core = at.x, at.y, at.core
    shared = net.copy(partial.at[:, :, 1 - core], other, at.sibling)
    yield
    shared.wait()

    def add(index, carry):
        i, j = lax.div(index, 4), lax.rem(index, 4)
        total[i, j] = (partial[i, j, core].astype(F32) + other[i, j].astype(F32)).astype(BF16)
        return carry

    lax.fori_loop(0, 16, add, 0)
    a = Scatter(net, lambda j: total.at[:, j, TOP, :], wide.at[0], at.y_ring)
    b = Scatter(net, lambda j: total.at[j, :, LOW, :], wide.at[1], at.x_ring)
    yield
    a.finish()
    add_into(total.at[:, y, TOP, :], wide.at[0, 0], wide.at[0, 1], wide.at[0, 2])
    a = Scatter(net, lambda j: total.at[j, y, TOP, :], thin.at[0], at.x_ring)
    b.finish()
    add_into(total.at[x, :, LOW, :], wide.at[1, 0], wide.at[1, 1], wide.at[1, 2])
    b = Scatter(net, lambda j: total.at[x, j, LOW, :], thin.at[1], at.y_ring)
    yield
    for index, steps, rows in ((0, a, TOP), (1, b, LOW)):
        steps.finish()
        extra = thin[index, 0].astype(F32) + thin[index, 1].astype(F32) + thin[index, 2].astype(F32)
        result(rows, total[x, y, rows, :].astype(F32) + extra)


def plane_scratch(width):
    return [
        pltpu.VMEM((4, 4, 2, 32, width), BF16),
        pltpu.VMEM((4, 4, 32, width), BF16),
        pltpu.VMEM((4, 4, 32, width), BF16),
        pltpu.VMEM((2, 3, 4, 16, width), BF16),
        pltpu.VMEM((2, 3, 16, width), BF16),
    ]


def norm_parts(value):
    center = value - jnp.mean(value, axis=-1, keepdims=True)
    rate = lax.rsqrt(jnp.mean(center * center, axis=-1, keepdims=True) + 1e-05)
    return center * rate, rate


def norm_back(grad, unit, rate, gain):
    inner = grad * gain
    even = jnp.mean(inner, axis=-1, keepdims=True)
    along = jnp.mean(inner * unit, axis=-1, keepdims=True)
    return rate * (inner - even - unit * along)


def column_sum(value):
    return jnp.sum(value, axis=0, keepdims=True)


def split_heads(pair):
    wide = pair.astype(F32)
    lane = lax.broadcasted_iota(jnp.int32, wide.shape, 1)
    both = [jnp.where(lane < 64, wide, 0.0), jnp.where(lane >= 64, wide, 0.0)]
    return jnp.concatenate(both, axis=0).astype(BF16)


def join_heads(wide):
    return jnp.concatenate([wide[0:64, 0:128], wide[64:128, 128:256]], axis=0).T


def slope_row(at, pair):
    first = jnp.where(
        at.z == 0, 1.0, jnp.where(at.z == 1, 0.25, jnp.where(at.z == 2, 0.0625, 0.015625))
    ).astype(F32)
    lane = lax.broadcasted_iota(jnp.int32, (1, 256), 1)
    even = 2.0 ** (-(2 * pair + 1) / 2.0)
    odd = 2.0 ** (-(2 * pair + 2) / 2.0)
    return first * jnp.where(lane < 128, even, odd).astype(F32)


def fill_distance(at, dist, start):
    def fill(block, carry):
        first = block * 256
        lane = lax.broadcasted_iota(jnp.int32, (256, 128), 1)
        query = (lane + at.ctx * 128).astype(F32)
        key = (lax.broadcasted_iota(jnp.int32, (256, 128), 0) + first).astype(F32)
        apart = query - key
        value = jnp.where((key >= start) & (apart >= 0.0), apart, -1.0)
        dist[pl.ds(pl.multiple_of(first, 256), 256), 0:128] = value
        dist[pl.ds(pl.multiple_of(first, 256), 256), 128:256] = value
        return carry

    lax.fori_loop(0, 8, fill, 0)


def masked_scores(keys, queries, dist, slope):
    raw = dot(keys, queries, 1, 1) * 0.125
    return jnp.where(dist >= 0.0, raw - slope * dist, -1000000000.0)


def key_block(kv, micro, block, first):
    low, y = block // 2, (block % 2) * 2
    return kv[micro, low, y : y + 2, :, :, first : first + 128].reshape(KEYS, 128)


def layer_kernel(
    x_ref, dy_ref, seg_ref, gain1_ref, shift1_ref, wq_ref, qb_ref, wk_ref, wv_ref, vb_ref, wo_ref, ob_ref,
    gain2_ref, shift2_ref, wu_ref, ub_ref, wd_ref, db_ref,
    bo_ref, dxin_ref, dqkv_ref, dwo_ref, dud_ref, sums_ref,
    w1, wo, w2, kv, seg_all, h1_ref, q_ref, o_ref, lse_ref, dist, score, dp_ref,
    part, slots, gathered, dg, g_ref, du_ref, do_ref, dq_ref,
    dkv, kv_other, kv_pair0, kv_pair1, ring0, ring1, gx, gy, gz,
    dw1, other1, total1, wide1, thin1,
    dwo_part, other_o, total_o, wide_o, thin_o,
    dw2, other2, total2, wide2, thin2,
    send, recv,
):
    at = Place()
    net = Net(send, recv)
    x, y, z, core, low = at.x, at.y, at.z, at.core, at.low
    partners = at.x_ring[1] + at.y_ring[1] + at.z_ring[1] + (at.sibling,)
    partners = partners + tuple(
        at.at(x, turn(y, step), 1 - core, z) for step in TO
    )
    at.greet(partners)

    mine = w1.at[x, y, core]
    mine[:, 0:256] = wq_ref[...]
    mine[:, 256:512] = wk_ref[...]
    mine[:, 512:768] = wv_ref[...]
    w1_steps = gather_plane(net, at, w1)
    next(w1_steps)
    wo[x, y, core] = wo_ref[...]
    wo_steps = gather_plane(net, at, wo)
    next(wo_steps)
    seg_all[low, y, core] = jnp.concatenate([seg_ref[...]] * 4, axis=0)
    seg = Gather(net, lambda j: seg_all.at[low, j, core], at.y_ring)
    mine = w2.at[x, y, core]
    mine[:, 0:1024] = wu_ref[...]
    mine[:, 1024:2048] = wd_ref[...]
    unit, _ = norm_parts(x_ref[...].reshape(256, 1024).astype(F32))
    h1_ref[...] = (unit * gain1_ref[...] + shift1_ref[...]).astype(BF16)
    next(w1_steps)
    seg.finish()
    view = seg_all.at[low, :, core]
    seg_pair = net.copy(view, view, at.pair)
    next(w1_steps)
    next(wo_steps)
    w2_steps = gather_plane(net, at, w2)
    next(w2_steps)
    seg_pair.wait()
    view = seg_all.at[:, :, core]
    seg_share = net.copy(view, view, at.sibling)
    run(w1_steps)
    h1 = h1_ref[...]
    wide = dot(h1, w1[:, :, :, :, 256:768].reshape(1024, 512), 1, 0)
    values = (wide[:, 256:512] + vb_ref[...]).astype(BF16)
    for micro in range(2):
        rows = slice(micro * 128, micro * 128 + 128)
        kv[micro, low, y, core, :, 0:256] = wide[rows, 0:256].astype(BF16)
        kv[micro, low, y, core, :, 256:512] = values[rows]

    def share(view):
        return net.copy(view, view, at.sibling)

    own = kv.at[0, low, y, core]
    a_pair = net.copy(own, own, at.pair)
    b_steps = Gather(net, lambda j: kv.at[1, low, j, core], at.y_ring)
    q_ref[...] = (dot(h1, w1[:, :, :, :, 0:256].reshape(1024, 256), 1, 0) + qb_ref[...]).astype(BF16)
    a_pair.wait()
    a_steps = Gather(net, lambda j: kv.at[0, :, j, core], at.y_ring)
    a_done = [share(kv.at[0, :, y, core])]
    next(wo_steps)
    seg_share.wait()
    found = jnp.zeros((2, 128), F32)
    for number in range(1, 4):
        below = (seg_all[:, :, :, 0:2, :] < number).astype(F32)
        below = jnp.sum(below.reshape(16, 2, 128), axis=0)
        below = jnp.sum(below, axis=-1, keepdims=True)
        found = jnp.where(seg_ref[...] == number, below, found)
    fill_distance(at, dist.at[0], found[0:1])
    b_steps.finish()
    view = kv.at[1, low, :, core]
    b_pair = net.copy(view, view, at.pair)
    b_done = [share(view)]
    fill_distance(at, dist.at[1], found[1:2])
    for view in a_steps.arrivals():
        a_done.append(share(view))
    a_steps.sent()
    next(w2_steps)
    for copy in a_done:
        copy.wait()
    for micro in range(2):
        if micro == 1:
            b_pair.wait()
            b_done.append(share(kv.at[1, 1 - low, :, core]))
            for copy in b_done:
                copy.wait()
        for pair in range(2):
            lanes = slice(pair * 128, pair * 128 + 128)
            queries = split_heads(q_ref[micro * 128 : micro * 128 + 128, lanes])
            slope = slope_row(at, pair)
            top = jnp.full((1, 256), -3.0e38, F32)
            for block in range(2048 // KEYS):
                rows = slice(block * KEYS, block * KEYS + KEYS)
                value = masked_scores(
                    key_block(kv, micro, block, pair * 128), queries, dist[micro, rows, :], slope
                )
                score[rows, :] = value
                top = jnp.maximum(top, jnp.max(value, axis=0, keepdims=True))
            summed = jnp.zeros((1, 256), F32)
            for block in range(2048 // KEYS):
                rows = slice(block * KEYS, block * KEYS + KEYS)
                value = jnp.exp(score[rows, :] - top)
                score[rows, :] = value
                summed = summed + column_sum(value)
            scale = 1.0 / summed
            mixed = jnp.zeros((128, 256), F32)
            for block in range(2048 // KEYS):
                rows = slice(block * KEYS, block * KEYS + KEYS)
                probs = (score[rows, :] * scale).astype(BF16)
                mixed = mixed + dot(key_block(kv, micro, block, 256 + pair * 128), probs, 0, 0)
            o_ref[micro * 128 : micro * 128 + 128, lanes] = join_heads(mixed).astype(BF16)
            lse_ref[micro * 2 + pair : micro * 2 + pair + 1, :] = top + jnp.log(summed)

    def scatter(index, value):
        part[index] = value.astype(BF16).reshape(4, 64, 1024)
        return Scatter(net, lambda j: part.at[index, j], slots.at[index], at.z_ring)

    def owned(index):
        extra = slots[index, 0].astype(F32) + slots[index, 1].astype(F32) + slots[index, 2].astype(F32)
        return part[index, z].astype(F32) + extra

    def up(first, width):
        return w2[:, :, :, :, first : first + width].reshape(1024, width)

    def put_grad(to, first, width, left, right):
        for i in range(4):
            value = dot(left(i), right, 0, 0).astype(BF16)
            to[i, :, :, :, first : first + width] = value.reshape(4, 2, 32, width)

    mixed = o_ref[...]
    run(wo_steps)
    steps = scatter(0, dot(mixed, wo[...].reshape(1024, 256), 1, 1))
    next(w2_steps)
    run(w2_steps)
    dyl = dy_ref[...].reshape(256, 1024)
    dg[...] = dot(dyl, up(1024, 1024), 1, 0)
    steps.finish()
    x1 = x_ref[z].astype(F32) + owned(0) + ob_ref[...]
    unit, rate = norm_parts(x1)
    gathered[0, z] = (unit * gain2_ref[...] + shift2_ref[...]).astype(BF16)
    steps = Gather(net, lambda j: gathered.at[0, j], at.z_ring)
    upstream = dy_ref[z].astype(F32)
    gx[x, 5:6, :] = column_sum(upstream)
    steps.finish()
    h2 = gathered[0].reshape(256, 1024)
    for i in range(2):
        cols = slice(i * 512, i * 512 + 512)
        u = dot(h2, up(i * 512, 512), 1, 0) + ub_ref[:, cols]
        tanh = jnp.tanh(0.7978845608028654 * (u + 0.044715 * u * u * u))
        g_ref[:, cols] = (0.5 * u * (1.0 + tanh)).astype(BF16)
        turned = 0.5 * u * (1.0 - tanh * tanh) * 0.7978845608028654 * (1.0 + 3 * 0.044715 * u * u)
        du_ref[:, cols] = (dg[:, cols] * (0.5 * (1.0 + tanh) + turned)).astype(BF16)
    du = du_ref[...]
    back = scatter(2, dot(du, up(0, 1024), 1, 1))
    put_grad(
        dw2, 1024, 1024, lambda i: dy_ref[:, :, i * 256 : i * 256 + 256].reshape(256, 256), g_ref[...]
    )
    put_grad(
        dw2, 0, 1024, lambda i: gathered[0, :, :, i * 256 : i * 256 + 256].reshape(256, 256), du
    )

    def put2(rows, value):
        dud_ref[rows, :] = value

    dw2_steps = scatter_plane(net, at, dw2, other2, total2, wide2, thin2, put2)
    next(dw2_steps)
    back.finish()
    dh2 = owned(2)
    dx1 = upstream + norm_back(dh2, unit, rate, gain2_ref[...])
    gathered[1, z] = dx1.astype(BF16)
    steps = Gather(net, lambda j: gathered.at[1, j], at.z_ring)
    front = scatter(1, dot(g_ref[...], up(1024, 1024), 1, 1))
    gx[x, 3:4, :] = column_sum(dh2 * unit)
    gx[x, 4:5, :] = column_sum(dh2)
    gx[x, 2:3, :] = column_sum(dx1)
    gx[x, 6:7, :] = column_sum(du.astype(F32))
    next(dw2_steps)
    steps.finish()
    do_ref[...] = dot(gathered[1].reshape(256, 1024), wo[...].reshape(1024, 256), 1, 0).astype(BF16)
    put_grad(
        dwo_part, 0, 256, lambda i: gathered[1, :, :, i * 256 : i * 256 + 256].reshape(256, 256), mixed
    )

    def put_o(rows, value):
        dwo_ref[rows, :] = value

    dwo_steps = scatter_plane(net, at, dwo_part, other_o, total_o, wide_o, thin_o, put_o)
    next(dwo_steps)
    front.finish()
    bo_ref[z] = (x1 + owned(1) + db_ref[...]).astype(BF16)
    bo_steps = Gather(net, lambda j: bo_ref.at[j], at.z_ring)

    shared = [None, None]
    a_steps = None

    def add_other(micro):
        def add(index, carry):
            i, j = lax.div(index, 4), lax.rem(index, 4)
            add_into(dkv.at[micro, i, j, core], kv_other.at[micro, i, j])
            return carry

        shared[micro].wait()
        lax.fori_loop(0, 8, add, 0)

    for micro in range(2):
        for pair in range(2):
            lanes = slice(pair * 128, pair * 128 + 128)
            here = slice(micro * 128, micro * 128 + 128)
            queries = split_heads(q_ref[here, lanes])
            grads = split_heads(do_ref[here, lanes])
            slope = slope_row(at, pair)
            lse = lse_ref[micro * 2 + pair : micro * 2 + pair + 1, :]
            inner = jnp.zeros((1, 256), F32)
            for block in range(2048 // KEYS):
                rows = slice(block * KEYS, block * KEYS + KEYS)
                a, b = block // 2, (block % 2) * 2
                value = masked_scores(
                    key_block(kv, micro, block, pair * 128), queries, dist[micro, rows, :], slope
                )
                probs = jnp.exp(value - lse)
                prob_grad = dot(key_block(kv, micro, block, 256 + pair * 128), grads, 1, 1)
                score[rows, :] = probs
                dp_ref[rows, :] = prob_grad
                inner = inner + column_sum(probs * prob_grad)
                dkv[micro, a, b : b + 2, :, :, 256 + pair * 128 : 384 + pair * 128] = (
                    dot(probs.astype(BF16), grads, 1, 0).astype(BF16).reshape(2, 2, 128, 128)
                )
            query_grad = jnp.zeros((128, 256), F32)
            for block in range(2048 // KEYS):
                rows = slice(block * KEYS, block * KEYS + KEYS)
                a, b = block // 2, (block % 2) * 2
                score_grad = (score[rows, :] * (dp_ref[rows, :] - inner)).astype(BF16)
                dkv[micro, a, b : b + 2, :, :, lanes] = (
                    (dot(score_grad, queries, 1, 0) * 0.125).astype(BF16).reshape(2, 2, 128, 128)
                )
                query_grad = query_grad + dot(
                    key_block(kv, micro, block, pair * 128), score_grad, 0, 0
                )
            dq_ref[here, lanes] = (join_heads(query_grad) * 0.125).astype(BF16)
            if micro == 0 and pair == 0:
                next(dw2_steps)
                next(dwo_steps)
            if micro == 1 and pair == 0:
                add_other(0)
                a_steps = Scatter(net, lambda j: dkv.at[0, :, j, core], ring0, at.y_ring)
                next(dwo_steps)
        shared[micro] = net.copy(dkv.at[micro, :, :, 1 - core], kv_other.at[micro], at.sibling)

    run(dw2_steps)
    run(dwo_steps)
    add_other(1)
    b_pair = net.copy(dkv.at[1, 1 - low, :, core], kv_pair1, at.pair)
    h1 = h1_ref[...]
    dq = dq_ref[...]

    def left(i):
        return h1[:, i * 256 : i * 256 + 256]

    put_grad(dw1, 0, 256, left, dq)
    a_steps.finish()
    add_into(dkv.at[0, :, y, core], ring0.at[0], ring0.at[1], ring0.at[2])
    a_pair = net.copy(dkv.at[0, 1 - low, y, core], kv_pair0, at.pair)
    b_pair.wait()
    add_into(dkv.at[1, low, :, core], kv_pair1)
    b_steps = Scatter(net, lambda j: dkv.at[1, low, j, core], ring1, at.y_ring)
    back = dot(dq, w1[:, :, :, :, 0:256].reshape(1024, 256), 1, 1)
    a_pair.wait()
    above = dkv[0, low, y, core].astype(F32) + kv_pair0[...].astype(F32)
    b_steps.finish()
    below = dkv[1, low, y, core].astype(F32) + (
        ring1[0].astype(F32) + ring1[1].astype(F32) + ring1[2].astype(F32)
    )
    dkv_own = jnp.concatenate([above, below], axis=0).astype(BF16)
    back = back + dot(dkv_own, w1[:, :, :, :, 256:768].reshape(1024, 512), 1, 1)
    steps = scatter(3, back)
    put_grad(dw1, 256, 512, left, dkv_own)

    def put1(rows, value):
        dqkv_ref[rows, :] = value

    dw1_steps = scatter_plane(net, at, dw1, other1, total1, wide1, thin1, put1)
    next(dw1_steps)
    unit, rate = norm_parts(x_ref[z].astype(F32))
    gx[x, 7:8, 0:256] = column_sum(dq.astype(F32))
    gx[x, 7:8, 256:512] = column_sum(dkv_own[:, 256:512].astype(F32))
    gx[x, 7:8, 512:1024] = jnp.zeros((1, 512), F32)
    next(dw1_steps)
    steps.finish()
    dh1 = owned(3)
    gx[x, 0:1, :] = column_sum(dh1 * unit)
    gx[x, 1:2, :] = column_sum(dh1)
    small = Gather(net, lambda j: gx.at[j], at.x_ring)
    dxin_ref[z] = (dx1 + norm_back(dh1, unit, rate, gain1_ref[...])).astype(BF16)
    steps = Gather(net, lambda j: dxin_ref.at[j], at.z_ring)
    small.finish()
    own = gy.at[y, core]
    gy[y, core] = gx[0] + gx[1] + gx[2] + gx[3]
    small = [net.copy(own, own, device) for device in at.y_ring[1] + (at.sibling,)]
    small = small + [net.copy(own, own, at.at(x, turn(y, step), 1 - core, z)) for step in TO]
    next(dw1_steps)
    for copy in small:
        copy.wait()
    total = gy[0, 0] + gy[0, 1]
    for i in range(1, 4):
        total = total + gy[i, 0] + gy[i, 1]
    gz[z] = total
    small = Gather(net, lambda j: gz.at[j], at.z_ring)
    run(dw1_steps)
    bo_steps.finish()
    small.finish()
    sums_ref[0:6, :] = gz[0, 0:6, :] + gz[1, 0:6, :] + gz[2, 0:6, :] + gz[3, 0:6, :]
    sums_ref[6:8, :] = gz[z, 6:8, :]
    steps.finish()


def write_kernel(
    bo_ref, dxin_ref, dqkv_ref, dwo_ref, dud_ref, sums_ref,
    block_ref, input_ref, g1_ref, s1_ref, dwq_ref, qb_ref, dwk_ref, dwv_ref, vb_ref, out_ref,
    ob_ref, g2_ref, s2_ref, dwu_ref, ub_ref, dwd_ref, db_ref,
):
    block_ref[...] = bo_ref[...].astype(F32)
    input_ref[...] = dxin_ref[...].astype(F32)
    dwq_ref[...] = dqkv_ref[:, 0:256]
    dwk_ref[...] = dqkv_ref[:, 256:512]
    dwv_ref[...] = dqkv_ref[:, 512:768]
    out_ref[...] = dwo_ref[...]
    dwu_ref[...] = dud_ref[:, 0:1024]
    dwd_ref[...] = dud_ref[:, 1024:2048]
    for index, ref in enumerate((g1_ref, s1_ref, ob_ref, g2_ref, s2_ref, db_ref, ub_ref)):
        ref[...] = sums_ref[index : index + 1, :]
    qb_ref[...] = sums_ref[7:8, 0:256]
    vb_ref[...] = sums_ref[7:8, 256:512]


def on_device(
    block_input, first_gain, first_shift, query_weight, query_bias, key_weight, value_weight, value_bias,
    output_weight, output_bias, second_gain, second_shift, up_weight, up_bias, down_weight, down_bias,
    segments, out_cotangent,
):
    vmem = pl.BlockSpec(memory_space=pltpu.VMEM)

    def row(value):
        return value.reshape(1, -1)

    def shapes(*pairs):
        return [jax.ShapeDtypeStruct(shape, kind) for shape, kind in pairs]

    results = pl.pallas_call(
        layer_kernel,
        out_shape=shapes(
            ((4, 64, 1024), BF16),
            ((4, 64, 1024), BF16),
            ((32, 768), F32),
            ((32, 256), F32),
            ((32, 2048), F32),
            ((8, 1024), F32),
        ),
        in_specs=[vmem] * 18,
        out_specs=[vmem] * 6,
        scratch_shapes=[
            pltpu.VMEM((4, 4, 2, 32, 768), BF16),
            pltpu.VMEM((4, 4, 2, 32, 256), BF16),
            pltpu.VMEM((4, 4, 2, 32, 2048), BF16),
            pltpu.VMEM((2, 2, 4, 2, 128, 512), BF16),
            pltpu.VMEM((2, 4, 2, 8, 128), jnp.int32),
            pltpu.VMEM((256, 1024), BF16),
            pltpu.VMEM((256, 256), BF16),
            pltpu.VMEM((256, 256), BF16),
            pltpu.VMEM((4, 256), F32),
            pltpu.VMEM((2, 2048, 256), F32),
            pltpu.VMEM((2048, 256), F32),
            pltpu.VMEM((2048, 256), F32),
            pltpu.VMEM((4, 4, 64, 1024), BF16),
            pltpu.VMEM((4, 3, 64, 1024), BF16),
            pltpu.VMEM((2, 4, 64, 1024), BF16),
            pltpu.VMEM((256, 1024), F32),
            pltpu.VMEM((256, 1024), BF16),
            pltpu.VMEM((256, 1024), BF16),
            pltpu.VMEM((256, 256), BF16),
            pltpu.VMEM((256, 256), BF16),
            pltpu.VMEM((2, 2, 4, 2, 128, 512), BF16),
            pltpu.VMEM((2, 2, 4, 128, 512), BF16),
            pltpu.VMEM((128, 512), BF16),
            pltpu.VMEM((4, 128, 512), BF16),
            pltpu.VMEM((3, 2, 128, 512), BF16),
            pltpu.VMEM((3, 128, 512), BF16),
            pltpu.VMEM((4, 8, 1024), F32),
            pltpu.VMEM((4, 2, 8, 1024), F32),
            pltpu.VMEM((4, 8, 1024), F32),
            *plane_scratch(768),
            *plane_scratch(256),
            *plane_scratch(2048),
            pltpu.SemaphoreType.DMA((COPIES,)),
            pltpu.SemaphoreType.DMA((COPIES,)),
        ],
        compiler_params=pltpu.CompilerParams(
            collective_id=1, has_side_effects=True, vmem_limit_bytes=VMEM_BYTES
        ),
        cost_estimate=pl.CostEstimate(
            flops=10_000_000_000, bytes_accessed=16_000_000, transcendentals=0
        ),
        name="layer",
    )(
        block_input.reshape(4, 64, 1024), out_cotangent.reshape(4, 64, 1024), segments.reshape(2, 128),
        row(first_gain), row(first_shift), query_weight, row(query_bias), key_weight, value_weight,
        row(value_bias), output_weight, row(output_bias), row(second_gain), row(second_shift), up_weight,
        row(up_bias), down_weight, row(down_bias),
    )
    wide, narrow = ((1, 1024), F32), ((1, 256), F32)
    square, tall, tokens = ((32, 256), F32), ((32, 1024), F32), ((4, 64, 1024), F32)
    outs = pl.pallas_call(
        write_kernel,
        out_shape=shapes(
            tokens, tokens, wide, wide, square, narrow, square, square, narrow, square, wide, wide, wide,
            tall, wide, tall, wide,
        ),
        in_specs=[vmem] * 6,
        out_specs=[vmem] * 17,
        name="write",
    )(*results)
    ends = {0: (2, 1, 128, 1024), 1: (2, 1, 128, 1024)}
    flat = (2, 3, 5, 8, 10, 11, 12, 14, 16)
    return tuple(
        out.reshape(ends[i]) if i in ends else (out.reshape(-1) if i in flat else out)
        for i, out in enumerate(outs)
    )


def solution(mesh):
    tokens = P(None, "seq", "ctx", None)
    matrix = P(("seq", "ctx"), "head")
    return jax.shard_map(
        on_device,
        mesh=mesh,
        in_specs=(
            tokens, P(), P(), matrix, P("head"), matrix, matrix, P("head"), matrix, P(), P(), P(),
            matrix, P("head"), matrix, P(), P(None, "seq", "ctx"), tokens,
        ),
        out_specs=(
            tokens, tokens, P(), P(), matrix, P("head"), matrix, matrix, P("head"), matrix, P(), P(),
            P(), matrix, P("head"), matrix, P(),
        ),
        check_vma=False,
    )
```

```python
import jax
import jax.numpy as jnp
from jax import lax
from jax.experimental import pallas as pl
from jax.experimental.pallas import tpu as pltpu
from jax.sharding import PartitionSpec as P

F32 = jnp.float32
BF16 = jnp.bfloat16
MESH = pl.DeviceIdType.MESH
VMEM_BYTES = 56 * 1024 * 1024
KEYS = 512
COPIES = 256


def dot(left, right, dim_left, dim_right):
    return lax.dot_general(
        left, right, (((dim_left,), (dim_right,)), ((), ())), preferred_element_type=F32
    )


def turn(index, by):
    return lax.rem(index + by, 4)


class Place:
    def __init__(self):
        self.seq = lax.axis_index("seq")
        self.ctx = lax.axis_index("ctx")
        self.z = lax.axis_index("head")
        self.core = lax.rem(self.ctx, 2)
        self.y = lax.rem(lax.div(self.ctx, 2), 4)
        self.low = lax.div(self.ctx, 8)
        self.x = self.seq * 2 + self.low
        self.x_plus = self.at(turn(self.x, 1), self.y, self.core, self.z)
        self.x_minus = self.at(turn(self.x, 3), self.y, self.core, self.z)
        self.y_plus = self.at(self.x, turn(self.y, 1), self.core, self.z)
        self.y_minus = self.at(self.x, turn(self.y, 3), self.core, self.z)
        self.z_plus = self.at(self.x, self.y, self.core, turn(self.z, 1))
        self.z_minus = self.at(self.x, self.y, self.core, turn(self.z, 3))
        self.x_across = self.at(turn(self.x, 2), self.y, self.core, self.z)
        self.y_across = self.at(self.x, turn(self.y, 2), self.core, self.z)
        self.z_across = self.at(self.x, self.y, self.core, turn(self.z, 2))
        self.x_ring = (self.x, (self.x_plus, self.x_minus, self.x_across))
        self.y_ring = (self.y, (self.y_plus, self.y_minus, self.y_across))
        self.z_ring = (self.z, (self.z_plus, self.z_minus, self.z_across))
        self.sibling = self.at(self.x, self.y, 1 - self.core, self.z)
        self.pair = self.at(self.seq * 2 + 1 - self.low, self.y, self.core, self.z)

    def at(self, x, y, core, z):
        return (lax.div(x, 2), (lax.rem(x, 2) * 4 + y) * 2 + core, z)

    def greet(self, partners):
        barrier = pltpu.get_barrier_semaphore()
        for partner in partners:
            pl.semaphore_signal(barrier, inc=1, device_id=partner, device_id_type=MESH)
        pl.semaphore_wait(barrier, len(partners))


class Net:
    def __init__(self, send, recv):
        self.send, self.recv, self.used = send, recv, 0

    def copy(self, src, dst, device):
        index = self.used
        self.used += 1
        made = pltpu.make_async_remote_copy(
            src_ref=src,
            dst_ref=dst,
            send_sem=self.send.at[index],
            recv_sem=self.recv.at[index],
            device_id=device,
            device_id_type=MESH,
        )
        made.start()
        return made


def run(steps):
    for _ in steps:
        pass


FROM = (3, 1, 2)
TO = (1, 3, 2)


def add_into(view, *others):
    value = view[...].astype(F32)
    for other in others:
        value = value + other[...].astype(F32)
    view[...] = value.astype(BF16)


class Gather:
    def __init__(self, net, region, ring):
        self.here, others = ring
        own = region(self.here)
        self.region = region
        self.copies = [net.copy(own, own, device) for device in others]

    def arrivals(self):
        for copy, step in zip(self.copies, FROM):
            copy.wait_recv()
            yield self.region(turn(self.here, step))

    def sent(self):
        for copy in self.copies:
            copy.wait_send()

    def finish(self):
        for _ in self.arrivals():
            pass
        self.sent()


class Scatter:
    def __init__(self, net, part, slots, ring):
        here, others = ring
        self.copies = [
            net.copy(part(turn(here, step)), slots.at[index], device)
            for index, (step, device) in enumerate(zip(TO, others))
        ]

    def finish(self):
        for copy in self.copies:
            copy.wait()


TOP, LOW = slice(0, 16), slice(16, 32)


def gather_plane(net, at, full):
    x, y, core = at.x, at.y, at.core
    done = []

    def share(view):
        done.append(net.copy(view, view, at.sibling))

    a = Gather(net, lambda j: full.at[j, y, core, TOP, :], at.x_ring)
    b = Gather(net, lambda j: full.at[x, j, core, LOW, :], at.y_ring)
    yield
    a.finish()
    a = Gather(net, lambda j: full.at[:, j, core, TOP, :], at.y_ring)
    b.finish()
    b = Gather(net, lambda j: full.at[j, :, core, LOW, :], at.x_ring)
    share(full.at[:, y, core, TOP, :])
    share(full.at[x, :, core, LOW, :])
    yield
    for one, two in zip(a.arrivals(), b.arrivals()):
        share(one)
        share(two)
    a.sent()
    b.sent()
    yield
    for copy in done:
        copy.wait()


def scatter_plane(net, at, partial, other, total, wide, thin, result):
    x, y, core = at.x, at.y, at.core
    shared = net.copy(partial.at[:, :, 1 - core], other, at.sibling)
    yield
    shared.wait()

    def add(index, carry):
        i, j = lax.div(index, 4), lax.rem(index, 4)
        total[i, j] = (partial[i, j, core].astype(F32) + other[i, j].astype(F32)).astype(BF16)
        return carry

    lax.fori_loop(0, 16, add, 0)
    a = Scatter(net, lambda j: total.at[:, j, TOP, :], wide.at[0], at.y_ring)
    b = Scatter(net, lambda j: total.at[j, :, LOW, :], wide.at[1], at.x_ring)
    yield
    a.finish()
    add_into(total.at[:, y, TOP, :], wide.at[0, 0], wide.at[0, 1], wide.at[0, 2])
    a = Scatter(net, lambda j: total.at[j, y, TOP, :], thin.at[0], at.x_ring)
    b.finish()
    add_into(total.at[x, :, LOW, :], wide.at[1, 0], wide.at[1, 1], wide.at[1, 2])
    b = Scatter(net, lambda j: total.at[x, j, LOW, :], thin.at[1], at.y_ring)
    yield
    for index, steps, rows in ((0, a, TOP), (1, b, LOW)):
        steps.finish()
        extra = thin[index, 0].astype(F32) + thin[index, 1].astype(F32) + thin[index, 2].astype(F32)
        result(rows, total[x, y, rows, :].astype(F32) + extra)


def plane_scratch(width):
    return [
        pltpu.VMEM((4, 4, 2, 32, width), BF16),
        pltpu.VMEM((4, 4, 32, width), BF16),
        pltpu.VMEM((4, 4, 32, width), BF16),
        pltpu.VMEM((2, 3, 4, 16, width), BF16),
        pltpu.VMEM((2, 3, 16, width), BF16),
    ]


def norm_parts(value):
    center = value - jnp.mean(value, axis=-1, keepdims=True)
    rate = lax.rsqrt(jnp.mean(center * center, axis=-1, keepdims=True) + 1e-05)
    return center * rate, rate


def norm_back(grad, unit, rate, gain):
    inner = grad * gain
    even = jnp.mean(inner, axis=-1, keepdims=True)
    along = jnp.mean(inner * unit, axis=-1, keepdims=True)
    return rate * (inner - even - unit * along)


def column_sum(value):
    return jnp.sum(value, axis=0, keepdims=True)


def split_heads(pair):
    wide = pair.astype(F32)
    lane = lax.broadcasted_iota(jnp.int32, wide.shape, 1)
    both = [jnp.where(lane < 64, wide, 0.0), jnp.where(lane >= 64, wide, 0.0)]
    return jnp.concatenate(both, axis=0).astype(BF16)


def join_heads(wide):
    return jnp.concatenate([wide[0:64, 0:128], wide[64:128, 128:256]], axis=0).T


def slope_row(at, pair):
    first = jnp.where(
        at.z == 0, 1.0, jnp.where(at.z == 1, 0.25, jnp.where(at.z == 2, 0.0625, 0.015625))
    ).astype(F32)
    first = first * jnp.where(pair == 0, 1.0, 0.5).astype(F32)
    lane = lax.broadcasted_iota(jnp.int32, (1, 256), 1)
    return first * jnp.where(lane < 128, 2.0**-0.5, 0.5).astype(F32)


def fill_distance(first_query, dist, base, chunks, start):
    def fill(block, carry):
        lane = lax.broadcasted_iota(jnp.int32, (256, 128), 1)
        query = (lane + first_query).astype(F32)
        key = (lax.broadcasted_iota(jnp.int32, (256, 128), 0) + block * 256).astype(F32)
        apart = query - key
        value = jnp.where((key >= start) & (apart >= 0.0), apart, -1.0)
        rows = pl.ds(pl.multiple_of(base + block * 256, 256), 256)
        dist[rows, 0:128] = value
        dist[rows, 128:256] = value
        return carry

    lax.fori_loop(0, chunks * 2, fill, 0)


def masked_scores(keys, queries, dist, slope):
    raw = dot(keys, queries, 1, 1) * 0.125
    return jnp.where(dist >= 0.0, raw - slope * dist, -1000000000.0)


def key_block(kv, block, first):
    low, y = block // 2, (block % 2) * 2
    return kv[low, y : y + 2, :, :, first : first + 128].reshape(KEYS, 128)


class Chips:
    def __init__(self, at):
        self.steps = []
        for dx in range(2):
            for dy in range(4):
                if dx or dy:
                    low = 1 - at.low if dx else at.low
                    y = turn(at.y, dy)
                    device = at.at(at.seq * 2 + low, y, at.core, at.z)
                    source = (low, turn(at.y, 4 - dy))
                    self.steps.append((dy % 2 == 0, low, y, device, source))

    def swap(self, net, src, dst):
        return [(net.copy(src(low, y), dst, device), source) for _, low, y, device, source in self.steps]

    def swap_even(self, net, src, dst):
        return [
            net.copy(src(low, lax.div(y, 2)), dst, device)
            for even, low, y, device, _ in self.steps
            if even
        ]


def tile_rows(buffer):
    rows = [jnp.concatenate([buffer[i, 0], buffer[i, 1]], axis=1) for i in range(2)]
    return jnp.concatenate(rows, axis=0)


def layer_kernel(
    x_ref, dy_ref, seg_ref, gain1_ref, shift1_ref, wq_ref, qb_ref, wk_ref, wv_ref, vb_ref, wo_ref, ob_ref,
    gain2_ref, shift2_ref, wu_ref, ub_ref, wd_ref, db_ref,
    bo_ref, dxin_ref, dqkv_ref, dwo_ref, dud_ref, sums_ref,
    w1, wo, wu, wd, seg_all, h1_ref, unit1,
    kv_send, q_send, kv, q_all, o_send, o_all, do_send, do_all, dq_send, dq_all,
    sums_kv, kv_out, kv_in, kv_back, kv_own, lse_ref, dist, score, dp_ref,
    part, slots, gathered, dg, g_ref, du_ref, gx, gy, gz,
    dw1, other1, total1, wide1, thin1,
    dwo_part, other_o, total_o, wide_o, thin_o,
    dwu_part, other_u, total_u, wide_u, thin_u,
    dwd_part, other_d, total_d, wide_d, thin_d,
    send, recv,
):
    at = Place()
    net = Net(send, recv)
    chips = Chips(at)
    x, y, z, core, low = at.x, at.y, at.z, at.core, at.low
    pair, odd = lax.div(y, 2), lax.rem(y, 2)
    partners = at.x_ring[1] + at.y_ring[1] + at.z_ring[1] + (at.sibling,)
    partners = partners + tuple(at.at(x, turn(y, step), 1 - core, z) for step in TO)
    partners = partners + tuple(
        at.at(at.seq * 2 + 1 - low, turn(y, step), core, z) for step in TO
    )
    at.greet(partners)

    mine = w1.at[x, y, core]
    mine[:, 0:256] = wq_ref[...]
    mine[:, 256:512] = wk_ref[...]
    mine[:, 512:768] = wv_ref[...]
    w1_steps = gather_plane(net, at, w1)
    next(w1_steps)
    seg_all[low, y, core] = jnp.concatenate([seg_ref[...]] * 4, axis=0)
    seg = Gather(net, lambda j: seg_all.at[low, j, core], at.y_ring)
    wo[x, y, core] = wo_ref[...]
    wu[x, y, core] = wu_ref[...]
    wd[x, y, core] = wd_ref[...]
    unit, _ = norm_parts(x_ref[...].reshape(256, 1024).astype(F32))
    unit1[...] = unit
    h1_ref[...] = (unit * gain1_ref[...] + shift1_ref[...]).astype(BF16)
    next(w1_steps)
    seg.finish()
    view = seg_all.at[low, :, core]
    seg_pair = net.copy(view, view, at.pair)
    wo_steps = gather_plane(net, at, wo)
    next(wo_steps)
    wd_steps = gather_plane(net, at, wd)
    next(wd_steps)
    wu_steps = gather_plane(net, at, wu)
    next(wu_steps)
    next(w1_steps)
    seg_pair.wait()
    view = seg_all.at[:, :, core]
    seg_share = net.copy(view, view, at.sibling)
    run(w1_steps)

    h1 = h1_ref[...]
    wide = dot(h1, w1[:, :, :, :, 256:768].reshape(1024, 512), 1, 0)
    keys = wide[:, 0:256].astype(BF16)
    values = (wide[:, 256:512] + vb_ref[...]).astype(BF16)
    for i in range(2):
        for j in range(2):
            rows, lanes = slice(i * 128, i * 128 + 128), slice(j * 128, j * 128 + 128)
            kv_send[i, j, :, 0:128] = keys[rows, lanes]
            kv_send[i, j, :, 128:256] = values[rows, lanes]
    kv_copies = chips.swap(
        net, lambda to_low, to_y: kv_send.at[to_low, lax.div(to_y, 2)], kv.at[low, y, core]
    )
    kv[low, y, core] = kv_send[low, pair]
    shares = [net.copy(kv.at[low, y, core], kv.at[low, y, core], at.sibling)]
    queries = (dot(h1, w1[:, :, :, :, 0:256].reshape(1024, 256), 1, 0) + qb_ref[...]).astype(BF16)
    for i in range(2):
        for j in range(2):
            q_send[i, j] = queries[i * 128 : i * 128 + 128, j * 128 : j * 128 + 128]
    q_copies = chips.swap_even(
        net, lambda to_low, to_pair: q_send.at[to_low, to_pair], q_all.at[low, pair]
    )
    q_all[low, pair] = q_send[low, pair]
    next(wo_steps)
    seg_share.wait()
    counts = []
    for number in range(1, 4):
        below = (seg_all[:, :, :, 0:2, :] < number).astype(F32)
        below = jnp.sum(below.reshape(16, 2, 128), axis=0)
        below = jnp.sum(below, axis=-1, keepdims=True)
        counts.append(jnp.where(low == 0, below[0:1], below[1:2]))
    bases = [0, 512, 1536, 3072]
    for n in range(4):
        there = seg_all[n // 2, (n % 2) * 2 + odd, core]
        there = jnp.where(low == 0, there[0:1], there[1:2])
        found = jnp.zeros((1, 128), F32)
        for number in range(1, 4):
            found = jnp.where(there == number, counts[number - 1], found)
        first_query = (n * 4 + odd * 2 + core) * 128
        fill_distance(first_query, dist, bases[n], n + 1, found)
    for copy, source in kv_copies:
        copy.wait_recv()
        view = kv.at[source[0], source[1], core]
        shares.append(net.copy(view, view, at.sibling))
    for copy, _ in kv_copies:
        copy.wait_send()
    next(wo_steps)
    next(wd_steps)
    for copy in q_copies + shares:
        copy.wait()

    slope = slope_row(at, pair)
    for n in range(4):
        queries = split_heads(q_all[n // 2, n % 2])
        top = jnp.full((1, 256), -3.0e38, F32)
        for block in range(n + 1):
            rows = slice(block * KEYS, block * KEYS + KEYS)
            value = masked_scores(
                key_block(kv, block, 0), queries,
                dist[bases[n] + block * KEYS : bases[n] + block * KEYS + KEYS, :], slope,
            )
            score[rows, :] = value
            top = jnp.maximum(top, jnp.max(value, axis=0, keepdims=True))
        summed = jnp.zeros((1, 256), F32)
        for block in range(n + 1):
            rows = slice(block * KEYS, block * KEYS + KEYS)
            value = jnp.exp(score[rows, :] - top)
            score[rows, :] = value
            summed = summed + column_sum(value)
        scale = 1.0 / summed
        mixed = jnp.zeros((128, 256), F32)
        for block in range(n + 1):
            rows = slice(block * KEYS, block * KEYS + KEYS)
            probs = (score[rows, :] * scale).astype(BF16)
            mixed = mixed + dot(key_block(kv, block, 128), probs, 0, 0)
        o_send[n // 2, n % 2] = join_heads(mixed).astype(BF16)
        lse_ref[n : n + 1, :] = top + jnp.log(summed)
    copies = chips.swap_even(
        net, lambda to_low, to_pair: o_send.at[to_low, to_pair], o_all.at[low, pair]
    )
    o_all[low, pair] = o_send[low, pair]

    def half(h):
        return slice(h * 32, h * 32 + 32)

    def scatter(index, value):
        part[index] = value.astype(BF16).reshape(4, 64, 1024)

        def one(h):
            return Scatter(
                net, lambda j: part.at[index, j, half(h), :], slots.at[index, h], at.z_ring
            )

        return [one(0), one(1)]

    def owned(index, h):
        extra = slots[index, h, 0].astype(F32) + slots[index, h, 1].astype(F32)
        return part[index, z, half(h), :].astype(F32) + (extra + slots[index, h, 2].astype(F32))

    def gather(buffer, h):
        return Gather(net, lambda j: buffer.at[j, half(h), :], at.z_ring)

    def put_grad(to, first, width, left, right):
        for i in range(4):
            value = dot(left(i), right, 0, 0).astype(BF16)
            to[i, :, :, :, first : first + width] = value.reshape(4, 2, 32, width)

    run(wo_steps)
    for copy in copies:
        copy.wait()
    mixed = tile_rows(o_all)
    steps = scatter(0, dot(mixed, wo[...].reshape(1024, 256), 1, 1))
    next(wu_steps)
    next(wd_steps)
    run(wd_steps)
    dyl = dy_ref[...].reshape(256, 1024)
    down = wd[...].reshape(1024, 1024)
    dg[...] = dot(dyl, down, 1, 0)
    x1, units, rates, gathers = [], [], [], []
    for h in range(2):
        steps[h].finish()
        x1.append(x_ref[z, half(h), :].astype(F32) + owned(0, h) + ob_ref[...])
        unit, rate = norm_parts(x1[h])
        gathered[0, z, half(h), :] = (unit * gain2_ref[...] + shift2_ref[...]).astype(BF16)
        gathers.append(gather(gathered.at[0], h))
        units.append(unit)
        rates.append(rate)
    upstream = [dy_ref[z, half(h), :].astype(F32) for h in range(2)]
    gx[x, 5:6, :] = column_sum(upstream[0]) + column_sum(upstream[1])
    next(wu_steps)
    run(wu_steps)
    up = wu[...].reshape(1024, 1024)
    for steps in gathers:
        steps.finish()
    h2 = gathered[0].reshape(256, 1024)
    for i in range(2):
        cols = slice(i * 512, i * 512 + 512)
        u = dot(h2, wu[:, :, :, :, cols].reshape(1024, 512), 1, 0) + ub_ref[:, cols]
        tanh = jnp.tanh(0.7978845608028654 * (u + 0.044715 * u * u * u))
        g_ref[:, cols] = (0.5 * u * (1.0 + tanh)).astype(BF16)
        turned = 0.5 * u * (1.0 - tanh * tanh) * 0.7978845608028654 * (1.0 + 3 * 0.044715 * u * u)
        du_ref[:, cols] = (dg[:, cols] * (0.5 * (1.0 + tanh) + turned)).astype(BF16)
    du = du_ref[...]
    back = scatter(2, dot(du, up, 1, 1))
    put_grad(
        dwd_part, 0, 1024, lambda i: dy_ref[:, :, i * 256 : i * 256 + 256].reshape(256, 256), g_ref[...]
    )

    def put_d(rows, value):
        dud_ref[rows, 1024:2048] = value

    def put_u(rows, value):
        dud_ref[rows, 0:1024] = value

    dwd_steps = scatter_plane(net, at, dwd_part, other_d, total_d, wide_d, thin_d, put_d)
    next(dwd_steps)
    put_grad(
        dwu_part, 0, 1024, lambda i: gathered[0, :, :, i * 256 : i * 256 + 256].reshape(256, 256), du
    )
    next(dwd_steps)
    dwu_steps = scatter_plane(net, at, dwu_part, other_u, total_u, wide_u, thin_u, put_u)
    next(dwu_steps)
    dx1, dh2, gathers = [], [], []
    for h in range(2):
        back[h].finish()
        dh2.append(owned(2, h))
        dx1.append(upstream[h] + norm_back(dh2[h], units[h], rates[h], gain2_ref[...]))
        gathered[1, z, half(h), :] = dx1[h].astype(BF16)
        gathers.append(gather(gathered.at[1], h))
    ffn = dot(g_ref[...], down, 1, 1)
    gx[x, 3:4, :] = column_sum(dh2[0] * units[0]) + column_sum(dh2[1] * units[1])
    gx[x, 4:5, :] = column_sum(dh2[0]) + column_sum(dh2[1])
    gx[x, 2:3, :] = column_sum(dx1[0]) + column_sum(dx1[1])
    gx[x, 6:7, :] = column_sum(du.astype(F32))
    for steps in gathers:
        steps.finish()
    grads = dot(gathered[1].reshape(256, 1024), wo[...].reshape(1024, 256), 1, 0).astype(BF16)
    for i in range(2):
        for j in range(2):
            do_send[i, j] = grads[i * 128 : i * 128 + 128, j * 128 : j * 128 + 128]
    copies = chips.swap_even(
        net, lambda to_low, to_pair: do_send.at[to_low, to_pair], do_all.at[low, pair]
    )
    do_all[low, pair] = do_send[low, pair]
    front = scatter(1, ffn)
    put_grad(
        dwo_part, 0, 256, lambda i: gathered[1, :, :, i * 256 : i * 256 + 256].reshape(256, 256), mixed
    )

    def put_o(rows, value):
        dwo_ref[rows, :] = value

    dwo_steps = scatter_plane(net, at, dwo_part, other_o, total_o, wide_o, thin_o, put_o)
    next(dwo_steps)
    for copy in copies:
        copy.wait()
    next(dwu_steps)

    for n in (3, 2, 1, 0):
        queries = split_heads(q_all[n // 2, n % 2])
        grads = split_heads(do_all[n // 2, n % 2])
        lse = lse_ref[n : n + 1, :]
        inner = jnp.zeros((1, 256), F32)

        def put_sum(block, lanes, value):
            i, j = block // 2, (block % 2) * 2
            value = value.reshape(2, 2, 128, 128)
            if n < 3:
                value = value + sums_kv[i, j : j + 2, :, :, lanes]
            sums_kv[i, j : j + 2, :, :, lanes] = value

        for block in range(n + 1):
            rows = slice(block * KEYS, block * KEYS + KEYS)
            value = masked_scores(
                key_block(kv, block, 0), queries,
                dist[bases[n] + block * KEYS : bases[n] + block * KEYS + KEYS, :], slope,
            )
            probs = jnp.exp(value - lse)
            prob_grad = dot(key_block(kv, block, 128), grads, 1, 1)
            score[rows, :] = probs
            dp_ref[rows, :] = prob_grad
            inner = inner + column_sum(probs * prob_grad)
            put_sum(block, slice(128, 256), dot(probs.astype(BF16), grads, 1, 0))
        query_grad = jnp.zeros((128, 256), F32)
        for block in range(n + 1):
            rows = slice(block * KEYS, block * KEYS + KEYS)
            score_grad = (score[rows, :] * (dp_ref[rows, :] - inner)).astype(BF16)
            put_sum(block, slice(0, 128), dot(score_grad, queries, 1, 0) * 0.125)
            query_grad = query_grad + dot(key_block(kv, block, 0), score_grad, 0, 0)
        dq_send[n // 2, n % 2] = (join_heads(query_grad) * 0.125).astype(BF16)

    kv_out[...] = sums_kv[:, :, 1 - core].astype(BF16)
    shared = net.copy(kv_out, kv_in, at.sibling)
    dq_copies = chips.swap_even(
        net, lambda to_low, to_pair: dq_send.at[to_low, to_pair], dq_all.at[low, pair]
    )
    dq_all[low, pair] = dq_send[low, pair]
    shared.wait()
    kv_back[...] = (sums_kv[:, :, core] + kv_in[...].astype(F32)).astype(BF16)
    kv_copies = chips.swap(
        net, lambda to_low, to_y: kv_back.at[to_low, to_y], kv_own.at[low, y]
    )
    kv_own[low, y] = kv_back[low, y]
    outs = []
    for h in range(2):
        front[h].finish()
        bo_ref[z, half(h), :] = (x1[h] + owned(1, h) + db_ref[...]).astype(BF16)
        outs.append(gather(bo_ref, h))
    h1 = h1_ref[...]

    def left(i):
        return h1[:, i * 256 : i * 256 + 256]

    for copy in dq_copies:
        copy.wait()
    dq = tile_rows(dq_all)
    put_grad(dw1, 0, 256, left, dq)
    direct = dot(dq, w1[:, :, :, :, 0:256].reshape(1024, 256), 1, 1)
    for copy, _ in kv_copies:
        copy.wait()
    whole = []
    for i in range(2):
        tiles = [
            (kv_own[i, j * 2].astype(F32) + kv_own[i, j * 2 + 1].astype(F32)).astype(BF16)
            for j in range(2)
        ]
        whole.append(
            jnp.concatenate(
                [tiles[0][:, 0:128], tiles[1][:, 0:128], tiles[0][:, 128:256], tiles[1][:, 128:256]],
                axis=1,
            )
        )
    dkv = jnp.concatenate(whole, axis=0)
    direct = direct + dot(dkv, w1[:, :, :, :, 256:768].reshape(1024, 512), 1, 1)
    steps = scatter(3, direct)
    gx[x, 0:1, :] = column_sum(direct * unit1[...])
    gx[x, 1:2, :] = column_sum(direct)
    gx[x, 7:8, 0:256] = column_sum(dq.astype(F32))
    gx[x, 7:8, 256:512] = column_sum(dkv[:, 256:512].astype(F32))
    gx[x, 7:8, 512:1024] = jnp.zeros((1, 512), F32)
    small = Gather(net, lambda j: gx.at[j], at.x_ring)
    put_grad(dw1, 256, 512, left, dkv)

    def put1(rows, value):
        dqkv_ref[rows, :] = value

    dw1_steps = scatter_plane(net, at, dw1, other1, total1, wide1, thin1, put1)
    next(dw1_steps)
    small.finish()
    own = gy.at[y, core]
    gy[y, core] = gx[0] + gx[1] + gx[2] + gx[3]
    small = [net.copy(own, own, device) for device in at.y_ring[1] + (at.sibling,)]
    small = small + [net.copy(own, own, at.at(x, turn(y, step), 1 - core, z)) for step in TO]
    next(dwd_steps)
    next(dwu_steps)
    next(dwo_steps)
    next(dw1_steps)
    gathers = []
    for h in range(2):
        steps[h].finish()
        unit, rate = norm_parts(x_ref[z, half(h), :].astype(F32))
        grad = dx1[h] + norm_back(owned(3, h), unit, rate, gain1_ref[...])
        dxin_ref[z, half(h), :] = grad.astype(BF16)
        gathers.append(gather(dxin_ref, h))
    for copy in small:
        copy.wait()
    total = gy[0, 0] + gy[0, 1]
    for i in range(1, 4):
        total = total + gy[i, 0] + gy[i, 1]
    gz[z] = total
    small = Gather(net, lambda j: gz.at[j], at.z_ring)
    next(dwo_steps)
    next(dw1_steps)
    for steps in (dwd_steps, dwu_steps, dwo_steps, dw1_steps):
        run(steps)
    small.finish()
    sums_ref[0:6, :] = gz[0, 0:6, :] + gz[1, 0:6, :] + gz[2, 0:6, :] + gz[3, 0:6, :]
    sums_ref[6:8, :] = gz[z, 6:8, :]
    for steps in outs + gathers:
        steps.finish()


def write_kernel(
    bo_ref, dxin_ref, dqkv_ref, dwo_ref, dud_ref, sums_ref,
    block_ref, input_ref, g1_ref, s1_ref, dwq_ref, qb_ref, dwk_ref, dwv_ref, vb_ref, out_ref,
    ob_ref, g2_ref, s2_ref, dwu_ref, ub_ref, dwd_ref, db_ref,
):
    block_ref[...] = bo_ref[...].astype(F32)
    input_ref[...] = dxin_ref[...].astype(F32)
    dwq_ref[...] = dqkv_ref[:, 0:256]
    dwk_ref[...] = dqkv_ref[:, 256:512]
    dwv_ref[...] = dqkv_ref[:, 512:768]
    out_ref[...] = dwo_ref[...]
    dwu_ref[...] = dud_ref[:, 0:1024]
    dwd_ref[...] = dud_ref[:, 1024:2048]
    for index, ref in enumerate((g1_ref, s1_ref, ob_ref, g2_ref, s2_ref, db_ref, ub_ref)):
        ref[...] = sums_ref[index : index + 1, :]
    qb_ref[...] = sums_ref[7:8, 0:256]
    vb_ref[...] = sums_ref[7:8, 256:512]


def on_device(
    block_input, first_gain, first_shift, query_weight, query_bias, key_weight, value_weight, value_bias,
    output_weight, output_bias, second_gain, second_shift, up_weight, up_bias, down_weight, down_bias,
    segments, out_cotangent,
):
    vmem = pl.BlockSpec(memory_space=pltpu.VMEM)

    def row(value):
        return value.reshape(1, -1)

    def shapes(*pairs):
        return [jax.ShapeDtypeStruct(shape, kind) for shape, kind in pairs]

    results = pl.pallas_call(
        layer_kernel,
        out_shape=shapes(
            ((4, 64, 1024), BF16),
            ((4, 64, 1024), BF16),
            ((32, 768), F32),
            ((32, 256), F32),
            ((32, 2048), F32),
            ((8, 1024), F32),
        ),
        in_specs=[vmem] * 18,
        out_specs=[vmem] * 6,
        scratch_shapes=[
            pltpu.VMEM((4, 4, 2, 32, 768), BF16),
            pltpu.VMEM((4, 4, 2, 32, 256), BF16),
            pltpu.VMEM((4, 4, 2, 32, 1024), BF16),
            pltpu.VMEM((4, 4, 2, 32, 1024), BF16),
            pltpu.VMEM((2, 4, 2, 8, 128), jnp.int32),
            pltpu.VMEM((256, 1024), BF16),
            pltpu.VMEM((256, 1024), F32),
            pltpu.VMEM((2, 2, 128, 256), BF16),
            pltpu.VMEM((2, 2, 128, 128), BF16),
            pltpu.VMEM((2, 4, 2, 128, 256), BF16),
            *[pltpu.VMEM((2, 2, 128, 128), BF16)] * 7,
            pltpu.VMEM((2, 4, 2, 128, 256), F32),
            *[pltpu.VMEM((2, 4, 128, 256), BF16)] * 4,
            pltpu.VMEM((4, 256), F32),
            pltpu.VMEM((5120, 256), F32),
            pltpu.VMEM((2048, 256), F32),
            pltpu.VMEM((2048, 256), F32),
            pltpu.VMEM((4, 4, 64, 1024), BF16),
            pltpu.VMEM((4, 2, 3, 32, 1024), BF16),
            pltpu.VMEM((2, 4, 64, 1024), BF16),
            pltpu.VMEM((256, 1024), F32),
            pltpu.VMEM((256, 1024), BF16),
            pltpu.VMEM((256, 1024), BF16),
            pltpu.VMEM((4, 8, 1024), F32),
            pltpu.VMEM((4, 2, 8, 1024), F32),
            pltpu.VMEM((4, 8, 1024), F32),
            *plane_scratch(768),
            *plane_scratch(256),
            *plane_scratch(1024),
            *plane_scratch(1024),
            pltpu.SemaphoreType.DMA((COPIES,)),
            pltpu.SemaphoreType.DMA((COPIES,)),
        ],
        compiler_params=pltpu.CompilerParams(
            collective_id=1, has_side_effects=True, vmem_limit_bytes=VMEM_BYTES
        ),
        cost_estimate=pl.CostEstimate(
            flops=10_000_000_000, bytes_accessed=16_000_000, transcendentals=0
        ),
        name="layer",
    )(
        block_input.reshape(4, 64, 1024), out_cotangent.reshape(4, 64, 1024), segments.reshape(2, 128),
        row(first_gain), row(first_shift), query_weight, row(query_bias), key_weight, value_weight,
        row(value_bias), output_weight, row(output_bias), row(second_gain), row(second_shift), up_weight,
        row(up_bias), down_weight, row(down_bias),
    )
    wide, narrow = ((1, 1024), F32), ((1, 256), F32)
    square, tall, tokens = ((32, 256), F32), ((32, 1024), F32), ((4, 64, 1024), F32)
    outs = pl.pallas_call(
        write_kernel,
        out_shape=shapes(
            tokens, tokens, wide, wide, square, narrow, square, square, narrow, square, wide, wide, wide,
            tall, wide, tall, wide,
        ),
        in_specs=[vmem] * 6,
        out_specs=[vmem] * 17,
        name="write",
    )(*results)
    ends = {0: (2, 1, 128, 1024), 1: (2, 1, 128, 1024)}
    flat = (2, 3, 5, 8, 10, 11, 12, 14, 16)
    return tuple(
        out.reshape(ends[i]) if i in ends else (out.reshape(-1) if i in flat else out)
        for i, out in enumerate(outs)
    )


def solution(mesh):
    tokens = P(None, "seq", "ctx", None)
    matrix = P(("seq", "ctx"), "head")
    return jax.shard_map(
        on_device,
        mesh=mesh,
        in_specs=(
            tokens, P(), P(), matrix, P("head"), matrix, matrix, P("head"), matrix, P(), P(), P(),
            matrix, P("head"), matrix, P(), P(None, "seq", "ctx"), tokens,
        ),
        out_specs=(
            tokens, tokens, P(), P(), matrix, P("head"), matrix, matrix, P("head"), matrix, P(), P(),
            P(), matrix, P("head"), matrix, P(),
        ),
        check_vma=False,
    )
```

```python
import jax
import jax.numpy as jnp
from jax import lax
from jax.experimental import pallas as pl
from jax.experimental.pallas import tpu as pltpu
from jax.sharding import PartitionSpec as P

F32 = jnp.float32
BF16 = jnp.bfloat16
MESH = pl.DeviceIdType.MESH
VMEM_BYTES = 56 * 1024 * 1024
KEYS = 512
COPIES = 225
SENDS = 40


def dot(left, right, dim_left, dim_right):
    return lax.dot_general(
        left, right, (((dim_left,), (dim_right,)), ((), ())), preferred_element_type=F32
    )


def turn(index, by):
    return lax.rem(index + by, 4)


class Place:
    def __init__(self):
        self.seq = lax.axis_index("seq")
        self.ctx = lax.axis_index("ctx")
        self.z = lax.axis_index("head")
        self.core = lax.rem(self.ctx, 2)
        self.y = lax.rem(lax.div(self.ctx, 2), 4)
        self.low = lax.div(self.ctx, 8)
        self.x = self.seq * 2 + self.low
        self.x_plus = self.at(turn(self.x, 1), self.y, self.core, self.z)
        self.x_minus = self.at(turn(self.x, 3), self.y, self.core, self.z)
        self.y_plus = self.at(self.x, turn(self.y, 1), self.core, self.z)
        self.y_minus = self.at(self.x, turn(self.y, 3), self.core, self.z)
        self.z_plus = self.at(self.x, self.y, self.core, turn(self.z, 1))
        self.z_minus = self.at(self.x, self.y, self.core, turn(self.z, 3))
        self.x_across = self.at(turn(self.x, 2), self.y, self.core, self.z)
        self.y_across = self.at(self.x, turn(self.y, 2), self.core, self.z)
        self.z_across = self.at(self.x, self.y, self.core, turn(self.z, 2))
        self.x_ring = (self.x, (self.x_plus, self.x_minus, self.x_across))
        self.y_ring = (self.y, (self.y_plus, self.y_minus, self.y_across))
        self.z_ring = (self.z, (self.z_plus, self.z_minus, self.z_across))
        self.sibling = self.at(self.x, self.y, 1 - self.core, self.z)
        self.pair = self.at(self.seq * 2 + 1 - self.low, self.y, self.core, self.z)

    def at(self, x, y, core, z):
        return (lax.div(x, 2), (lax.rem(x, 2) * 4 + y) * 2 + core, z)

    def greet(self, partners):
        barrier = pltpu.get_barrier_semaphore()
        for partner in partners:
            pl.semaphore_signal(barrier, inc=1, device_id=partner, device_id_type=MESH)
        pl.semaphore_wait(barrier, len(partners))


class Copy:
    def __init__(self, net, made, index):
        self.net, self.made, self.index = net, made, index

    def wait_recv(self):
        self.made.wait_recv()

    def wait_send(self):
        self.made.wait_send()
        self.net.free.append(self.index)

    def wait(self):
        self.wait_send()
        self.wait_recv()


class Net:
    def __init__(self, send, recv):
        self.send, self.recv, self.used, self.free, self.most = send, recv, 0, [], 0

    def copy(self, src, dst, device):
        index = self.free.pop() if self.free else self.most
        self.most = max(self.most, index + 1)
        made = pltpu.make_async_remote_copy(
            src_ref=src,
            dst_ref=dst,
            send_sem=self.send.at[index],
            recv_sem=self.recv.at[self.used],
            device_id=device,
            device_id_type=MESH,
        )
        self.used += 1
        made.start()
        return Copy(self, made, index)


def run(steps):
    for _ in steps:
        pass


FROM = (3, 1, 2)
TO = (1, 3, 2)


def add_into(view, *others):
    value = view[...].astype(F32)
    for other in others:
        value = value + other[...].astype(F32)
    view[...] = value.astype(BF16)


class Gather:
    def __init__(self, net, region, ring):
        self.here, others = ring
        own = region(self.here)
        self.region = region
        self.copies = [net.copy(own, own, device) for device in others]

    def arrivals(self):
        for copy, step in zip(self.copies, FROM):
            copy.wait_recv()
            yield self.region(turn(self.here, step))

    def sent(self):
        for copy in self.copies:
            copy.wait_send()

    def finish(self):
        for _ in self.arrivals():
            pass
        self.sent()


class Scatter:
    def __init__(self, net, part, slots, ring):
        here, others = ring
        self.copies = [
            net.copy(part(turn(here, step)), slots.at[index], device)
            for index, (step, device) in enumerate(zip(TO, others))
        ]

    def finish(self):
        for copy in self.copies:
            copy.wait()


TOP, LOW = slice(0, 16), slice(16, 32)


def gather_plane(net, at, full, urgent=False):
    x, y, core = at.x, at.y, at.core
    done = []

    def share(view):
        done.append(net.copy(view, view, at.sibling))

    a = Gather(net, lambda j: full.at[j, y, core, TOP, :], at.x_ring)
    b = Gather(net, lambda j: full.at[x, j, core, LOW, :], at.y_ring)
    yield
    a.finish()
    a = Gather(net, lambda j: full.at[:, j, core, TOP, :], at.y_ring)
    b.finish()
    b = Gather(net, lambda j: full.at[j, :, core, LOW, :], at.x_ring)
    if urgent:
        share(full.at[:, y, core, TOP, :])
        share(full.at[x, :, core, LOW, :])
    yield
    for one, two in zip(a.arrivals(), b.arrivals()):
        if urgent:
            share(one)
            share(two)
    if not urgent:
        share(full.at[:, :, core])
    a.sent()
    b.sent()
    yield
    for copy in done:
        copy.wait()


def scatter_plane(net, at, partial, other, total, wide, thin, result):
    x, y, core = at.x, at.y, at.core
    shared = net.copy(partial.at[:, :, 1 - core], other, at.sibling)
    yield
    shared.wait()

    def add(index, carry):
        i, j = lax.div(index, 4), lax.rem(index, 4)
        total[i, j] = (partial[i, j, core].astype(F32) + other[i, j].astype(F32)).astype(BF16)
        return carry

    lax.fori_loop(0, 16, add, 0)
    a = Scatter(net, lambda j: total.at[:, j, TOP, :], wide.at[0], at.y_ring)
    b = Scatter(net, lambda j: total.at[j, :, LOW, :], wide.at[1], at.x_ring)
    yield
    a.finish()
    add_into(total.at[:, y, TOP, :], wide.at[0, 0], wide.at[0, 1], wide.at[0, 2])
    a = Scatter(net, lambda j: total.at[j, y, TOP, :], thin.at[0], at.x_ring)
    b.finish()
    add_into(total.at[x, :, LOW, :], wide.at[1, 0], wide.at[1, 1], wide.at[1, 2])
    b = Scatter(net, lambda j: total.at[x, j, LOW, :], thin.at[1], at.y_ring)
    yield
    for index, steps, rows in ((0, a, TOP), (1, b, LOW)):
        steps.finish()
        extra = thin[index, 0].astype(F32) + thin[index, 1].astype(F32) + thin[index, 2].astype(F32)
        result(rows, total[x, y, rows, :].astype(F32) + extra)


def sum_small(net, at, by_x, by_y, by_z):
    x, y, z, core = at.x, at.y, at.z, at.core
    steps = Gather(net, lambda j: by_x.at[j], at.x_ring)
    yield
    steps.finish()
    by_y[y, core] = by_x[0] + by_x[1] + by_x[2] + by_x[3]
    own = by_y.at[y, core]
    copies = [net.copy(own, own, device) for device in at.y_ring[1] + (at.sibling,)]
    copies = copies + [net.copy(own, own, at.at(x, turn(y, step), 1 - core, z)) for step in TO]
    yield
    for copy in copies:
        copy.wait()
    total = by_y[0, 0] + by_y[0, 1]
    for i in range(1, 4):
        total = total + by_y[i, 0] + by_y[i, 1]
    by_z[z] = total
    steps = Gather(net, lambda j: by_z.at[j], at.z_ring)
    yield
    steps.finish()


def plane_scratch(width):
    return [
        pltpu.VMEM((4, 4, 2, 32, width), BF16),
        pltpu.VMEM((4, 4, 32, width), BF16),
        pltpu.VMEM((4, 4, 32, width), BF16),
        pltpu.VMEM((2, 3, 4, 16, width), BF16),
        pltpu.VMEM((2, 3, 16, width), BF16),
    ]


def norm_parts(value):
    center = value - jnp.mean(value, axis=-1, keepdims=True)
    rate = lax.rsqrt(jnp.mean(center * center, axis=-1, keepdims=True) + 1e-05)
    return center * rate, rate


def norm_back(grad, unit, rate, gain):
    inner = grad * gain
    even = jnp.mean(inner, axis=-1, keepdims=True)
    along = jnp.mean(inner * unit, axis=-1, keepdims=True)
    return rate * (inner - even - unit * along)


def column_sum(value):
    return jnp.sum(value, axis=0, keepdims=True)


def split_heads(pair):
    wide = pair.astype(F32)
    lane = lax.broadcasted_iota(jnp.int32, wide.shape, 1)
    both = [jnp.where(lane < 64, wide, 0.0), jnp.where(lane >= 64, wide, 0.0)]
    return jnp.concatenate(both, axis=0).astype(BF16)


def join_heads(wide):
    return jnp.concatenate([wide[0:64, 0:128], wide[64:128, 128:256]], axis=0).T


def slope_row(at, pair):
    first = jnp.where(
        at.z == 0, 1.0, jnp.where(at.z == 1, 0.25, jnp.where(at.z == 2, 0.0625, 0.015625))
    ).astype(F32)
    first = first * jnp.where(pair == 0, 1.0, 0.5).astype(F32)
    lane = lax.broadcasted_iota(jnp.int32, (1, 256), 1)
    return first * jnp.where(lane < 128, 2.0**-0.5, 0.5).astype(F32)


def fill_distance(first_query, dist, base, chunks, start):
    def fill(block, carry):
        lane = lax.broadcasted_iota(jnp.int32, (256, 128), 1)
        query = (lane + first_query).astype(F32)
        key = (lax.broadcasted_iota(jnp.int32, (256, 128), 0) + block * 256).astype(F32)
        apart = query - key
        value = jnp.where((key >= start) & (apart >= 0.0), apart, -1.0)
        rows = pl.ds(pl.multiple_of(base + block * 256, 256), 256)
        dist[rows, 0:128] = value
        dist[rows, 128:256] = value
        return carry

    lax.fori_loop(0, chunks * 2, fill, 0)


def masked_scores(keys, queries, dist, slope):
    raw = dot(keys, queries, 1, 1) * 0.125
    return jnp.where(dist >= 0.0, raw - slope * dist, -1000000000.0)


def key_block(kv, block, first):
    low, y = block // 2, (block % 2) * 2
    return kv[low, y : y + 2, :, :, first : first + 128].reshape(KEYS, 128)


class Chips:
    def __init__(self, at):
        self.steps = []
        for dx in range(2):
            for dy in range(4):
                if dx or dy:
                    low = 1 - at.low if dx else at.low
                    y = turn(at.y, dy)
                    device = at.at(at.seq * 2 + low, y, at.core, at.z)
                    source = (low, turn(at.y, 4 - dy))
                    self.steps.append((dy % 2 == 0, low, y, device, source))

    def swap(self, net, src, dst):
        return [(net.copy(src(low, y), dst, device), source) for _, low, y, device, source in self.steps]

    def swap_even(self, net, src, dst):
        return [
            net.copy(src(low, lax.div(y, 2)), dst, device)
            for even, low, y, device, _ in self.steps
            if even
        ]


def tile_rows(buffer):
    rows = [jnp.concatenate([buffer[i, 0], buffer[i, 1]], axis=1) for i in range(2)]
    return jnp.concatenate(rows, axis=0)


def layer_kernel(
    x_ref, dy_ref, seg_ref, gain1_ref, shift1_ref, wq_ref, qb_ref, wk_ref, wv_ref, vb_ref, wo_ref, ob_ref,
    gain2_ref, shift2_ref, wu_ref, ub_ref, wd_ref, db_ref,
    bo_ref, dxin_ref, dqkv_ref, dwo_ref, dud_ref, sums_ref,
    w1, wo, wu, wd, seg_all, h1_ref, unit1,
    kv_send, q_send, kv, q_all, o_send, o_all, do_send, do_all, dq_send, dq_all,
    sums_kv, kv_out, kv_in, kv_back, kv_own, dist, score, dp_ref,
    part, slots, gathered, dg, g_ref, du_ref, gx, gy, gz, hx, hy, hz,
    dw1, other1, total1, wide1, thin1,
    dwq, other_q, total_q, wide_q, thin_q,
    dwu_part, other_u, total_u, wide_u, thin_u,
    dwd_part, other_d, total_d, wide_d, thin_d,
    send, recv,
):
    at = Place()
    net = Net(send, recv)
    chips = Chips(at)
    x, y, z, core, low = at.x, at.y, at.z, at.core, at.low
    pair, odd = lax.div(y, 2), lax.rem(y, 2)
    partners = at.x_ring[1] + at.y_ring[1] + at.z_ring[1] + (at.sibling,)
    partners = partners + tuple(at.at(x, turn(y, step), 1 - core, z) for step in TO)
    partners = partners + tuple(
        at.at(at.seq * 2 + 1 - low, turn(y, step), core, z) for step in TO
    )
    at.greet(partners)

    mine = w1.at[x, y, core]
    mine[:, 0:256] = wq_ref[...]
    mine[:, 256:512] = wk_ref[...]
    mine[:, 512:768] = wv_ref[...]
    w1_steps = gather_plane(net, at, w1, urgent=True)
    next(w1_steps)
    seg_all[low, y, core] = jnp.concatenate([seg_ref[...]] * 4, axis=0)
    seg = Gather(net, lambda j: seg_all.at[low, j, core], at.y_ring)
    wo[x, y, core] = wo_ref[...]
    wu[x, y, core] = wu_ref[...]
    wd[x, y, core] = wd_ref[...]
    unit, _ = norm_parts(x_ref[...].reshape(256, 1024).astype(F32))
    unit1[...] = unit
    h1_ref[...] = (unit * gain1_ref[...] + shift1_ref[...]).astype(BF16)
    next(w1_steps)
    seg.finish()
    view = seg_all.at[low, :, core]
    seg_pair = net.copy(view, view, at.pair)
    next(w1_steps)
    wo_steps = gather_plane(net, at, wo)
    next(wo_steps)
    wd_steps = gather_plane(net, at, wd)
    next(wd_steps)
    wu_steps = gather_plane(net, at, wu)
    next(wu_steps)
    seg_pair.wait()
    view = seg_all.at[:, :, core]
    seg_share = net.copy(view, view, at.sibling)
    run(w1_steps)

    h1 = h1_ref[...]
    wide = dot(h1, w1[:, :, :, :, 256:768].reshape(1024, 512), 1, 0)
    keys = wide[:, 0:256].astype(BF16)
    values = (wide[:, 256:512] + vb_ref[...]).astype(BF16)
    for i in range(2):
        for j in range(2):
            rows, lanes = slice(i * 128, i * 128 + 128), slice(j * 128, j * 128 + 128)
            kv_send[i, j, :, 0:128] = keys[rows, lanes]
            kv_send[i, j, :, 128:256] = values[rows, lanes]
    kv_copies = chips.swap(
        net, lambda to_low, to_y: kv_send.at[to_low, lax.div(to_y, 2)], kv.at[low, y, core]
    )
    kv[low, y, core] = kv_send[low, pair]
    shares = []
    queries = (dot(h1, w1[:, :, :, :, 0:256].reshape(1024, 256), 1, 0) + qb_ref[...]).astype(BF16)
    for i in range(2):
        for j in range(2):
            q_send[i, j] = queries[i * 128 : i * 128 + 128, j * 128 : j * 128 + 128]
    q_copies = chips.swap_even(
        net, lambda to_low, to_pair: q_send.at[to_low, to_pair], q_all.at[low, pair]
    )
    q_all[low, pair] = q_send[low, pair]
    next(wo_steps)
    seg_share.wait()
    counts = []
    for number in range(1, 4):
        below = (seg_all[:, :, :, 0:2, :] < number).astype(F32)
        below = jnp.sum(below.reshape(16, 2, 128), axis=0)
        below = jnp.sum(below, axis=-1, keepdims=True)
        counts.append(jnp.where(low == 0, below[0:1], below[1:2]))
    bases = [0, 512, 1536, 3072]
    for n in range(4):
        there = seg_all[n // 2, (n % 2) * 2 + odd, core]
        there = jnp.where(low == 0, there[0:1], there[1:2])
        found = jnp.zeros((1, 128), F32)
        for number in range(1, 4):
            found = jnp.where(there == number, counts[number - 1], found)
        first_query = (n * 4 + odd * 2 + core) * 128
        fill_distance(first_query, dist, bases[n], n + 1, found)
    for index, (copy, source) in enumerate(kv_copies):
        copy.wait_recv()
        if index == 2:
            view = kv.at[low, :, core]
            shares.append(net.copy(view, view, at.sibling))
        if index > 2:
            view = kv.at[source[0], source[1], core]
            shares.append(net.copy(view, view, at.sibling))
    for copy, _ in kv_copies:
        copy.wait_send()
    next(wd_steps)
    for copy in q_copies:
        copy.wait()
    for copy in shares:
        copy.wait()

    slope = slope_row(at, pair)
    for n in range(4):
        queries = split_heads(q_all[n // 2, n % 2])
        top = jnp.full((1, 256), -3.0e38, F32)
        for block in range(n + 1):
            rows = slice(block * KEYS, block * KEYS + KEYS)
            value = masked_scores(
                key_block(kv, block, 0), queries,
                dist[bases[n] + block * KEYS : bases[n] + block * KEYS + KEYS, :], slope,
            )
            score[rows, :] = value
            top = jnp.maximum(top, jnp.max(value, axis=0, keepdims=True))
        summed = jnp.zeros((1, 256), F32)
        for block in range(n + 1):
            rows = slice(block * KEYS, block * KEYS + KEYS)
            value = jnp.exp(score[rows, :] - top)
            score[rows, :] = value
            summed = summed + column_sum(value)
        scale = 1.0 / summed
        mixed = jnp.zeros((128, 256), F32)
        for block in range(n + 1):
            rows = slice(block * KEYS, block * KEYS + KEYS)
            probs = score[rows, :] * scale
            dist[bases[n] + block * KEYS : bases[n] + block * KEYS + KEYS, :] = probs
            mixed = mixed + dot(key_block(kv, block, 128), probs.astype(BF16), 0, 0)
        o_send[n // 2, n % 2] = join_heads(mixed).astype(BF16)
    copies = chips.swap_even(
        net, lambda to_low, to_pair: o_send.at[to_low, to_pair], o_all.at[low, pair]
    )
    o_all[low, pair] = o_send[low, pair]
    next(wo_steps)

    def half(h):
        return slice(h * 32, h * 32 + 32)

    def scatter_half(index, h):
        return Scatter(net, lambda j: part.at[index, j, half(h), :], slots.at[index, h], at.z_ring)

    def scatter(index, value):
        part[index] = value.astype(BF16).reshape(4, 64, 1024)
        return [scatter_half(index, 0), scatter_half(index, 1)]

    def owned(index, h):
        extra = slots[index, h, 0].astype(F32) + slots[index, h, 1].astype(F32)
        return part[index, z, half(h), :].astype(F32) + (extra + slots[index, h, 2].astype(F32))

    def gather(buffer, h):
        return Gather(net, lambda j: buffer.at[j, half(h), :], at.z_ring)

    def put_grad(to, first, width, left, right):
        for i in range(4):
            value = dot(left(i), right, 0, 0).astype(BF16)
            to[i, :, :, :, first : first + width] = value.reshape(4, 2, 32, width)

    run(wo_steps)
    for copy in copies:
        copy.wait()
    next(wu_steps)
    mixed = tile_rows(o_all)
    steps = scatter(0, dot(mixed, wo[...].reshape(1024, 256), 1, 1))
    next(wd_steps)
    x1, units, rates, gathers = [], [], [], []
    for h in range(2):
        steps[h].finish()
        x1.append(x_ref[z, half(h), :].astype(F32) + owned(0, h) + ob_ref[...])
        unit, rate = norm_parts(x1[h])
        gathered[0, z, half(h), :] = (unit * gain2_ref[...] + shift2_ref[...]).astype(BF16)
        gathers.append(gather(gathered.at[0], h))
        units.append(unit)
        rates.append(rate)
    upstream = [dy_ref[z, half(h), :].astype(F32) for h in range(2)]
    gx[x] = jnp.zeros((8, 1024), F32)
    gx[x, 5:6, :] = column_sum(upstream[0]) + column_sum(upstream[1])
    next(wu_steps)
    run(wd_steps)
    down = wd[...].reshape(1024, 1024)
    dg[...] = dot(dy_ref[...].reshape(256, 1024), down, 1, 0).reshape(4, 64, 1024)
    run(wu_steps)
    up = wu[...].reshape(1024, 1024)
    back = []
    for h in range(2):
        gathers[h].finish()
        h2 = gathered[0, :, half(h), :].reshape(128, 1024)
        for i in range(2):
            cols = slice(i * 512, i * 512 + 512)
            u = dot(h2, wu[:, :, :, :, cols].reshape(1024, 512), 1, 0) + ub_ref[:, cols]
            tanh = jnp.tanh(0.7978845608028654 * (u + 0.044715 * u * u * u))
            g_ref[:, half(h), cols] = (0.5 * u * (1.0 + tanh)).astype(BF16).reshape(4, 32, 512)
            turned = 0.5 * u * (1.0 - tanh * tanh) * 0.7978845608028654 * (1.0 + 3 * 0.044715 * u * u)
            turned = (0.5 * (1.0 + tanh) + turned).reshape(4, 32, 512)
            du_ref[:, half(h), cols] = (dg[:, half(h), cols] * turned).astype(BF16)
        value = dot(du_ref[:, half(h), :].reshape(128, 1024), up, 1, 1).astype(BF16)
        part[2, :, half(h), :] = value.reshape(4, 32, 1024)
        back.append(scatter_half(2, h))
    du = du_ref[...].reshape(256, 1024)
    g = g_ref[...].reshape(256, 1024)
    put_grad(
        dwd_part, 0, 1024, lambda i: dy_ref[:, :, i * 256 : i * 256 + 256].reshape(256, 256), g
    )

    def put_d(rows, value):
        dud_ref[rows, 1024:2048] = value

    def put_u(rows, value):
        dud_ref[rows, 0:1024] = value

    dwd_steps = scatter_plane(net, at, dwd_part, other_d, total_d, wide_d, thin_d, put_d)
    next(dwd_steps)
    put_grad(
        dwu_part, 0, 1024, lambda i: gathered[0, :, :, i * 256 : i * 256 + 256].reshape(256, 256), du
    )
    dwu_steps = scatter_plane(net, at, dwu_part, other_u, total_u, wide_u, thin_u, put_u)
    next(dwu_steps)
    dx1, dh2, gathers = [], [], []
    for h in range(2):
        back[h].finish()
        dh2.append(owned(2, h))
        dx1.append(upstream[h] + norm_back(dh2[h], units[h], rates[h], gain2_ref[...]))
        gathered[1, z, half(h), :] = dx1[h].astype(BF16)
        gathers.append(gather(gathered.at[1], h))
        if h == 0:
            next(dwd_steps)
    gx[x, 3:4, :] = column_sum(dh2[0] * units[0]) + column_sum(dh2[1] * units[1])
    gx[x, 4:5, :] = column_sum(dh2[0]) + column_sum(dh2[1])
    gx[x, 2:3, :] = column_sum(dx1[0]) + column_sum(dx1[1])
    gx[x, 6:7, :] = column_sum(du.astype(F32))
    early = sum_small(net, at, gx, gy, gz)
    next(early)
    ffn = dot(g, down, 1, 1)
    for steps in gathers:
        steps.finish()
    grads = dot(gathered[1].reshape(256, 1024), wo[...].reshape(1024, 256), 1, 0).astype(BF16)
    for i in range(2):
        for j in range(2):
            do_send[i, j] = grads[i * 128 : i * 128 + 128, j * 128 : j * 128 + 128]
    copies = chips.swap_even(
        net, lambda to_low, to_pair: do_send.at[to_low, to_pair], do_all.at[low, pair]
    )
    do_all[low, pair] = do_send[low, pair]
    front = scatter(1, ffn)
    put_grad(
        dwq, 256, 256, lambda i: gathered[1, :, :, i * 256 : i * 256 + 256].reshape(256, 256), mixed
    )
    for copy in copies:
        copy.wait()
    next(early)
    next(dwd_steps)
    next(dwu_steps)

    shared = []
    for n in (3, 2, 1, 0):
        queries = split_heads(q_all[n // 2, n % 2])
        grads = split_heads(do_all[n // 2, n % 2])
        inner = jnp.zeros((1, 256), F32)

        def put_sum(block, lanes, value):
            i, j = block // 2, (block % 2) * 2
            value = value.reshape(2, 2, 128, 128)
            if n < 3:
                value = value + sums_kv[i, j : j + 2, :, :, lanes]
            sums_kv[i, j : j + 2, :, :, lanes] = value

        for block in range(n + 1):
            rows = slice(block * KEYS, block * KEYS + KEYS)
            probs = dist[bases[n] + block * KEYS : bases[n] + block * KEYS + KEYS, :]
            prob_grad = dot(key_block(kv, block, 128), grads, 1, 1)
            dp_ref[rows, :] = prob_grad
            inner = inner + column_sum(probs * prob_grad)
            put_sum(block, slice(128, 256), dot(probs.astype(BF16), grads, 1, 0))
        query_grad = jnp.zeros((128, 256), F32)
        for block in range(n + 1):
            rows = slice(block * KEYS, block * KEYS + KEYS)
            probs = dist[bases[n] + block * KEYS : bases[n] + block * KEYS + KEYS, :]
            score_grad = (probs * (dp_ref[rows, :] - inner)).astype(BF16)
            put_sum(block, slice(0, 128), dot(score_grad, queries, 1, 0) * 0.125)
            query_grad = query_grad + dot(key_block(kv, block, 0), score_grad, 0, 0)
        dq_send[n // 2, n % 2] = (join_heads(query_grad) * 0.125).astype(BF16)
        i, chunk = n // 2, slice((n % 2) * 2, (n % 2) * 2 + 2)
        kv_out[i, chunk] = sums_kv[i, chunk, 1 - core].astype(BF16)
        shared.append(net.copy(kv_out.at[i, chunk], kv_in.at[i, chunk], at.sibling))

    dq_copies = chips.swap_even(
        net, lambda to_low, to_pair: dq_send.at[to_low, to_pair], dq_all.at[low, pair]
    )
    dq_all[low, pair] = dq_send[low, pair]
    for copy in shared:
        copy.wait()
    kv_back[...] = (sums_kv[:, :, core] + kv_in[...].astype(F32)).astype(BF16)
    kv_copies = chips.swap(
        net, lambda to_low, to_y: kv_back.at[to_low, to_y], kv_own.at[low, y]
    )
    kv_own[low, y] = kv_back[low, y]
    next(early)
    next(dwu_steps)
    run(dwd_steps)
    outs = []
    for h in range(2):
        front[h].finish()
        bo_ref[z, half(h), :] = (x1[h] + owned(1, h) + db_ref[...]).astype(BF16)
        outs.append(gather(bo_ref, h))
    h1 = h1_ref[...]

    def left(i):
        return h1[:, i * 256 : i * 256 + 256]

    for copy in dq_copies:
        copy.wait()
    dq = tile_rows(dq_all)
    put_grad(dwq, 0, 256, left, dq)

    def put_q(rows, value):
        dqkv_ref[rows, 0:256] = value[:, 0:256]
        dwo_ref[rows, :] = value[:, 256:512]

    dwq_steps = scatter_plane(net, at, dwq, other_q, total_q, wide_q, thin_q, put_q)
    next(dwq_steps)
    direct = dot(dq, w1[:, :, :, :, 0:256].reshape(1024, 256), 1, 1)
    for copy, _ in kv_copies:
        copy.wait()
    whole = []
    for i in range(2):
        tiles = [
            (kv_own[i, j * 2].astype(F32) + kv_own[i, j * 2 + 1].astype(F32)).astype(BF16)
            for j in range(2)
        ]
        whole.append(
            jnp.concatenate(
                [tiles[0][:, 0:128], tiles[1][:, 0:128], tiles[0][:, 128:256], tiles[1][:, 128:256]],
                axis=1,
            )
        )
    dkv = jnp.concatenate(whole, axis=0)
    direct = direct + dot(dkv, w1[:, :, :, :, 256:768].reshape(1024, 512), 1, 1)
    steps = scatter(3, direct)
    gain_sum, shift_sum = column_sum(direct * unit1[...]), column_sum(direct)
    query_sum, value_sum = column_sum(dq.astype(F32)), column_sum(dkv[:, 256:512].astype(F32))
    bias_sum = jnp.concatenate([query_sum, value_sum, jnp.zeros((1, 512), F32)], axis=1)
    for i in range(8):
        lanes = slice(i * 128, i * 128 + 128)
        hx[x, i : i + 1, 0:128] = gain_sum[:, lanes]
        hx[x, i : i + 1, 128:256] = shift_sum[:, lanes]
        hx[x, i : i + 1, 256:384] = bias_sum[:, lanes]
    late = sum_small(net, at, hx, hy, hz)
    next(late)
    next(dwq_steps)
    put_grad(dw1, 0, 512, left, dkv)

    def put1(rows, value):
        dqkv_ref[rows, 256:768] = value

    dw1_steps = scatter_plane(net, at, dw1, other1, total1, wide1, thin1, put1)
    next(dw1_steps)
    next(late)
    next(dw1_steps)
    gathers = []
    for h in range(2):
        steps[h].finish()
        unit, rate = norm_parts(x_ref[z, half(h), :].astype(F32))
        grad = dx1[h] + norm_back(owned(3, h), unit, rate, gain1_ref[...])
        dxin_ref[z, half(h), :] = grad.astype(BF16)
        gathers.append(gather(dxin_ref, h))
    next(late)
    next(dwq_steps)
    next(dw1_steps)
    run(dwu_steps)
    run(dwq_steps)
    run(dw1_steps)
    run(early)
    run(late)
    sums_ref[2:6, :] = gz[0, 2:6, :] + gz[1, 2:6, :] + gz[2, 2:6, :] + gz[3, 2:6, :]
    sums_ref[6:7, :] = gz[z, 6:7, :]
    over = hz[0, :, 0:256] + hz[1, :, 0:256] + hz[2, :, 0:256] + hz[3, :, 0:256]
    for i in range(8):
        lanes = slice(i * 128, i * 128 + 128)
        sums_ref[0:1, lanes] = over[i : i + 1, 0:128]
        sums_ref[1:2, lanes] = over[i : i + 1, 128:256]
        sums_ref[7:8, lanes] = hz[z, i : i + 1, 256:384]
    for steps in outs + gathers:
        steps.finish()


def write_kernel(
    bo_ref, dxin_ref, dqkv_ref, dwo_ref, dud_ref, sums_ref,
    block_ref, input_ref, g1_ref, s1_ref, dwq_ref, qb_ref, dwk_ref, dwv_ref, vb_ref, out_ref,
    ob_ref, g2_ref, s2_ref, dwu_ref, ub_ref, dwd_ref, db_ref,
):
    block_ref[...] = bo_ref[...].astype(F32)
    input_ref[...] = dxin_ref[...].astype(F32)
    dwq_ref[...] = dqkv_ref[:, 0:256]
    dwk_ref[...] = dqkv_ref[:, 256:512]
    dwv_ref[...] = dqkv_ref[:, 512:768]
    out_ref[...] = dwo_ref[...]
    dwu_ref[...] = dud_ref[:, 0:1024]
    dwd_ref[...] = dud_ref[:, 1024:2048]
    for index, ref in enumerate((g1_ref, s1_ref, ob_ref, g2_ref, s2_ref, db_ref, ub_ref)):
        ref[...] = sums_ref[index : index + 1, :]
    qb_ref[...] = sums_ref[7:8, 0:256]
    vb_ref[...] = sums_ref[7:8, 256:512]


def on_device(
    block_input, first_gain, first_shift, query_weight, query_bias, key_weight, value_weight, value_bias,
    output_weight, output_bias, second_gain, second_shift, up_weight, up_bias, down_weight, down_bias,
    segments, out_cotangent,
):
    vmem = pl.BlockSpec(memory_space=pltpu.VMEM)

    def row(value):
        return value.reshape(1, -1)

    def shapes(*pairs):
        return [jax.ShapeDtypeStruct(shape, kind) for shape, kind in pairs]

    results = pl.pallas_call(
        layer_kernel,
        out_shape=shapes(
            ((4, 64, 1024), BF16),
            ((4, 64, 1024), BF16),
            ((32, 768), F32),
            ((32, 256), F32),
            ((32, 2048), F32),
            ((8, 1024), F32),
        ),
        in_specs=[vmem] * 18,
        out_specs=[vmem] * 6,
        scratch_shapes=[
            pltpu.VMEM((4, 4, 2, 32, 768), BF16),
            pltpu.VMEM((4, 4, 2, 32, 256), BF16),
            pltpu.VMEM((4, 4, 2, 32, 1024), BF16),
            pltpu.VMEM((4, 4, 2, 32, 1024), BF16),
            pltpu.VMEM((2, 4, 2, 8, 128), jnp.int32),
            pltpu.VMEM((256, 1024), BF16),
            pltpu.VMEM((256, 1024), F32),
            pltpu.VMEM((2, 2, 128, 256), BF16),
            pltpu.VMEM((2, 2, 128, 128), BF16),
            pltpu.VMEM((2, 4, 2, 128, 256), BF16),
            *[pltpu.VMEM((2, 2, 128, 128), BF16)] * 7,
            pltpu.VMEM((2, 4, 2, 128, 256), F32),
            *[pltpu.VMEM((2, 4, 128, 256), BF16)] * 4,
            pltpu.VMEM((5120, 256), F32),
            pltpu.VMEM((2048, 256), F32),
            pltpu.VMEM((2048, 256), F32),
            pltpu.VMEM((4, 4, 64, 1024), BF16),
            pltpu.VMEM((4, 2, 3, 32, 1024), BF16),
            pltpu.VMEM((2, 4, 64, 1024), BF16),
            pltpu.VMEM((4, 64, 1024), F32),
            pltpu.VMEM((4, 64, 1024), BF16),
            pltpu.VMEM((4, 64, 1024), BF16),
            pltpu.VMEM((4, 8, 1024), F32),
            pltpu.VMEM((4, 2, 8, 1024), F32),
            pltpu.VMEM((4, 8, 1024), F32),
            pltpu.VMEM((4, 8, 384), F32),
            pltpu.VMEM((4, 2, 8, 384), F32),
            pltpu.VMEM((4, 8, 384), F32),
            *plane_scratch(512),
            *plane_scratch(512),
            *plane_scratch(1024),
            *plane_scratch(1024),
            pltpu.SemaphoreType.DMA((SENDS,)),
            pltpu.SemaphoreType.DMA((COPIES,)),
        ],
        compiler_params=pltpu.CompilerParams(
            collective_id=1, has_side_effects=True, vmem_limit_bytes=VMEM_BYTES
        ),
        cost_estimate=pl.CostEstimate(
            flops=10_000_000_000, bytes_accessed=16_000_000, transcendentals=0
        ),
        name="layer",
    )(
        block_input.reshape(4, 64, 1024), out_cotangent.reshape(4, 64, 1024), segments.reshape(2, 128),
        row(first_gain), row(first_shift), query_weight, row(query_bias), key_weight, value_weight,
        row(value_bias), output_weight, row(output_bias), row(second_gain), row(second_shift), up_weight,
        row(up_bias), down_weight, row(down_bias),
    )
    wide, narrow = ((1, 1024), F32), ((1, 256), F32)
    square, tall, tokens = ((32, 256), F32), ((32, 1024), F32), ((4, 64, 1024), F32)
    outs = pl.pallas_call(
        write_kernel,
        out_shape=shapes(
            tokens, tokens, wide, wide, square, narrow, square, square, narrow, square, wide, wide, wide,
            tall, wide, tall, wide,
        ),
        in_specs=[vmem] * 6,
        out_specs=[vmem] * 17,
        name="write",
    )(*results)
    ends = {0: (2, 1, 128, 1024), 1: (2, 1, 128, 1024)}
    flat = (2, 3, 5, 8, 10, 11, 12, 14, 16)
    return tuple(
        out.reshape(ends[i]) if i in ends else (out.reshape(-1) if i in flat else out)
        for i, out in enumerate(outs)
    )


def solution(mesh):
    tokens = P(None, "seq", "ctx", None)
    matrix = P(("seq", "ctx"), "head")
    return jax.shard_map(
        on_device,
        mesh=mesh,
        in_specs=(
            tokens, P(), P(), matrix, P("head"), matrix, matrix, P("head"), matrix, P(), P(), P(),
            matrix, P("head"), matrix, P(), P(None, "seq", "ctx"), tokens,
        ),
        out_specs=(
            tokens, tokens, P(), P(), matrix, P("head"), matrix, matrix, P("head"), matrix, P(), P(),
            P(), matrix, P("head"), matrix, P(),
        ),
        check_vma=False,
    )
```

```python
import jax
import jax.numpy as jnp
from jax import lax
from jax.experimental import pallas as pl
from jax.experimental.pallas import tpu as pltpu
from jax.sharding import PartitionSpec as P

F32 = jnp.float32
BF16 = jnp.bfloat16
MESH = pl.DeviceIdType.MESH
VMEM_BYTES = 56 * 1024 * 1024
KEYS = 512
COPIES = 120
SENDS = 18


def dot(left, right, dim_left, dim_right):
    return lax.dot_general(
        left, right, (((dim_left,), (dim_right,)), ((), ())), preferred_element_type=F32
    )


def turn(index, by):
    return lax.rem(index + by, 4)


class Place:
    def __init__(self):
        self.seq = lax.axis_index("seq")
        self.ctx = lax.axis_index("ctx")
        self.z = lax.axis_index("head")
        self.core = lax.rem(self.ctx, 2)
        self.y = lax.rem(lax.div(self.ctx, 2), 4)
        self.low = lax.div(self.ctx, 8)
        self.x = self.seq * 2 + self.low
        self.x_plus = self.at(turn(self.x, 1), self.y, self.core, self.z)
        self.x_minus = self.at(turn(self.x, 3), self.y, self.core, self.z)
        self.y_plus = self.at(self.x, turn(self.y, 1), self.core, self.z)
        self.y_minus = self.at(self.x, turn(self.y, 3), self.core, self.z)
        self.z_plus = self.at(self.x, self.y, self.core, turn(self.z, 1))
        self.z_minus = self.at(self.x, self.y, self.core, turn(self.z, 3))
        self.x_across = self.at(turn(self.x, 2), self.y, self.core, self.z)
        self.y_across = self.at(self.x, turn(self.y, 2), self.core, self.z)
        self.z_across = self.at(self.x, self.y, self.core, turn(self.z, 2))
        self.x_ring = (self.x, (self.x_plus, self.x_minus, self.x_across))
        self.y_ring = (self.y, (self.y_plus, self.y_minus, self.y_across))
        self.z_ring = (self.z, (self.z_plus, self.z_minus, self.z_across))
        self.sibling = self.at(self.x, self.y, 1 - self.core, self.z)
        self.pair = self.at(self.seq * 2 + 1 - self.low, self.y, self.core, self.z)

    def at(self, x, y, core, z):
        return (lax.div(x, 2), (lax.rem(x, 2) * 4 + y) * 2 + core, z)

    def greet(self, partners):
        barrier = pltpu.get_barrier_semaphore()
        for partner in partners:
            pl.semaphore_signal(barrier, inc=1, device_id=partner, device_id_type=MESH)
        pl.semaphore_wait(barrier, len(partners))


class Copy:
    def __init__(self, net, made, index):
        self.net, self.made, self.index = net, made, index

    def wait_recv(self):
        self.made.wait_recv()

    def wait_send(self):
        self.made.wait_send()
        self.net.free.append(self.index)

    def wait(self):
        self.wait_send()
        self.wait_recv()


class Net:
    def __init__(self, send, recv):
        self.send, self.recv, self.used, self.free, self.most = send, recv, 0, [], 0

    def copy(self, src, dst, device):
        index = self.free.pop() if self.free else self.most
        self.most = max(self.most, index + 1)
        made = pltpu.make_async_remote_copy(
            src_ref=src,
            dst_ref=dst,
            send_sem=self.send.at[index],
            recv_sem=self.recv.at[self.used],
            device_id=device,
            device_id_type=MESH,
        )
        self.used += 1
        made.start()
        return Copy(self, made, index)

    def copies(self, each, whole):
        index = self.free.pop() if self.free else self.most
        self.most = max(self.most, index + 1)
        sems = {"send_sem": self.send.at[index], "recv_sem": self.recv.at[self.used]}
        self.used += 1
        for src, dst, device in each:
            pltpu.make_async_remote_copy(
                src_ref=src, dst_ref=dst, device_id=device, device_id_type=MESH, **sems
            ).start()
        made = pltpu.make_async_remote_copy(
            src_ref=whole, dst_ref=whole, device_id=each[0][2], device_id_type=MESH, **sems
        )
        return [Copy(self, made, index)]


def run(steps):
    for _ in steps:
        pass


FROM = (3, 1, 2)
TO = (1, 3, 2)


def add_into(view, *others):
    value = view[...].astype(F32)
    for other in others:
        value = value + other[...].astype(F32)
    view[...] = value.astype(BF16)


class Gather:
    def __init__(self, net, region, ring, apart=False):
        self.here, others = ring
        own = region(self.here)
        self.region, self.apart = region, apart
        if apart:
            self.copies = [net.copy(own, own, device) for device in others]
        else:
            self.copies = net.copies([(own, own, device) for device in others], region(slice(0, 3)))

    def arrivals(self):
        for copy, step in zip(self.copies, FROM):
            copy.wait_recv()
            yield self.region(turn(self.here, step))

    def sent(self):
        for copy in self.copies:
            copy.wait_send()

    def finish(self):
        for copy in self.copies:
            copy.wait()


class Scatter:
    def __init__(self, net, part, slots, ring):
        here, others = ring
        self.copies = net.copies(
            [
                (part(turn(here, step)), slots.at[index], device)
                for index, (step, device) in enumerate(zip(TO, others))
            ],
            slots,
        )

    def finish(self):
        for copy in self.copies:
            copy.wait()


TOP, LOW = slice(0, 16), slice(16, 32)


def gather_plane(net, at, full, urgent=False):
    x, y, core = at.x, at.y, at.core
    done = []

    def share(view):
        done.append(net.copy(view, view, at.sibling))

    a = Gather(net, lambda j: full.at[j, y, core, TOP, :], at.x_ring)
    b = Gather(net, lambda j: full.at[x, j, core, LOW, :], at.y_ring)
    yield
    a.finish()
    a = Gather(net, lambda j: full.at[:, j, core, TOP, :], at.y_ring, urgent)
    b.finish()
    b = Gather(net, lambda j: full.at[j, :, core, LOW, :], at.x_ring, urgent)
    if urgent:
        share(full.at[:, y, core, TOP, :])
        share(full.at[x, :, core, LOW, :])
    yield
    if urgent:
        for one, two in zip(a.arrivals(), b.arrivals()):
            share(one)
            share(two)
        a.sent()
        b.sent()
    else:
        a.finish()
        b.finish()
        share(full.at[:, :, core])
    yield
    for copy in done:
        copy.wait()


def scatter_plane(net, at, partial, other, total, wide, thin, result):
    x, y, core = at.x, at.y, at.core
    shared = net.copy(partial.at[:, :, 1 - core], other, at.sibling)
    yield
    shared.wait()

    def add(index, carry):
        i, j = lax.div(index, 4), lax.rem(index, 4)
        total[i, j] = (partial[i, j, core].astype(F32) + other[i, j].astype(F32)).astype(BF16)
        return carry

    lax.fori_loop(0, 16, add, 0)
    a = Scatter(net, lambda j: total.at[:, j, TOP, :], wide.at[0], at.y_ring)
    b = Scatter(net, lambda j: total.at[j, :, LOW, :], wide.at[1], at.x_ring)
    yield
    a.finish()
    add_into(total.at[:, y, TOP, :], wide.at[0, 0], wide.at[0, 1], wide.at[0, 2])
    a = Scatter(net, lambda j: total.at[j, y, TOP, :], thin.at[0], at.x_ring)
    b.finish()
    add_into(total.at[x, :, LOW, :], wide.at[1, 0], wide.at[1, 1], wide.at[1, 2])
    b = Scatter(net, lambda j: total.at[x, j, LOW, :], thin.at[1], at.y_ring)
    yield
    for index, steps, rows in ((0, a, TOP), (1, b, LOW)):
        steps.finish()
        extra = thin[index, 0].astype(F32) + thin[index, 1].astype(F32) + thin[index, 2].astype(F32)
        result(rows, total[x, y, rows, :].astype(F32) + extra)


def sum_small(net, at, by_x, by_y, by_z, urgent):
    x, y, z, core = at.x, at.y, at.z, at.core
    steps = Gather(net, lambda j: by_x.at[j], at.x_ring)
    yield
    steps.finish()
    by_y[y, core] = by_x[0] + by_x[1] + by_x[2] + by_x[3]
    own = by_y.at[y, core]
    if urgent:
        copies = [net.copy(own, own, device) for device in at.y_ring[1] + (at.sibling,)]
        copies = copies + [net.copy(own, own, at.at(x, turn(y, step), 1 - core, z)) for step in TO]
        yield
        for copy in copies:
            copy.wait()
    else:
        steps = Gather(net, lambda j: by_y.at[j, core], at.y_ring)
        yield
        steps.finish()
        view = by_y.at[:, core]
        copy = net.copy(view, view, at.sibling)
        yield
        copy.wait()
    total = by_y[0, 0] + by_y[0, 1]
    for i in range(1, 4):
        total = total + by_y[i, 0] + by_y[i, 1]
    by_z[z] = total
    steps = Gather(net, lambda j: by_z.at[j], at.z_ring)
    yield
    steps.finish()


def plane_scratch(width):
    return [
        pltpu.VMEM((4, 4, 2, 32, width), BF16),
        pltpu.VMEM((4, 4, 32, width), BF16),
        pltpu.VMEM((4, 4, 32, width), BF16),
        pltpu.VMEM((2, 3, 4, 16, width), BF16),
        pltpu.VMEM((2, 3, 16, width), BF16),
    ]


def norm_parts(value):
    center = value - jnp.mean(value, axis=-1, keepdims=True)
    rate = lax.rsqrt(jnp.mean(center * center, axis=-1, keepdims=True) + 1e-05)
    return center * rate, rate


def norm_back(grad, unit, rate, gain):
    inner = grad * gain
    even = jnp.mean(inner, axis=-1, keepdims=True)
    along = jnp.mean(inner * unit, axis=-1, keepdims=True)
    return rate * (inner - even - unit * along)


def column_sum(value):
    return jnp.sum(value, axis=0, keepdims=True)


def slope_of(at):
    by_z = jnp.where(at.z == 0, 1.0, jnp.where(at.z == 1, 0.25, jnp.where(at.z == 2, 0.0625, 0.015625)))
    by_y = jnp.where(at.y == 0, 2.0**-0.5, jnp.where(at.y == 1, 0.5, jnp.where(at.y == 2, 2.0**-1.5, 0.25)))
    return by_z.astype(F32) * by_y.astype(F32)


def fill_distance(first_query, dist, base, chunks, lanes, start):
    def fill(block, carry):
        lane = lax.broadcasted_iota(jnp.int32, (256, 128), 1)
        query = (lane + first_query).astype(F32)
        key = (lax.broadcasted_iota(jnp.int32, (256, 128), 0) + block * 256).astype(F32)
        apart = query - key
        value = jnp.where((key >= start) & (apart >= 0.0), apart, -1.0)
        rows = pl.ds(pl.multiple_of(base + block * 256, 256), 256)
        dist[rows, lanes] = value
        return carry

    lax.fori_loop(0, chunks * 2, fill, 0)


def masked_scores(keys, queries, dist, slope):
    raw = dot(keys, queries, 1, 0) * 0.125
    return jnp.where(dist >= 0.0, raw - slope * dist, -1000000000.0)


def key_block(kvq, block):
    low, y = block // 2, (block % 2) * 2
    return kvq[low, y : y + 2, :, 0:128, :].reshape(KEYS, 128)


class Chips:
    def __init__(self, at):
        self.steps = []
        for dx in range(2):
            for dy in range(4):
                if dx or dy:
                    low = 1 - at.low if dx else at.low
                    y = turn(at.y, dy)
                    device = at.at(at.seq * 2 + low, y, at.core, at.z)
                    source = (low, turn(at.y, 4 - dy))
                    self.steps.append((low, y, device, source))

    def swap(self, net, src, dst):
        return [(net.copy(src.at[low, y], dst, device), source) for low, y, device, source in self.steps]


def join_tiles(tiles, first):
    rows = [
        jnp.concatenate([tiles[i, j, first : first + 64, :].astype(F32) for j in range(4)], axis=0).T
        for i in range(2)
    ]
    return jnp.concatenate(rows, axis=0).astype(BF16)


def pad_heads(tiles, n, first, above):
    i, j = n // 2, (n % 2) * 2
    wide = [tiles[i, j + k, first : first + 64, :].astype(F32) for k in range(2)]
    wide = jnp.concatenate(wide, axis=1)
    both = [wide, jnp.zeros((64, 256), F32)]
    return jnp.concatenate(both if above else both[::-1], axis=0).astype(BF16)


def layer_kernel(
    x_ref, dy_ref, seg_ref, gain1_ref, shift1_ref, wq_ref, qb_ref, wk_ref, wv_ref, vb_ref, wo_ref, ob_ref,
    gain2_ref, shift2_ref, wu_ref, ub_ref, wd_ref, db_ref,
    bo_ref, dxin_ref, dqkv_ref, dwo_ref, dud_ref, sums_ref,
    w1, wo, wu, wd, seg_all, h1_ref, unit1,
    kvq_send, kvq, o_send, o_all, do_send, do_all, sums_kv, kv_out, kv_in, back_send, own_all, dist, score, dp_ref,
    part, slots, gathered, dg, g_ref, du_ref, gx, gy, gz, hx, hy, hz,
    dw1, other1, total1, wide1, thin1,
    dwo_part, other_o, total_o, wide_o, thin_o,
    dwu_part, other_u, total_u, wide_u, thin_u,
    dwd_part, other_d, total_d, wide_d, thin_d,
    send, recv,
):
    at = Place()
    net = Net(send, recv)
    chips = Chips(at)
    x, y, z, core, low = at.x, at.y, at.z, at.core, at.low
    partners = at.x_ring[1] + at.y_ring[1] + at.z_ring[1] + (at.sibling,)
    partners = partners + tuple(at.at(x, turn(y, step), 1 - core, z) for step in TO)
    partners = partners + tuple(
        at.at(at.seq * 2 + 1 - low, turn(y, step), core, z) for step in TO
    )
    at.greet(partners)

    mine = w1.at[x, y, core]
    mine[:, 0:256] = wq_ref[...]
    mine[:, 256:512] = wk_ref[...]
    mine[:, 512:768] = wv_ref[...]
    w1_steps = gather_plane(net, at, w1, urgent=True)
    next(w1_steps)
    seg_all[low, y, core] = jnp.concatenate([seg_ref[...]] * 4, axis=0)
    seg = Gather(net, lambda j: seg_all.at[low, j, core], at.y_ring)
    wo[x, y, core] = wo_ref[...]
    wu[x, y, core] = wu_ref[...]
    wd[x, y, core] = wd_ref[...]
    unit, _ = norm_parts(x_ref[...].reshape(256, 1024).astype(F32))
    unit1[...] = unit
    h1_ref[...] = (unit * gain1_ref[...] + shift1_ref[...]).astype(BF16)
    next(w1_steps)
    seg.finish()
    view = seg_all.at[low, :, core]
    seg_pair = net.copy(view, view, at.pair)
    next(w1_steps)
    wo_steps = gather_plane(net, at, wo)
    next(wo_steps)
    wd_steps = gather_plane(net, at, wd)
    next(wd_steps)
    wu_steps = gather_plane(net, at, wu)
    next(wu_steps)
    seg_pair.wait()
    view = seg_all.at[:, :, core]
    seg_share = net.copy(view, view, at.sibling)
    run(w1_steps)

    h1 = h1_ref[...]
    wide = dot(h1, w1[...].reshape(1024, 768), 1, 0)
    turned = (wide[:, 0:256] + qb_ref[...]).T.astype(BF16)
    keys, values = wide[:, 256:512], wide[:, 512:768] + vb_ref[...]
    for i in range(2):
        for j in range(4):
            rows, lanes = slice(i * 128, i * 128 + 128), slice(j * 64, j * 64 + 64)
            tile = jnp.concatenate([keys[rows, lanes], values[rows, lanes]], axis=1)
            kvq_send[i, j, 0:128, :] = tile.astype(BF16)
            kvq_send[i, j, 128:192, :] = turned[lanes, rows]
    kv_copies = chips.swap(net, kvq_send, kvq.at[low, y, core])
    kvq[low, y, core] = kvq_send[low, y]
    shares = []
    next(wo_steps)
    seg_share.wait()
    counts = []
    for number in range(1, 4):
        below = (seg_all[:, :, :, 0:2, :] < number).astype(F32)
        below = jnp.sum(below.reshape(16, 2, 128), axis=0)
        below = jnp.sum(below, axis=-1, keepdims=True)
        counts.append(jnp.where(low == 0, below[0:1], below[1:2]))
    bases = [0, 512, 1536, 3072]
    for n in range(4):
        for k in range(2):
            there = seg_all[n // 2, (n % 2) * 2 + k, core]
            there = jnp.where(low == 0, there[0:1], there[1:2])
            found = jnp.zeros((1, 128), F32)
            for number in range(1, 4):
                found = jnp.where(there == number, counts[number - 1], found)
            first_query = (n * 4 + k * 2 + core) * 128
            fill_distance(
                first_query, dist, bases[n], n + 1, slice(k * 128, k * 128 + 128), found
            )
    for index, (copy, source) in enumerate(kv_copies):
        copy.wait_recv()
        if index == 2:
            view = kvq.at[low, :, core, 0:128, :]
            shares.append(net.copy(view, view, at.sibling))
        if index > 2:
            view = kvq.at[source[0], source[1], core, 0:128, :]
            shares.append(net.copy(view, view, at.sibling))
    for copy, _ in kv_copies:
        copy.wait_send()
    next(wd_steps)
    for copy in shares:
        copy.wait()

    slope = slope_of(at)
    for n in range(4):
        queries = pad_heads(kvq.at[:, :, core], n, 128, True)
        top = jnp.full((1, 256), -3.0e38, F32)
        for block in range(n + 1):
            rows = slice(block * KEYS, block * KEYS + KEYS)
            value = masked_scores(
                key_block(kvq, block), queries,
                dist[bases[n] + block * KEYS : bases[n] + block * KEYS + KEYS, :], slope,
            )
            score[rows, :] = value
            top = jnp.maximum(top, jnp.max(value, axis=0, keepdims=True))
        summed = jnp.zeros((1, 256), F32)
        for block in range(n + 1):
            rows = slice(block * KEYS, block * KEYS + KEYS)
            value = jnp.exp(score[rows, :] - top)
            score[rows, :] = value
            summed = summed + column_sum(value)
        scale = 1.0 / summed
        mixed = jnp.zeros((128, 256), F32)
        for block in range(n + 1):
            rows = slice(block * KEYS, block * KEYS + KEYS)
            probs = score[rows, :] * scale
            dist[bases[n] + block * KEYS : bases[n] + block * KEYS + KEYS, :] = probs
            mixed = mixed + dot(key_block(kvq, block), probs.astype(BF16), 0, 0)
        for k in range(2):
            lanes = slice(k * 128, k * 128 + 128)
            o_send[n // 2, (n % 2) * 2 + k] = mixed[64:128, lanes].astype(BF16)
    copies = chips.swap(net, o_send, o_all.at[low, y])
    o_all[low, y] = o_send[low, y]
    next(wo_steps)

    def half(h):
        return slice(h * 32, h * 32 + 32)

    def scatter_half(index, h):
        return Scatter(net, lambda j: part.at[index, j, half(h), :], slots.at[index, h], at.z_ring)

    def scatter(index, value):
        part[index] = value.astype(BF16).reshape(4, 64, 1024)
        return [scatter_half(index, 0), scatter_half(index, 1)]

    def owned(index, h):
        extra = slots[index, h, 0].astype(F32) + slots[index, h, 1].astype(F32)
        return part[index, z, half(h), :].astype(F32) + (extra + slots[index, h, 2].astype(F32))

    def gather(buffer, h):
        return Gather(net, lambda j: buffer.at[j, half(h), :], at.z_ring)

    def put_sums(to, sums):
        for i in range(8):
            for j, value in enumerate(sums):
                to[x, i : i + 1, j * 128 : j * 128 + 128] = value[:, i * 128 : i * 128 + 128]

    def put_grad(to, first, width, left, right):
        for i in range(4):
            value = dot(left(i), right, 0, 0).astype(BF16)
            to[i, :, :, :, first : first + width] = value.reshape(4, 2, 32, width)

    run(wo_steps)
    next(wu_steps)
    for copy, _ in copies:
        copy.wait()
    mixed = join_tiles(o_all, 0)
    steps = scatter(0, dot(mixed, wo[...].reshape(1024, 256), 1, 1))
    next(wd_steps)
    x1, units, rates, gathers = [], [], [], []
    for h in range(2):
        steps[h].finish()
        x1.append(x_ref[z, half(h), :].astype(F32) + owned(0, h) + ob_ref[...])
        unit, rate = norm_parts(x1[h])
        gathered[0, z, half(h), :] = (unit * gain2_ref[...] + shift2_ref[...]).astype(BF16)
        gathers.append(gather(gathered.at[0], h))
        units.append(unit)
        rates.append(rate)
        if h == 0:
            next(wu_steps)
    upstream = [dy_ref[z, half(h), :].astype(F32) for h in range(2)]
    dy_sum = column_sum(upstream[0]) + column_sum(upstream[1])
    run(wd_steps)
    down = wd[...].reshape(1024, 1024)
    dg[...] = dot(dy_ref[...].reshape(256, 1024), down, 1, 0).reshape(4, 64, 1024)
    run(wu_steps)
    up = wu[...].reshape(1024, 1024)
    back = []
    for h in range(2):
        gathers[h].finish()
        h2 = gathered[0, :, half(h), :].reshape(128, 1024)
        for i in range(2):
            cols = slice(i * 512, i * 512 + 512)
            u = dot(h2, wu[:, :, :, :, cols].reshape(1024, 512), 1, 0) + ub_ref[:, cols]
            tanh = jnp.tanh(0.7978845608028654 * (u + 0.044715 * u * u * u))
            g_ref[:, half(h), cols] = (0.5 * u * (1.0 + tanh)).astype(BF16).reshape(4, 32, 512)
            turned = 0.5 * u * (1.0 - tanh * tanh) * 0.7978845608028654 * (1.0 + 3 * 0.044715 * u * u)
            turned = (0.5 * (1.0 + tanh) + turned).reshape(4, 32, 512)
            du_ref[:, half(h), cols] = (dg[:, half(h), cols] * turned).astype(BF16)
        value = dot(du_ref[:, half(h), :].reshape(128, 1024), up, 1, 1).astype(BF16)
        part[2, :, half(h), :] = value.reshape(4, 32, 1024)
        back.append(scatter_half(2, h))
    du = du_ref[...].reshape(256, 1024)
    g = g_ref[...].reshape(256, 1024)
    put_grad(
        dwd_part, 0, 1024, lambda i: dy_ref[:, :, i * 256 : i * 256 + 256].reshape(256, 256), g
    )

    def put_d(rows, value):
        dud_ref[rows, 1024:2048] = value

    def put_u(rows, value):
        dud_ref[rows, 0:512] = value

    dwd_steps = scatter_plane(net, at, dwd_part, other_d, total_d, wide_d, thin_d, put_d)
    next(dwd_steps)
    def h2_columns(i):
        return gathered[0, :, :, i * 256 : i * 256 + 256].reshape(256, 256)

    put_grad(dwu_part, 0, 512, h2_columns, du[:, 0:512])
    dwu_steps = scatter_plane(net, at, dwu_part, other_u, total_u, wide_u, thin_u, put_u)
    put_grad(dwo_part, 0, 512, h2_columns, du[:, 512:1024])
    dx1, dh2, gathers = [], [], []
    for h in range(2):
        back[h].finish()
        dh2.append(owned(2, h))
        dx1.append(upstream[h] + norm_back(dh2[h], units[h], rates[h], gain2_ref[...]))
        gathered[1, z, half(h), :] = dx1[h].astype(BF16)
        gathers.append(gather(gathered.at[1], h))
        if h == 0:
            next(dwd_steps)
            next(dwu_steps)
    early_sums = (
        column_sum(dx1[0]) + column_sum(dx1[1]),
        column_sum(dh2[0] * units[0]) + column_sum(dh2[1] * units[1]),
        column_sum(dh2[0]) + column_sum(dh2[1]),
        dy_sum,
        column_sum(du.astype(F32)),
    )
    put_sums(gx, early_sums)
    early = sum_small(net, at, gx, gy, gz, False)
    next(early)
    next(dwu_steps)
    ffn = dot(g, down, 1, 1)
    for steps in gathers:
        steps.finish()
    grads = dot(gathered[1].reshape(256, 1024), wo[...].reshape(1024, 256), 1, 0).T.astype(BF16)
    for i in range(2):
        for j in range(4):
            do_send[i, j] = grads[j * 64 : j * 64 + 64, i * 128 : i * 128 + 128]
    copies = chips.swap(net, do_send, do_all.at[low, y])
    do_all[low, y] = do_send[low, y]
    front = scatter(1, ffn)
    put_grad(
        dwo_part, 512, 256, lambda i: gathered[1, :, :, i * 256 : i * 256 + 256].reshape(256, 256), mixed
    )

    def put_o(rows, value):
        dud_ref[rows, 512:1024] = value[:, 0:512]
        dwo_ref[rows, :] = value[:, 512:768]

    dwo_steps = scatter_plane(net, at, dwo_part, other_o, total_o, wide_o, thin_o, put_o)
    next(dwo_steps)
    for copy, _ in copies:
        copy.wait()
    next(dwd_steps)
    next(dwu_steps)
    next(dwo_steps)
    next(early)

    shared = []
    lane = lax.broadcasted_iota(jnp.int32, (1, 1, 1, 128), 3)
    scale = jnp.where(lane < 64, 0.125, 1.0).astype(F32)
    scale = scale.reshape(1, 1, 128)
    for n in (3, 2, 1, 0):
        queries = pad_heads(kvq.at[:, :, core], n, 128, True)
        grads = pad_heads(do_all, n, 0, False)
        right = jnp.concatenate([queries, grads], axis=1)
        inner = jnp.zeros((1, 256), F32)
        for block in range(n + 1):
            rows = slice(block * KEYS, block * KEYS + KEYS)
            probs = dist[bases[n] + block * KEYS : bases[n] + block * KEYS + KEYS, :]
            prob_grad = dot(key_block(kvq, block), grads, 1, 0)
            dp_ref[rows, :] = prob_grad
            inner = inner + column_sum(probs * prob_grad)
        query_grad = jnp.zeros((128, 256), F32)
        for block in range(n + 1):
            rows = slice(block * KEYS, block * KEYS + KEYS)
            probs = dist[bases[n] + block * KEYS : bases[n] + block * KEYS + KEYS, :]
            score_grad = (probs * (dp_ref[rows, :] - inner)).astype(BF16)
            both = jnp.concatenate([score_grad, probs.astype(BF16)], axis=1)
            i, j = block // 2, (block % 2) * 2
            value = dot(both, right, 1, 1).reshape(2, 2, 128, 128)
            if n < 3:
                value = value + sums_kv[i, j : j + 2]
            sums_kv[i, j : j + 2] = value
            query_grad = query_grad + dot(key_block(kvq, block), score_grad, 0, 0)
        query_grad = (query_grad * 0.125).astype(BF16)
        for k in range(2):
            lanes = slice(k * 128, k * 128 + 128)
            back_send[n // 2, (n % 2) * 2 + k, 128:192, :] = query_grad[0:64, lanes]
        i, chunk = n // 2, slice((n % 2) * 2, (n % 2) * 2 + 2)
        kv_out[i, chunk] = (sums_kv[i, chunk, 1 - core] * scale).astype(BF16)
        shared.append(net.copy(kv_out.at[i, chunk], kv_in.at[i, chunk], at.sibling))

    for copy in shared:
        copy.wait()
    back_send[:, :, 0:128, :] = (sums_kv[:, :, core] * scale + kv_in[...].astype(F32)).astype(BF16)
    kv_copies = chips.swap(net, back_send, own_all.at[low, y])
    own_all[low, y] = back_send[low, y]
    run(dwd_steps)
    outs = []
    for h in range(2):
        front[h].finish()
        bo_ref[z, half(h), :] = (x1[h] + owned(1, h) + db_ref[...]).astype(BF16)
        outs.append(gather(bo_ref, h))
    h1 = h1_ref[...]

    def left(i):
        return h1[:, i * 256 : i * 256 + 256]

    for copy, _ in kv_copies:
        copy.wait()
    dq = join_tiles(own_all, 128)
    whole = []
    for i in range(2):
        tiles = [own_all[i, j, 0:128, :].astype(F32) for j in range(4)]
        keys = [tile[:, 0:64] for tile in tiles]
        values = [tile[:, 64:128] for tile in tiles]
        whole.append(jnp.concatenate(keys + values, axis=1))
    dkv = jnp.concatenate(whole, axis=0).astype(BF16)
    dqkv = jnp.concatenate([dq, dkv], axis=1)
    put_grad(dw1, 0, 768, left, dqkv)

    def put1(rows, value):
        dqkv_ref[rows, :] = value

    dw1_steps = scatter_plane(net, at, dw1, other1, total1, wide1, thin1, put1)
    next(dw1_steps)
    direct = dot(dqkv, w1[...].reshape(1024, 768), 1, 1)
    steps = scatter(3, direct)
    gain_sum, shift_sum = column_sum(direct * unit1[...]), column_sum(direct)
    query_sum, value_sum = column_sum(dq.astype(F32)), column_sum(dkv[:, 256:512].astype(F32))
    bias_sum = jnp.concatenate([query_sum, value_sum, jnp.zeros((1, 512), F32)], axis=1)
    put_sums(hx, (gain_sum, shift_sum, bias_sum))
    late = sum_small(net, at, hx, hy, hz, True)
    next(late)
    next(early)
    next(dwo_steps)
    next(late)
    next(dw1_steps)
    run(dwu_steps)
    next(early)
    gathers = []
    for h in range(2):
        steps[h].finish()
        unit, rate = norm_parts(x_ref[z, half(h), :].astype(F32))
        grad = dx1[h] + norm_back(owned(3, h), unit, rate, gain1_ref[...])
        dxin_ref[z, half(h), :] = grad.astype(BF16)
        gathers.append(gather(dxin_ref, h))
    next(late)
    next(dw1_steps)
    run(dwo_steps)
    run(dw1_steps)
    run(early)
    run(late)
    early_over = gz[0, :, 0:512] + gz[1, :, 0:512] + gz[2, :, 0:512] + gz[3, :, 0:512]
    late_over = hz[0, :, 0:256] + hz[1, :, 0:256] + hz[2, :, 0:256] + hz[3, :, 0:256]
    for i in range(8):
        lanes = slice(i * 128, i * 128 + 128)
        for j in range(2):
            sums_ref[j : j + 1, lanes] = late_over[i : i + 1, j * 128 : j * 128 + 128]
        for j in range(4):
            sums_ref[j + 2 : j + 3, lanes] = early_over[i : i + 1, j * 128 : j * 128 + 128]
        sums_ref[6:7, lanes] = gz[z, i : i + 1, 512:640]
        sums_ref[7:8, lanes] = hz[z, i : i + 1, 256:384]
    for steps in outs + gathers:
        steps.finish()


def write_kernel(
    bo_ref, dxin_ref, dqkv_ref, dwo_ref, dud_ref, sums_ref,
    block_ref, input_ref, g1_ref, s1_ref, dwq_ref, qb_ref, dwk_ref, dwv_ref, vb_ref, out_ref,
    ob_ref, g2_ref, s2_ref, dwu_ref, ub_ref, dwd_ref, db_ref,
):
    block_ref[...] = bo_ref[...].astype(F32)
    input_ref[...] = dxin_ref[...].astype(F32)
    dwq_ref[...] = dqkv_ref[:, 0:256]
    dwk_ref[...] = dqkv_ref[:, 256:512]
    dwv_ref[...] = dqkv_ref[:, 512:768]
    out_ref[...] = dwo_ref[...]
    dwu_ref[...] = dud_ref[:, 0:1024]
    dwd_ref[...] = dud_ref[:, 1024:2048]
    for index, ref in enumerate((g1_ref, s1_ref, ob_ref, g2_ref, s2_ref, db_ref, ub_ref)):
        ref[...] = sums_ref[index : index + 1, :]
    qb_ref[...] = sums_ref[7:8, 0:256]
    vb_ref[...] = sums_ref[7:8, 256:512]


def on_device(
    block_input, first_gain, first_shift, query_weight, query_bias, key_weight, value_weight, value_bias,
    output_weight, output_bias, second_gain, second_shift, up_weight, up_bias, down_weight, down_bias,
    segments, out_cotangent,
):
    vmem = pl.BlockSpec(memory_space=pltpu.VMEM)

    def row(value):
        return value.reshape(1, -1)

    def shapes(*pairs):
        return [jax.ShapeDtypeStruct(shape, kind) for shape, kind in pairs]

    results = pl.pallas_call(
        layer_kernel,
        out_shape=shapes(
            ((4, 64, 1024), BF16),
            ((4, 64, 1024), BF16),
            ((32, 768), F32),
            ((32, 256), F32),
            ((32, 2048), F32),
            ((8, 1024), F32),
        ),
        in_specs=[vmem] * 18,
        out_specs=[vmem] * 6,
        scratch_shapes=[
            pltpu.VMEM((4, 4, 2, 32, 768), BF16),
            pltpu.VMEM((4, 4, 2, 32, 256), BF16),
            pltpu.VMEM((4, 4, 2, 32, 1024), BF16),
            pltpu.VMEM((4, 4, 2, 32, 1024), BF16),
            pltpu.VMEM((2, 4, 2, 8, 128), jnp.int32),
            pltpu.VMEM((256, 1024), BF16),
            pltpu.VMEM((256, 1024), F32),
            pltpu.VMEM((2, 4, 192, 128), BF16),
            pltpu.VMEM((2, 4, 2, 192, 128), BF16),
            *[pltpu.VMEM((2, 4, 64, 128), BF16)] * 4,
            pltpu.VMEM((2, 4, 2, 128, 128), F32),
            *[pltpu.VMEM((2, 4, 128, 128), BF16)] * 2,
            *[pltpu.VMEM((2, 4, 192, 128), BF16)] * 2,
            pltpu.VMEM((5120, 256), F32),
            pltpu.VMEM((2048, 256), F32),
            pltpu.VMEM((2048, 256), F32),
            pltpu.VMEM((4, 4, 64, 1024), BF16),
            pltpu.VMEM((4, 2, 3, 32, 1024), BF16),
            pltpu.VMEM((2, 4, 64, 1024), BF16),
            pltpu.VMEM((4, 64, 1024), F32),
            pltpu.VMEM((4, 64, 1024), BF16),
            pltpu.VMEM((4, 64, 1024), BF16),
            pltpu.VMEM((4, 8, 640), F32),
            pltpu.VMEM((4, 2, 8, 640), F32),
            pltpu.VMEM((4, 8, 640), F32),
            pltpu.VMEM((4, 8, 384), F32),
            pltpu.VMEM((4, 2, 8, 384), F32),
            pltpu.VMEM((4, 8, 384), F32),
            *plane_scratch(768),
            *plane_scratch(768),
            *plane_scratch(512),
            *plane_scratch(1024),
            pltpu.SemaphoreType.DMA((SENDS,)),
            pltpu.SemaphoreType.DMA((COPIES,)),
        ],
        compiler_params=pltpu.CompilerParams(
            collective_id=1, has_side_effects=True, vmem_limit_bytes=VMEM_BYTES
        ),
        cost_estimate=pl.CostEstimate(
            flops=10_000_000_000, bytes_accessed=16_000_000, transcendentals=0
        ),
        name="layer",
    )(
        block_input.reshape(4, 64, 1024), out_cotangent.reshape(4, 64, 1024), segments.reshape(2, 128),
        row(first_gain), row(first_shift), query_weight, row(query_bias), key_weight, value_weight,
        row(value_bias), output_weight, row(output_bias), row(second_gain), row(second_shift), up_weight,
        row(up_bias), down_weight, row(down_bias),
    )
    wide, narrow = ((1, 1024), F32), ((1, 256), F32)
    square, tall, tokens = ((32, 256), F32), ((32, 1024), F32), ((4, 64, 1024), F32)
    outs = pl.pallas_call(
        write_kernel,
        out_shape=shapes(
            tokens, tokens, wide, wide, square, narrow, square, square, narrow, square, wide, wide, wide,
            tall, wide, tall, wide,
        ),
        in_specs=[vmem] * 6,
        out_specs=[vmem] * 17,
        name="write",
    )(*results)
    ends = {0: (2, 1, 128, 1024), 1: (2, 1, 128, 1024)}
    flat = (2, 3, 5, 8, 10, 11, 12, 14, 16)
    return tuple(
        out.reshape(ends[i]) if i in ends else (out.reshape(-1) if i in flat else out)
        for i, out in enumerate(outs)
    )


def solution(mesh):
    tokens = P(None, "seq", "ctx", None)
    matrix = P(("seq", "ctx"), "head")
    return jax.shard_map(
        on_device,
        mesh=mesh,
        in_specs=(
            tokens, P(), P(), matrix, P("head"), matrix, matrix, P("head"), matrix, P(), P(), P(),
            matrix, P("head"), matrix, P(), P(None, "seq", "ctx"), tokens,
        ),
        out_specs=(
            tokens, tokens, P(), P(), matrix, P("head"), matrix, matrix, P("head"), matrix, P(), P(),
            P(), matrix, P("head"), matrix, P(),
        ),
        check_vma=False,
    )
```

```python
import jax
import jax.numpy as jnp
from jax import lax
from jax.experimental import pallas as pl
from jax.experimental.pallas import tpu as pltpu
from jax.sharding import PartitionSpec as P

F32 = jnp.float32
BF16 = jnp.bfloat16
MESH = pl.DeviceIdType.MESH
VMEM_BYTES = 56 * 1024 * 1024
KEYS = 512
COPIES = 121
SENDS = 18


def dot(left, right, dim_left, dim_right):
    return lax.dot_general(
        left, right, (((dim_left,), (dim_right,)), ((), ())), preferred_element_type=F32
    )


def turn(index, by):
    return lax.rem(index + by, 4)


class Place:
    def __init__(self):
        self.seq = lax.axis_index("seq")
        self.ctx = lax.axis_index("ctx")
        self.z = lax.axis_index("head")
        self.core = lax.rem(self.ctx, 2)
        self.y = lax.rem(lax.div(self.ctx, 2), 4)
        self.low = lax.div(self.ctx, 8)
        self.x = self.seq * 2 + self.low
        self.x_plus = self.at(turn(self.x, 1), self.y, self.core, self.z)
        self.x_minus = self.at(turn(self.x, 3), self.y, self.core, self.z)
        self.y_plus = self.at(self.x, turn(self.y, 1), self.core, self.z)
        self.y_minus = self.at(self.x, turn(self.y, 3), self.core, self.z)
        self.z_plus = self.at(self.x, self.y, self.core, turn(self.z, 1))
        self.z_minus = self.at(self.x, self.y, self.core, turn(self.z, 3))
        self.x_across = self.at(turn(self.x, 2), self.y, self.core, self.z)
        self.y_across = self.at(self.x, turn(self.y, 2), self.core, self.z)
        self.z_across = self.at(self.x, self.y, self.core, turn(self.z, 2))
        self.x_ring = (self.x, (self.x_plus, self.x_minus, self.x_across))
        self.y_ring = (self.y, (self.y_plus, self.y_minus, self.y_across))
        self.z_ring = (self.z, (self.z_plus, self.z_minus, self.z_across))
        self.sibling = self.at(self.x, self.y, 1 - self.core, self.z)
        self.pair = self.at(self.seq * 2 + 1 - self.low, self.y, self.core, self.z)

    def at(self, x, y, core, z):
        return (lax.div(x, 2), (lax.rem(x, 2) * 4 + y) * 2 + core, z)

    def greet(self, partners):
        barrier = pltpu.get_barrier_semaphore()
        for partner in partners:
            pl.semaphore_signal(barrier, inc=1, device_id=partner, device_id_type=MESH)
        pl.semaphore_wait(barrier, len(partners))


class Copy:
    def __init__(self, net, made, index):
        self.net, self.made, self.index = net, made, index

    def wait_recv(self):
        self.made.wait_recv()

    def wait_send(self):
        self.made.wait_send()
        self.net.free.append(self.index)

    def wait(self):
        self.wait_send()
        self.wait_recv()


class Net:
    def __init__(self, send, recv):
        self.send, self.recv, self.used, self.free, self.most = send, recv, 0, [], 0

    def copy(self, src, dst, device):
        index = self.free.pop() if self.free else self.most
        self.most = max(self.most, index + 1)
        made = pltpu.make_async_remote_copy(
            src_ref=src,
            dst_ref=dst,
            send_sem=self.send.at[index],
            recv_sem=self.recv.at[self.used],
            device_id=device,
            device_id_type=MESH,
        )
        self.used += 1
        made.start()
        return Copy(self, made, index)

    def copies(self, each, whole):
        index = self.free.pop() if self.free else self.most
        self.most = max(self.most, index + 1)
        sems = {"send_sem": self.send.at[index], "recv_sem": self.recv.at[self.used]}
        self.used += 1
        for src, dst, device in each:
            pltpu.make_async_remote_copy(
                src_ref=src, dst_ref=dst, device_id=device, device_id_type=MESH, **sems
            ).start()
        made = pltpu.make_async_remote_copy(
            src_ref=whole, dst_ref=whole, device_id=each[0][2], device_id_type=MESH, **sems
        )
        return [Copy(self, made, index)]


def run(steps):
    for _ in steps:
        pass


FROM = (3, 1, 2)
TO = (1, 3, 2)


def add_into(view, *others):
    value = view[...].astype(F32)
    for other in others:
        value = value + other[...].astype(F32)
    view[...] = value.astype(BF16)


class Gather:
    def __init__(self, net, region, ring, apart=False):
        self.here, others = ring
        own = region(self.here)
        self.region, self.apart = region, apart
        if apart:
            self.copies = [net.copy(own, own, device) for device in others]
        else:
            self.copies = net.copies([(own, own, device) for device in others], region(slice(0, 3)))

    def arrivals(self):
        for copy, step in zip(self.copies, FROM):
            copy.wait_recv()
            yield self.region(turn(self.here, step))

    def sent(self):
        for copy in self.copies:
            copy.wait_send()

    def finish(self):
        for copy in self.copies:
            copy.wait()


class Scatter:
    def __init__(self, net, part, slots, ring):
        here, others = ring
        self.copies = net.copies(
            [
                (part(turn(here, step)), slots.at[index], device)
                for index, (step, device) in enumerate(zip(TO, others))
            ],
            slots,
        )

    def finish(self):
        for copy in self.copies:
            copy.wait()


TOP, LOW = slice(0, 16), slice(16, 32)


def gather_plane(net, at, full, urgent=False, around=None):
    x, y, core = at.x, at.y, at.core
    done = []

    def share(view):
        done.append(net.copy(view, view, at.sibling))

    a = Gather(net, lambda j: full.at[j, y, core, TOP, :], at.x_ring)
    b = Gather(net, lambda j: full.at[x, j, core, LOW, :], at.y_ring)
    yield
    a.finish()
    a = Gather(net, lambda j: full.at[:, j, core, TOP, :], at.y_ring, urgent)
    b.finish()
    b = Gather(net, lambda j: full.at[j, :, core, LOW, :], at.x_ring, urgent)
    if urgent:
        share(full.at[:, y, core, TOP, :])
        share(full.at[x, :, core, LOW, :])
    yield
    if urgent:
        for one, two in zip(a.arrivals(), b.arrivals()):
            share(one)
            share(two)
        a.sent()
        b.sent()
    else:
        a.finish()
        b.finish()
        if around is None:
            share(full.at[:, :, core])
        else:
            steps = Gather(net, lambda j: around.at[j, :, :, core], at.z_ring)
            yield
            steps.finish()
            share(around.at[:, :, :, core])
    yield
    for copy in done:
        copy.wait()


def scatter_plane(net, at, partial, other, total, wide, thin, result):
    x, y, core = at.x, at.y, at.core
    shared = net.copy(partial.at[:, :, 1 - core], other, at.sibling)
    yield
    shared.wait()

    def add(index, carry):
        i, j = lax.div(index, 4), lax.rem(index, 4)
        total[i, j] = (partial[i, j, core].astype(F32) + other[i, j].astype(F32)).astype(BF16)
        return carry

    lax.fori_loop(0, 16, add, 0)
    a = Scatter(net, lambda j: total.at[:, j, TOP, :], wide.at[0], at.y_ring)
    b = Scatter(net, lambda j: total.at[j, :, LOW, :], wide.at[1], at.x_ring)
    yield
    a.finish()
    add_into(total.at[:, y, TOP, :], wide.at[0, 0], wide.at[0, 1], wide.at[0, 2])
    a = Scatter(net, lambda j: total.at[j, y, TOP, :], thin.at[0], at.x_ring)
    b.finish()
    add_into(total.at[x, :, LOW, :], wide.at[1, 0], wide.at[1, 1], wide.at[1, 2])
    b = Scatter(net, lambda j: total.at[x, j, LOW, :], thin.at[1], at.y_ring)
    yield
    for index, steps, rows in ((0, a, TOP), (1, b, LOW)):
        steps.finish()
        extra = thin[index, 0].astype(F32) + thin[index, 1].astype(F32) + thin[index, 2].astype(F32)
        result(rows, total[x, y, rows, :].astype(F32) + extra)


def sum_small(net, at, by_x, by_y, by_z, urgent):
    x, y, z, core = at.x, at.y, at.z, at.core
    steps = Gather(net, lambda j: by_x.at[j], at.x_ring)
    yield
    steps.finish()
    by_y[y, core] = by_x[0] + by_x[1] + by_x[2] + by_x[3]
    own = by_y.at[y, core]
    if urgent:
        copies = [net.copy(own, own, device) for device in at.y_ring[1] + (at.sibling,)]
        copies = copies + [net.copy(own, own, at.at(x, turn(y, step), 1 - core, z)) for step in TO]
        yield
        for copy in copies:
            copy.wait()
    else:
        steps = Gather(net, lambda j: by_y.at[j, core], at.y_ring)
        yield
        steps.finish()
        view = by_y.at[:, core]
        copy = net.copy(view, view, at.sibling)
        yield
        copy.wait()
    total = by_y[0, 0] + by_y[0, 1]
    for i in range(1, 4):
        total = total + by_y[i, 0] + by_y[i, 1]
    by_z[z] = total
    steps = Gather(net, lambda j: by_z.at[j], at.z_ring)
    yield
    steps.finish()


def plane_scratch(width):
    return [
        pltpu.VMEM((4, 4, 2, 32, width), BF16),
        pltpu.VMEM((4, 4, 32, width), BF16),
        pltpu.VMEM((4, 4, 32, width), BF16),
        pltpu.VMEM((2, 3, 4, 16, width), BF16),
        pltpu.VMEM((2, 3, 16, width), BF16),
    ]


def norm_parts(value):
    center = value - jnp.mean(value, axis=-1, keepdims=True)
    rate = lax.rsqrt(jnp.mean(center * center, axis=-1, keepdims=True) + 1e-05)
    return center * rate, rate


def norm_back(grad, unit, rate, gain):
    inner = grad * gain
    even = jnp.mean(inner, axis=-1, keepdims=True)
    along = jnp.mean(inner * unit, axis=-1, keepdims=True)
    return rate * (inner - even - unit * along)


def column_sum(value):
    return jnp.sum(value, axis=0, keepdims=True)


def slope_of(at):
    by_z = jnp.where(at.z == 0, 1.0, jnp.where(at.z == 1, 0.25, jnp.where(at.z == 2, 0.0625, 0.015625)))
    by_y = jnp.where(at.y == 0, 2.0**-0.5, jnp.where(at.y == 1, 0.5, jnp.where(at.y == 2, 2.0**-1.5, 0.25)))
    return by_z.astype(F32) * by_y.astype(F32)


def fill_distance(first_query, dist, base, chunks, lanes, start):
    def fill(block, carry):
        lane = lax.broadcasted_iota(jnp.int32, (256, 128), 1)
        query = (lane + first_query).astype(F32)
        key = (lax.broadcasted_iota(jnp.int32, (256, 128), 0) + block * 256).astype(F32)
        apart = query - key
        value = jnp.where((key >= start) & (apart >= 0.0), apart, -1.0)
        rows = pl.ds(pl.multiple_of(base + block * 256, 256), 256)
        dist[rows, lanes] = value
        return carry

    lax.fori_loop(0, chunks * 2, fill, 0)


def masked_scores(keys, queries, dist, slope):
    raw = dot(keys, queries, 1, 0) * 0.125
    return jnp.where(dist >= 0.0, raw - slope * dist, -1000000000.0)


def key_block(kvq, block):
    low, y = block // 2, (block % 2) * 2
    return kvq[low, y : y + 2, :, 0:128, :].reshape(KEYS, 128)


class Chips:
    def __init__(self, at):
        self.steps = []
        for dx in range(2):
            for dy in range(4):
                if dx or dy:
                    low = 1 - at.low if dx else at.low
                    y = turn(at.y, dy)
                    device = at.at(at.seq * 2 + low, y, at.core, at.z)
                    source = (low, turn(at.y, 4 - dy))
                    self.steps.append((low, y, device, source))

    def swap(self, net, src, dst):
        return [(net.copy(src.at[low, y], dst, device), source) for low, y, device, source in self.steps]


def join_tiles(tiles, first):
    rows = [
        jnp.concatenate([tiles[i, j, first : first + 64, :].astype(F32) for j in range(4)], axis=0).T
        for i in range(2)
    ]
    return jnp.concatenate(rows, axis=0).astype(BF16)


def pad_heads(tiles, n, first, above):
    i, j = n // 2, (n % 2) * 2
    wide = [tiles[i, j + k, first : first + 64, :].astype(F32) for k in range(2)]
    wide = jnp.concatenate(wide, axis=1)
    both = [wide, jnp.zeros((64, 256), F32)]
    return jnp.concatenate(both if above else both[::-1], axis=0).astype(BF16)


def layer_kernel(
    x_ref, dy_ref, seg_ref, gain1_ref, shift1_ref, wq_ref, qb_ref, wk_ref, wv_ref, vb_ref, wo_ref, ob_ref,
    gain2_ref, shift2_ref, wu_ref, ub_ref, wd_ref, db_ref,
    bo_ref, dxin_ref, dqkv_ref, dwo_ref, dud_ref, sums_ref,
    w1, wo, wu, wd, seg_all, h1_ref, unit1,
    kvq_send, kvq, o_send, o_all, do_send, do_all, sums_kv, kv_out, kv_in, back_send, own_all, dist, score, dp_ref,
    o_out, o_in, do_out, do_in, part, slots, gathered, dg, g_ref, du_ref, gx, gy, gz, hx, hy, hz,
    dw1, other1, total1, wide1, thin1,
    dwo_part, other_o, total_o, wide_o, thin_o,
    dwu_part, other_u, total_u, wide_u, thin_u,
    dwd_part, other_d, total_d, wide_d, thin_d,
    send, recv,
):
    at = Place()
    net = Net(send, recv)
    chips = Chips(at)
    x, y, z, core, low = at.x, at.y, at.z, at.core, at.low
    partners = at.x_ring[1] + at.y_ring[1] + at.z_ring[1] + (at.sibling,)
    partners = partners + tuple(at.at(x, turn(y, step), 1 - core, z) for step in TO)
    partners = partners + tuple(
        at.at(at.seq * 2 + 1 - low, turn(y, step), core, z) for step in TO
    )
    at.greet(partners)

    mine = w1.at[x, y, core]
    mine[:, 0:256] = wq_ref[...]
    mine[:, 256:512] = wk_ref[...]
    mine[:, 512:768] = wv_ref[...]
    w1_steps = gather_plane(net, at, w1, urgent=True)
    next(w1_steps)
    wo[z, x, y, core] = wo_ref[...]
    wo_steps = gather_plane(net, at, wo.at[z], around=wo)
    next(wo_steps)
    seg_all[low, y, core] = jnp.concatenate([seg_ref[...]] * 4, axis=0)
    seg = Gather(net, lambda j: seg_all.at[low, j, core], at.y_ring)
    wu[x, y, core] = wu_ref[...]
    wd[x, y, core] = wd_ref[...]
    unit, _ = norm_parts(x_ref[...].reshape(256, 1024).astype(F32))
    unit1[...] = unit
    h1_ref[...] = (unit * gain1_ref[...] + shift1_ref[...]).astype(BF16)
    next(w1_steps)
    seg.finish()
    view = seg_all.at[low, :, core]
    seg_pair = net.copy(view, view, at.pair)
    next(w1_steps)
    next(wo_steps)
    wd_steps = gather_plane(net, at, wd)
    next(wd_steps)
    seg_pair.wait()
    view = seg_all.at[:, :, core]
    seg_share = net.copy(view, view, at.sibling)
    run(w1_steps)

    h1 = h1_ref[...]
    wide = dot(h1, w1[...].reshape(1024, 768), 1, 0)
    turned = (wide[:, 0:256] + qb_ref[...]).T.astype(BF16)
    keys, values = wide[:, 256:512], wide[:, 512:768] + vb_ref[...]
    for i in range(2):
        for j in range(4):
            rows, lanes = slice(i * 128, i * 128 + 128), slice(j * 64, j * 64 + 64)
            tile = jnp.concatenate([keys[rows, lanes], values[rows, lanes]], axis=1)
            kvq_send[i, j, 0:128, :] = tile.astype(BF16)
            kvq_send[i, j, 128:192, :] = turned[lanes, rows]
    kv_copies = chips.swap(net, kvq_send, kvq.at[low, y, core])
    kvq[low, y, core] = kvq_send[low, y]
    shares = []
    seg_share.wait()
    counts = []
    for number in range(1, 4):
        below = (seg_all[:, :, :, 0:2, :] < number).astype(F32)
        below = jnp.sum(below.reshape(16, 2, 128), axis=0)
        below = jnp.sum(below, axis=-1, keepdims=True)
        counts.append(jnp.where(low == 0, below[0:1], below[1:2]))
    bases = [0, 512, 1536, 3072]
    for n in range(4):
        for k in range(2):
            there = seg_all[n // 2, (n % 2) * 2 + k, core]
            there = jnp.where(low == 0, there[0:1], there[1:2])
            found = jnp.zeros((1, 128), F32)
            for number in range(1, 4):
                found = jnp.where(there == number, counts[number - 1], found)
            first_query = (n * 4 + k * 2 + core) * 128
            fill_distance(
                first_query, dist, bases[n], n + 1, slice(k * 128, k * 128 + 128), found
            )
    next(wo_steps)
    for index, (copy, source) in enumerate(kv_copies):
        copy.wait_recv()
        if index == 2:
            view = kvq.at[low, :, core, 0:128, :]
            shares.append(net.copy(view, view, at.sibling))
        if index > 2:
            view = kvq.at[source[0], source[1], core, 0:128, :]
            shares.append(net.copy(view, view, at.sibling))
    for copy, _ in kv_copies:
        copy.wait_send()
    wu_steps = gather_plane(net, at, wu)
    next(wu_steps)
    next(wd_steps)
    for copy in shares:
        copy.wait()

    slope = slope_of(at)
    for n in range(4):
        queries = pad_heads(kvq.at[:, :, core], n, 128, True)
        top = jnp.full((1, 256), -3.0e38, F32)
        for block in range(n + 1):
            rows = slice(block * KEYS, block * KEYS + KEYS)
            value = masked_scores(
                key_block(kvq, block), queries,
                dist[bases[n] + block * KEYS : bases[n] + block * KEYS + KEYS, :], slope,
            )
            score[rows, :] = value
            top = jnp.maximum(top, jnp.max(value, axis=0, keepdims=True))
        summed = jnp.zeros((1, 256), F32)
        for block in range(n + 1):
            rows = slice(block * KEYS, block * KEYS + KEYS)
            value = jnp.exp(score[rows, :] - top)
            score[rows, :] = value
            summed = summed + column_sum(value)
        scale = 1.0 / summed
        mixed = jnp.zeros((128, 256), F32)
        for block in range(n + 1):
            rows = slice(block * KEYS, block * KEYS + KEYS)
            probs = score[rows, :] * scale
            dist[bases[n] + block * KEYS : bases[n] + block * KEYS + KEYS, :] = probs
            mixed = mixed + dot(key_block(kvq, block), probs.astype(BF16), 0, 0)
        for k in range(2):
            lanes = slice(k * 128, k * 128 + 128)
            o_send[n // 2, (n % 2) * 2 + k] = mixed[64:128, lanes].astype(BF16)
    copies = chips.swap(net, o_send, o_all.at[low, y])
    o_all[low, y] = o_send[low, y]
    next(wo_steps)

    def half(h):
        return slice(h * 32, h * 32 + 32)

    def scatter_half(index, h):
        return Scatter(net, lambda j: part.at[index, j, half(h), :], slots.at[index, h], at.z_ring)

    def scatter(index, value):
        part[index] = value.astype(BF16).reshape(4, 64, 1024)
        return [scatter_half(index, 0), scatter_half(index, 1)]

    def owned(index, h):
        extra = slots[index, h, 0].astype(F32) + slots[index, h, 1].astype(F32)
        return part[index, z, half(h), :].astype(F32) + (extra + slots[index, h, 2].astype(F32))

    def gather(buffer, h):
        return Gather(net, lambda j: buffer.at[j, half(h), :], at.z_ring)

    def put_sums(to, sums):
        for i in range(8):
            for j, value in enumerate(sums):
                to[x, i : i + 1, j * 128 : j * 128 + 128] = value[:, i * 128 : i * 128 + 128]

    def put_grad(to, first, width, left, right):
        for i in range(4):
            value = dot(left(i), right, 0, 0).astype(BF16)
            to[i, :, :, :, first : first + width] = value.reshape(4, 2, 32, width)

    next(wu_steps)
    for copy, _ in copies:
        copy.wait()
    mixed = join_tiles(o_all, 0)

    def swap_rows(src, dst):
        dst[z] = src[z]
        return net.copies(
            [
                (src.at[turn(z, step)], dst.at[z], device)
                for step, device in zip(TO, at.z_ring[1])
            ],
            dst.at[0:3],
        )

    o_out[...] = mixed.reshape(4, 64, 256)
    copies = swap_rows(o_out, o_in)
    next(wd_steps)
    run(wo_steps)
    for copy in copies:
        copy.wait()
    added = ob_ref[...]
    for j in range(4):
        added = added + dot(o_in[j], wo[j].reshape(1024, 256), 1, 1)
    x1, units, rates, gathers = [], [], [], []
    for h in range(2):
        x1.append(x_ref[z, half(h), :].astype(F32) + added[half(h), :])
        unit, rate = norm_parts(x1[h])
        gathered[0, z, half(h), :] = (unit * gain2_ref[...] + shift2_ref[...]).astype(BF16)
        gathers.append(gather(gathered.at[0], h))
        units.append(unit)
        rates.append(rate)
        if h == 0:
            next(wu_steps)
    upstream = [dy_ref[z, half(h), :].astype(F32) for h in range(2)]
    dy_sum = column_sum(upstream[0]) + column_sum(upstream[1])
    run(wd_steps)
    down = wd[...].reshape(1024, 1024)
    dg[...] = dot(dy_ref[...].reshape(256, 1024), down, 1, 0).reshape(4, 64, 1024)
    run(wu_steps)
    up = wu[...].reshape(1024, 1024)
    back = []
    for h in range(2):
        gathers[h].finish()
        h2 = gathered[0, :, half(h), :].reshape(128, 1024)
        for i in range(2):
            cols = slice(i * 512, i * 512 + 512)
            u = dot(h2, wu[:, :, :, :, cols].reshape(1024, 512), 1, 0) + ub_ref[:, cols]
            tanh = jnp.tanh(0.7978845608028654 * (u + 0.044715 * u * u * u))
            g_ref[:, half(h), cols] = (0.5 * u * (1.0 + tanh)).astype(BF16).reshape(4, 32, 512)
            turned = 0.5 * u * (1.0 - tanh * tanh) * 0.7978845608028654 * (1.0 + 3 * 0.044715 * u * u)
            turned = (0.5 * (1.0 + tanh) + turned).reshape(4, 32, 512)
            du_ref[:, half(h), cols] = (dg[:, half(h), cols] * turned).astype(BF16)
        value = dot(du_ref[:, half(h), :].reshape(128, 1024), up, 1, 1).astype(BF16)
        part[2, :, half(h), :] = value.reshape(4, 32, 1024)
        back.append(scatter_half(2, h))
    du = du_ref[...].reshape(256, 1024)
    g = g_ref[...].reshape(256, 1024)
    put_grad(
        dwd_part, 0, 1024, lambda i: dy_ref[:, :, i * 256 : i * 256 + 256].reshape(256, 256), g
    )

    def put_d(rows, value):
        dud_ref[rows, 1024:2048] = value

    def put_u(rows, value):
        dud_ref[rows, 0:768] = value

    dwd_steps = scatter_plane(net, at, dwd_part, other_d, total_d, wide_d, thin_d, put_d)
    next(dwd_steps)
    def h2_columns(i):
        return gathered[0, :, :, i * 256 : i * 256 + 256].reshape(256, 256)

    put_grad(dwu_part, 0, 768, h2_columns, du[:, 0:768])
    dwu_steps = scatter_plane(net, at, dwu_part, other_u, total_u, wide_u, thin_u, put_u)
    put_grad(dwo_part, 0, 256, h2_columns, du[:, 768:1024])
    dx1, dh2, gathers = [], [], []
    for h in range(2):
        back[h].finish()
        dh2.append(owned(2, h))
        dx1.append(upstream[h] + norm_back(dh2[h], units[h], rates[h], gain2_ref[...]))
        gathered[1, z, half(h), :] = dx1[h].astype(BF16)
        if h == 0:
            next(dwd_steps)
            next(dwu_steps)
    for j in range(4):
        do_out[j] = dot(gathered[1, z], wo[j].reshape(1024, 256), 1, 0).astype(BF16)
    copies = swap_rows(do_out, do_in)
    gathers = [gather(gathered.at[1], 0), gather(gathered.at[1], 1)]
    early_sums = (
        column_sum(dx1[0]) + column_sum(dx1[1]),
        column_sum(dh2[0] * units[0]) + column_sum(dh2[1] * units[1]),
        column_sum(dh2[0]) + column_sum(dh2[1]),
        dy_sum,
        column_sum(du.astype(F32)),
    )
    put_sums(gx, early_sums)
    early = sum_small(net, at, gx, gy, gz, False)
    next(early)
    ffn = dot(g, down, 1, 1)
    for copy in copies:
        copy.wait()
    grads = do_in[...].reshape(256, 256).astype(F32).T.astype(BF16)
    for i in range(2):
        for j in range(4):
            do_send[i, j] = grads[j * 64 : j * 64 + 64, i * 128 : i * 128 + 128]
    copies = chips.swap(net, do_send, do_all.at[low, y])
    do_all[low, y] = do_send[low, y]
    front = scatter(1, ffn)
    def put_o(rows, value):
        dud_ref[rows, 768:1024] = value[:, 0:256]
        dwo_ref[rows, :] = value[:, 256:512]

    for copy, _ in copies:
        copy.wait()
    next(dwd_steps)
    next(dwu_steps)
    next(early)

    shared = []
    lane = lax.broadcasted_iota(jnp.int32, (1, 1, 1, 128), 3)
    scale = jnp.where(lane < 64, 0.125, 1.0).astype(F32)
    scale = scale.reshape(1, 1, 128)
    for n in (3, 2, 1, 0):
        queries = pad_heads(kvq.at[:, :, core], n, 128, True)
        grads = pad_heads(do_all, n, 0, False)
        right = jnp.concatenate([queries, grads], axis=1)
        inner = jnp.zeros((1, 256), F32)
        for block in range(n + 1):
            rows = slice(block * KEYS, block * KEYS + KEYS)
            probs = dist[bases[n] + block * KEYS : bases[n] + block * KEYS + KEYS, :]
            prob_grad = dot(key_block(kvq, block), grads, 1, 0)
            dp_ref[rows, :] = prob_grad
            inner = inner + column_sum(probs * prob_grad)
        query_grad = jnp.zeros((128, 256), F32)
        for block in range(n + 1):
            rows = slice(block * KEYS, block * KEYS + KEYS)
            probs = dist[bases[n] + block * KEYS : bases[n] + block * KEYS + KEYS, :]
            score_grad = (probs * (dp_ref[rows, :] - inner)).astype(BF16)
            both = jnp.concatenate([score_grad, probs.astype(BF16)], axis=1)
            i, j = block // 2, (block % 2) * 2
            value = dot(both, right, 1, 1).reshape(2, 2, 128, 128)
            if n < 3:
                value = value + sums_kv[i, j : j + 2]
            sums_kv[i, j : j + 2] = value
            query_grad = query_grad + dot(key_block(kvq, block), score_grad, 0, 0)
        query_grad = (query_grad * 0.125).astype(BF16)
        for k in range(2):
            lanes = slice(k * 128, k * 128 + 128)
            back_send[n // 2, (n % 2) * 2 + k, 128:192, :] = query_grad[0:64, lanes]
        i, chunk = n // 2, slice((n % 2) * 2, (n % 2) * 2 + 2)
        kv_out[i, chunk] = (sums_kv[i, chunk, 1 - core] * scale).astype(BF16)
        shared.append(net.copy(kv_out.at[i, chunk], kv_in.at[i, chunk], at.sibling))
        if n == 3:
            for steps in gathers:
                steps.finish()
            put_grad(
                dwo_part, 256, 256,
                lambda i: gathered[1, :, :, i * 256 : i * 256 + 256].reshape(256, 256), mixed,
            )
            dwo_steps = scatter_plane(net, at, dwo_part, other_o, total_o, wide_o, thin_o, put_o)
            next(dwo_steps)

    for copy in shared:
        copy.wait()
    back_send[:, :, 0:128, :] = (sums_kv[:, :, core] * scale + kv_in[...].astype(F32)).astype(BF16)
    kv_copies = chips.swap(net, back_send, own_all.at[low, y])
    own_all[low, y] = back_send[low, y]
    run(dwd_steps)
    outs = []
    for h in range(2):
        front[h].finish()
        bo_ref[z, half(h), :] = (x1[h] + owned(1, h) + db_ref[...]).astype(BF16)
        outs.append(gather(bo_ref, h))
    h1 = h1_ref[...]

    def left(i):
        return h1[:, i * 256 : i * 256 + 256]

    for copy, _ in kv_copies:
        copy.wait()
    next(dwo_steps)
    dq = join_tiles(own_all, 128)
    whole = []
    for i in range(2):
        tiles = [own_all[i, j, 0:128, :].astype(F32) for j in range(4)]
        keys = [tile[:, 0:64] for tile in tiles]
        values = [tile[:, 64:128] for tile in tiles]
        whole.append(jnp.concatenate(keys + values, axis=1))
    dkv = jnp.concatenate(whole, axis=0).astype(BF16)
    dqkv = jnp.concatenate([dq, dkv], axis=1)
    put_grad(dw1, 0, 768, left, dqkv)

    def put1(rows, value):
        dqkv_ref[rows, :] = value

    dw1_steps = scatter_plane(net, at, dw1, other1, total1, wide1, thin1, put1)
    next(dw1_steps)
    direct = dot(dqkv, w1[...].reshape(1024, 768), 1, 1)
    steps = scatter(3, direct)
    gain_sum, shift_sum = column_sum(direct * unit1[...]), column_sum(direct)
    query_sum, value_sum = column_sum(dq.astype(F32)), column_sum(dkv[:, 256:512].astype(F32))
    bias_sum = jnp.concatenate([query_sum, value_sum, jnp.zeros((1, 512), F32)], axis=1)
    put_sums(hx, (gain_sum, shift_sum, bias_sum))
    late = sum_small(net, at, hx, hy, hz, True)
    next(late)
    next(early)
    next(dwu_steps)
    next(dw1_steps)
    next(late)
    next(early)
    gathers = []
    for h in range(2):
        steps[h].finish()
        unit, rate = norm_parts(x_ref[z, half(h), :].astype(F32))
        grad = dx1[h] + norm_back(owned(3, h), unit, rate, gain1_ref[...])
        dxin_ref[z, half(h), :] = grad.astype(BF16)
        gathers.append(gather(dxin_ref, h))
    next(late)
    next(dwo_steps)
    next(dw1_steps)
    run(dwu_steps)
    run(dwo_steps)
    run(dw1_steps)
    run(early)
    run(late)
    early_over = gz[0, :, 0:512] + gz[1, :, 0:512] + gz[2, :, 0:512] + gz[3, :, 0:512]
    late_over = hz[0, :, 0:256] + hz[1, :, 0:256] + hz[2, :, 0:256] + hz[3, :, 0:256]
    for i in range(8):
        lanes = slice(i * 128, i * 128 + 128)
        for j in range(2):
            sums_ref[j : j + 1, lanes] = late_over[i : i + 1, j * 128 : j * 128 + 128]
        for j in range(4):
            sums_ref[j + 2 : j + 3, lanes] = early_over[i : i + 1, j * 128 : j * 128 + 128]
        sums_ref[6:7, lanes] = gz[z, i : i + 1, 512:640]
        sums_ref[7:8, lanes] = hz[z, i : i + 1, 256:384]
    for steps in outs + gathers:
        steps.finish()


def write_kernel(
    bo_ref, dxin_ref, dqkv_ref, dwo_ref, dud_ref, sums_ref,
    block_ref, input_ref, g1_ref, s1_ref, dwq_ref, qb_ref, dwk_ref, dwv_ref, vb_ref, out_ref,
    ob_ref, g2_ref, s2_ref, dwu_ref, ub_ref, dwd_ref, db_ref,
):
    block_ref[...] = bo_ref[...].astype(F32)
    input_ref[...] = dxin_ref[...].astype(F32)
    dwq_ref[...] = dqkv_ref[:, 0:256]
    dwk_ref[...] = dqkv_ref[:, 256:512]
    dwv_ref[...] = dqkv_ref[:, 512:768]
    out_ref[...] = dwo_ref[...]
    dwu_ref[...] = dud_ref[:, 0:1024]
    dwd_ref[...] = dud_ref[:, 1024:2048]
    for index, ref in enumerate((g1_ref, s1_ref, ob_ref, g2_ref, s2_ref, db_ref, ub_ref)):
        ref[...] = sums_ref[index : index + 1, :]
    qb_ref[...] = sums_ref[7:8, 0:256]
    vb_ref[...] = sums_ref[7:8, 256:512]


def on_device(
    block_input, first_gain, first_shift, query_weight, query_bias, key_weight, value_weight, value_bias,
    output_weight, output_bias, second_gain, second_shift, up_weight, up_bias, down_weight, down_bias,
    segments, out_cotangent,
):
    vmem = pl.BlockSpec(memory_space=pltpu.VMEM)

    def row(value):
        return value.reshape(1, -1)

    def shapes(*pairs):
        return [jax.ShapeDtypeStruct(shape, kind) for shape, kind in pairs]

    results = pl.pallas_call(
        layer_kernel,
        out_shape=shapes(
            ((4, 64, 1024), BF16),
            ((4, 64, 1024), BF16),
            ((32, 768), F32),
            ((32, 256), F32),
            ((32, 2048), F32),
            ((8, 1024), F32),
        ),
        in_specs=[vmem] * 18,
        out_specs=[vmem] * 6,
        scratch_shapes=[
            pltpu.VMEM((4, 4, 2, 32, 768), BF16),
            pltpu.VMEM((4, 4, 4, 2, 32, 256), BF16),
            pltpu.VMEM((4, 4, 2, 32, 1024), BF16),
            pltpu.VMEM((4, 4, 2, 32, 1024), BF16),
            pltpu.VMEM((2, 4, 2, 8, 128), jnp.int32),
            pltpu.VMEM((256, 1024), BF16),
            pltpu.VMEM((256, 1024), F32),
            pltpu.VMEM((2, 4, 192, 128), BF16),
            pltpu.VMEM((2, 4, 2, 192, 128), BF16),
            *[pltpu.VMEM((2, 4, 64, 128), BF16)] * 4,
            pltpu.VMEM((2, 4, 2, 128, 128), F32),
            *[pltpu.VMEM((2, 4, 128, 128), BF16)] * 2,
            *[pltpu.VMEM((2, 4, 192, 128), BF16)] * 2,
            pltpu.VMEM((5120, 256), F32),
            pltpu.VMEM((2048, 256), F32),
            pltpu.VMEM((2048, 256), F32),
            *[pltpu.VMEM((4, 64, 256), BF16)] * 4,
            pltpu.VMEM((4, 4, 64, 1024), BF16),
            pltpu.VMEM((4, 2, 3, 32, 1024), BF16),
            pltpu.VMEM((2, 4, 64, 1024), BF16),
            pltpu.VMEM((4, 64, 1024), F32),
            pltpu.VMEM((4, 64, 1024), BF16),
            pltpu.VMEM((4, 64, 1024), BF16),
            pltpu.VMEM((4, 8, 640), F32),
            pltpu.VMEM((4, 2, 8, 640), F32),
            pltpu.VMEM((4, 8, 640), F32),
            pltpu.VMEM((4, 8, 384), F32),
            pltpu.VMEM((4, 2, 8, 384), F32),
            pltpu.VMEM((4, 8, 384), F32),
            *plane_scratch(768),
            *plane_scratch(512),
            *plane_scratch(768),
            *plane_scratch(1024),
            pltpu.SemaphoreType.DMA((SENDS,)),
            pltpu.SemaphoreType.DMA((COPIES,)),
        ],
        compiler_params=pltpu.CompilerParams(
            collective_id=1, has_side_effects=True, vmem_limit_bytes=VMEM_BYTES
        ),
        cost_estimate=pl.CostEstimate(
            flops=10_000_000_000, bytes_accessed=16_000_000, transcendentals=0
        ),
        name="layer",
    )(
        block_input.reshape(4, 64, 1024), out_cotangent.reshape(4, 64, 1024), segments.reshape(2, 128),
        row(first_gain), row(first_shift), query_weight, row(query_bias), key_weight, value_weight,
        row(value_bias), output_weight, row(output_bias), row(second_gain), row(second_shift), up_weight,
        row(up_bias), down_weight, row(down_bias),
    )
    wide, narrow = ((1, 1024), F32), ((1, 256), F32)
    square, tall, tokens = ((32, 256), F32), ((32, 1024), F32), ((4, 64, 1024), F32)
    outs = pl.pallas_call(
        write_kernel,
        out_shape=shapes(
            tokens, tokens, wide, wide, square, narrow, square, square, narrow, square, wide, wide, wide,
            tall, wide, tall, wide,
        ),
        in_specs=[vmem] * 6,
        out_specs=[vmem] * 17,
        name="write",
    )(*results)
    ends = {0: (2, 1, 128, 1024), 1: (2, 1, 128, 1024)}
    flat = (2, 3, 5, 8, 10, 11, 12, 14, 16)
    return tuple(
        out.reshape(ends[i]) if i in ends else (out.reshape(-1) if i in flat else out)
        for i, out in enumerate(outs)
    )


def solution(mesh):
    tokens = P(None, "seq", "ctx", None)
    matrix = P(("seq", "ctx"), "head")
    return jax.shard_map(
        on_device,
        mesh=mesh,
        in_specs=(
            tokens, P(), P(), matrix, P("head"), matrix, matrix, P("head"), matrix, P(), P(), P(),
            matrix, P("head"), matrix, P(), P(None, "seq", "ctx"), tokens,
        ),
        out_specs=(
            tokens, tokens, P(), P(), matrix, P("head"), matrix, matrix, P("head"), matrix, P(), P(),
            P(), matrix, P("head"), matrix, P(),
        ),
        check_vma=False,
    )
```

```python
import jax
import jax.numpy as jnp
from jax import lax
from jax.experimental import pallas as pl
from jax.experimental.pallas import tpu as pltpu
from jax.sharding import PartitionSpec as P

F32 = jnp.float32
BF16 = jnp.bfloat16
MESH = pl.DeviceIdType.MESH
VMEM_BYTES = 56 * 1024 * 1024
KEYS = 512
COPIES = 121
SENDS = 18


def dot(left, right, dim_left, dim_right):
    return lax.dot_general(
        left, right, (((dim_left,), (dim_right,)), ((), ())), preferred_element_type=F32
    )


def turn(index, by):
    return lax.rem(index + by, 4)


class Place:
    def __init__(self):
        self.seq = lax.axis_index("seq")
        self.ctx = lax.axis_index("ctx")
        self.z = lax.axis_index("head")
        self.core = lax.rem(self.ctx, 2)
        self.y = lax.rem(lax.div(self.ctx, 2), 4)
        self.low = lax.div(self.ctx, 8)
        self.x = self.seq * 2 + self.low
        self.x_plus = self.at(turn(self.x, 1), self.y, self.core, self.z)
        self.x_minus = self.at(turn(self.x, 3), self.y, self.core, self.z)
        self.y_plus = self.at(self.x, turn(self.y, 1), self.core, self.z)
        self.y_minus = self.at(self.x, turn(self.y, 3), self.core, self.z)
        self.z_plus = self.at(self.x, self.y, self.core, turn(self.z, 1))
        self.z_minus = self.at(self.x, self.y, self.core, turn(self.z, 3))
        self.x_across = self.at(turn(self.x, 2), self.y, self.core, self.z)
        self.y_across = self.at(self.x, turn(self.y, 2), self.core, self.z)
        self.z_across = self.at(self.x, self.y, self.core, turn(self.z, 2))
        self.x_ring = (self.x, (self.x_plus, self.x_minus, self.x_across))
        self.y_ring = (self.y, (self.y_plus, self.y_minus, self.y_across))
        self.z_ring = (self.z, (self.z_plus, self.z_minus, self.z_across))
        self.sibling = self.at(self.x, self.y, 1 - self.core, self.z)
        self.pair = self.at(self.seq * 2 + 1 - self.low, self.y, self.core, self.z)

    def at(self, x, y, core, z):
        return (lax.div(x, 2), (lax.rem(x, 2) * 4 + y) * 2 + core, z)

    def greet(self, partners):
        barrier = pltpu.get_barrier_semaphore()
        for partner in partners:
            pl.semaphore_signal(barrier, inc=1, device_id=partner, device_id_type=MESH)
        pl.semaphore_wait(barrier, len(partners))


class Copy:
    def __init__(self, net, made, index):
        self.net, self.made, self.index = net, made, index

    def wait_recv(self):
        self.made.wait_recv()

    def wait_send(self):
        self.made.wait_send()
        self.net.free.append(self.index)

    def wait(self):
        self.wait_send()
        self.wait_recv()


class Net:
    def __init__(self, send, recv):
        self.send, self.recv, self.used, self.free, self.most = send, recv, 0, [], 0

    def copy(self, src, dst, device):
        index = self.free.pop() if self.free else self.most
        self.most = max(self.most, index + 1)
        made = pltpu.make_async_remote_copy(
            src_ref=src,
            dst_ref=dst,
            send_sem=self.send.at[index],
            recv_sem=self.recv.at[self.used],
            device_id=device,
            device_id_type=MESH,
        )
        self.used += 1
        made.start()
        return Copy(self, made, index)

    def copies(self, each, whole):
        index = self.free.pop() if self.free else self.most
        self.most = max(self.most, index + 1)
        sems = {"send_sem": self.send.at[index], "recv_sem": self.recv.at[self.used]}
        self.used += 1
        for src, dst, device in each:
            pltpu.make_async_remote_copy(
                src_ref=src, dst_ref=dst, device_id=device, device_id_type=MESH, **sems
            ).start()
        made = pltpu.make_async_remote_copy(
            src_ref=whole, dst_ref=whole, device_id=each[0][2], device_id_type=MESH, **sems
        )
        return [Copy(self, made, index)]


def run(steps):
    for _ in steps:
        pass


FROM = (3, 1, 2)
TO = (1, 3, 2)


def add_into(view, *others):
    value = view[...].astype(F32)
    for other in others:
        value = value + other[...].astype(F32)
    view[...] = value.astype(BF16)


class Gather:
    def __init__(self, net, region, ring, apart=False):
        self.here, others = ring
        own = region(self.here)
        self.region, self.apart = region, apart
        if apart:
            self.copies = [net.copy(own, own, device) for device in others]
        else:
            self.copies = net.copies([(own, own, device) for device in others], region(slice(0, 3)))

    def arrivals(self):
        for copy, step in zip(self.copies, FROM):
            copy.wait_recv()
            yield self.region(turn(self.here, step))

    def sent(self):
        for copy in self.copies:
            copy.wait_send()

    def finish(self):
        for copy in self.copies:
            copy.wait()


class Scatter:
    def __init__(self, net, part, slots, ring):
        here, others = ring
        self.copies = net.copies(
            [
                (part(turn(here, step)), slots.at[index], device)
                for index, (step, device) in enumerate(zip(TO, others))
            ],
            slots,
        )

    def finish(self):
        for copy in self.copies:
            copy.wait()


TOP, LOW = slice(0, 16), slice(16, 32)


def gather_plane(net, at, full, urgent=False, around=None):
    x, y, core = at.x, at.y, at.core
    done = []

    def share(view):
        done.append(net.copy(view, view, at.sibling))

    a = Gather(net, lambda j: full.at[j, y, core, TOP, :], at.x_ring)
    b = Gather(net, lambda j: full.at[x, j, core, LOW, :], at.y_ring)
    yield
    a.finish()
    a = Gather(net, lambda j: full.at[:, j, core, TOP, :], at.y_ring, urgent)
    b.finish()
    b = Gather(net, lambda j: full.at[j, :, core, LOW, :], at.x_ring, urgent)
    if urgent:
        share(full.at[:, y, core, TOP, :])
        share(full.at[x, :, core, LOW, :])
    yield
    if urgent:
        for one, two in zip(a.arrivals(), b.arrivals()):
            share(one)
            share(two)
        a.sent()
        b.sent()
    else:
        a.finish()
        b.finish()
        if around is None:
            share(full.at[:, :, core])
        else:
            steps = Gather(net, lambda j: around.at[j, :, :, core], at.z_ring)
            yield
            steps.finish()
            share(around.at[:, :, :, core])
    yield
    for copy in done:
        copy.wait()


def scatter_plane(net, at, partial, other, total, wide, thin, result):
    x, y, core = at.x, at.y, at.core
    shared = net.copy(partial.at[:, :, 1 - core], other, at.sibling)
    yield
    shared.wait()

    def add(index, carry):
        i, j = lax.div(index, 4), lax.rem(index, 4)
        total[i, j] = (partial[i, j, core].astype(F32) + other[i, j].astype(F32)).astype(BF16)
        return carry

    lax.fori_loop(0, 16, add, 0)
    a = Scatter(net, lambda j: total.at[:, j, TOP, :], wide.at[0], at.y_ring)
    b = Scatter(net, lambda j: total.at[j, :, LOW, :], wide.at[1], at.x_ring)
    yield
    a.finish()
    add_into(total.at[:, y, TOP, :], wide.at[0, 0], wide.at[0, 1], wide.at[0, 2])
    a = Scatter(net, lambda j: total.at[j, y, TOP, :], thin.at[0], at.x_ring)
    b.finish()
    add_into(total.at[x, :, LOW, :], wide.at[1, 0], wide.at[1, 1], wide.at[1, 2])
    b = Scatter(net, lambda j: total.at[x, j, LOW, :], thin.at[1], at.y_ring)
    yield
    for index, steps, rows in ((0, a, TOP), (1, b, LOW)):
        steps.finish()
        extra = thin[index, 0].astype(F32) + thin[index, 1].astype(F32) + thin[index, 2].astype(F32)
        result(rows, total[x, y, rows, :].astype(F32) + extra)


def sum_small(net, at, by_x, by_y, by_z, urgent):
    x, y, z, core = at.x, at.y, at.z, at.core
    steps = Gather(net, lambda j: by_x.at[j], at.x_ring)
    yield
    steps.finish()
    by_y[y, core] = by_x[0] + by_x[1] + by_x[2] + by_x[3]
    own = by_y.at[y, core]
    if urgent:
        copies = [net.copy(own, own, device) for device in at.y_ring[1] + (at.sibling,)]
        copies = copies + [net.copy(own, own, at.at(x, turn(y, step), 1 - core, z)) for step in TO]
        yield
        for copy in copies:
            copy.wait()
    else:
        steps = Gather(net, lambda j: by_y.at[j, core], at.y_ring)
        yield
        steps.finish()
        view = by_y.at[:, core]
        copy = net.copy(view, view, at.sibling)
        yield
        copy.wait()
    total = by_y[0, 0] + by_y[0, 1]
    for i in range(1, 4):
        total = total + by_y[i, 0] + by_y[i, 1]
    by_z[z] = total
    steps = Gather(net, lambda j: by_z.at[j], at.z_ring)
    yield
    steps.finish()


def plane_scratch(width):
    return [
        pltpu.VMEM((4, 4, 2, 32, width), BF16),
        pltpu.VMEM((4, 4, 32, width), BF16),
        pltpu.VMEM((4, 4, 32, width), BF16),
        pltpu.VMEM((2, 3, 4, 16, width), BF16),
        pltpu.VMEM((2, 3, 16, width), BF16),
    ]


def norm_parts(value):
    center = value - jnp.mean(value, axis=-1, keepdims=True)
    rate = lax.rsqrt(jnp.mean(center * center, axis=-1, keepdims=True) + 1e-05)
    return center * rate, rate


def norm_back(grad, unit, rate, gain):
    inner = grad * gain
    even = jnp.mean(inner, axis=-1, keepdims=True)
    along = jnp.mean(inner * unit, axis=-1, keepdims=True)
    return rate * (inner - even - unit * along)


def column_sum(value):
    return jnp.sum(value, axis=0, keepdims=True)


def slope_of(at):
    by_z = jnp.where(at.z == 0, 1.0, jnp.where(at.z == 1, 0.25, jnp.where(at.z == 2, 0.0625, 0.015625)))
    by_y = jnp.where(at.y == 0, 2.0**-0.5, jnp.where(at.y == 1, 0.5, jnp.where(at.y == 2, 2.0**-1.5, 0.25)))
    return by_z.astype(F32) * by_y.astype(F32)


def fill_distance(first_query, dist, base, chunks, lanes, start):
    def fill(block, carry):
        lane = lax.broadcasted_iota(jnp.int32, (256, 128), 1)
        query = (lane + first_query).astype(F32)
        key = (lax.broadcasted_iota(jnp.int32, (256, 128), 0) + block * 256).astype(F32)
        apart = query - key
        value = jnp.where((key >= start) & (apart >= 0.0), apart, -1.0)
        rows = pl.ds(pl.multiple_of(base + block * 256, 256), 256)
        dist[rows, lanes] = value
        return carry

    lax.fori_loop(0, chunks * 2, fill, 0)


def masked_scores(keys, queries, dist, slope):
    raw = dot(keys, queries, 1, 0) * 0.125
    return jnp.where(dist >= 0.0, raw - slope * dist, -1000000000.0)


def key_block(kvq, block):
    low, y = block // 2, (block % 2) * 2
    return kvq[low, y : y + 2, :, 0:128, :].reshape(KEYS, 128)


class Chips:
    def __init__(self, at):
        self.steps = []
        for dx in range(2):
            for dy in range(4):
                if dx or dy:
                    low = 1 - at.low if dx else at.low
                    y = turn(at.y, dy)
                    device = at.at(at.seq * 2 + low, y, at.core, at.z)
                    source = (low, turn(at.y, 4 - dy))
                    self.steps.append((low, y, device, source))

    def swap(self, net, src, dst):
        return [(net.copy(src.at[low, y], dst, device), source) for low, y, device, source in self.steps]


def join_tiles(tiles, first):
    rows = [
        jnp.concatenate([tiles[i, j, first : first + 64, :].astype(F32) for j in range(4)], axis=0).T
        for i in range(2)
    ]
    return jnp.concatenate(rows, axis=0).astype(BF16)


def pad_heads(tiles, n, first, above):
    i, j = n // 2, (n % 2) * 2
    wide = [tiles[i, j + k, first : first + 64, :].astype(F32) for k in range(2)]
    wide = jnp.concatenate(wide, axis=1)
    both = [wide, jnp.zeros((64, 256), F32)]
    return jnp.concatenate(both if above else both[::-1], axis=0).astype(BF16)


def layer_kernel(
    x_ref, dy_ref, seg_ref, gain1_ref, shift1_ref, wq_ref, qb_ref, wk_ref, wv_ref, vb_ref, wo_ref, ob_ref,
    gain2_ref, shift2_ref, wu_ref, ub_ref, wd_ref, db_ref,
    bo_ref, dxin_ref, dqkv_ref, dwo_ref, dud_ref, sums_ref,
    w1, wo, wu, wd, seg_all, h1_ref, unit1,
    kvq_send, kvq, o_send, o_all, do_send, do_all, sums_kv, kv_out, kv_in, back_send, own_all, dist, score, dp_ref,
    o_out, o_in, do_out, do_in, part, slots, gathered, dg, g_ref, du_ref, gx, gy, gz, hx, hy, hz,
    dw1, other1, total1, wide1, thin1,
    dwo_part, other_o, total_o, wide_o, thin_o,
    dwu_part, other_u, total_u, wide_u, thin_u,
    dwd_part, other_d, total_d, wide_d, thin_d,
    send, recv,
):
    at = Place()
    net = Net(send, recv)
    chips = Chips(at)
    x, y, z, core, low = at.x, at.y, at.z, at.core, at.low
    partners = at.x_ring[1] + at.y_ring[1] + at.z_ring[1] + (at.sibling,)
    partners = partners + tuple(at.at(x, turn(y, step), 1 - core, z) for step in TO)
    partners = partners + tuple(
        at.at(at.seq * 2 + 1 - low, turn(y, step), core, z) for step in TO
    )
    at.greet(partners)

    mine = w1.at[x, y, core]
    mine[:, 0:256] = wq_ref[...]
    mine[:, 256:512] = wk_ref[...]
    mine[:, 512:768] = wv_ref[...]
    w1_steps = gather_plane(net, at, w1, urgent=True)
    next(w1_steps)
    wo[z, x, y, core] = wo_ref[...]
    wo_steps = gather_plane(net, at, wo.at[z], around=wo)
    next(wo_steps)
    seg_all[low, y, core] = jnp.concatenate([seg_ref[...]] * 4, axis=0)
    seg = Gather(net, lambda j: seg_all.at[low, j, core], at.y_ring)
    wu[x, y, core] = wu_ref[...]
    wd[x, y, core] = wd_ref[...]
    unit, _ = norm_parts(x_ref[...].reshape(256, 1024).astype(F32))
    unit1[...] = unit
    h1_ref[...] = (unit * gain1_ref[...] + shift1_ref[...]).astype(BF16)
    next(w1_steps)
    seg.finish()
    view = seg_all.at[low, :, core]
    seg_pair = net.copy(view, view, at.pair)
    next(w1_steps)
    next(wo_steps)
    wd_steps = gather_plane(net, at, wd)
    next(wd_steps)
    seg_pair.wait()
    view = seg_all.at[:, :, core]
    seg_share = net.copy(view, view, at.sibling)
    run(w1_steps)

    h1 = h1_ref[...]
    wide = dot(h1, w1[...].reshape(1024, 768), 1, 0)
    turned = (wide[:, 0:256] + qb_ref[...]).T.astype(BF16)
    keys, values = wide[:, 256:512], wide[:, 512:768] + vb_ref[...]
    for i in range(2):
        for j in range(4):
            rows, lanes = slice(i * 128, i * 128 + 128), slice(j * 64, j * 64 + 64)
            tile = jnp.concatenate([keys[rows, lanes], values[rows, lanes]], axis=1)
            kvq_send[i, j, 0:128, :] = tile.astype(BF16)
            kvq_send[i, j, 128:192, :] = turned[lanes, rows]
    kv_copies = chips.swap(net, kvq_send, kvq.at[low, y, core])
    kvq[low, y, core] = kvq_send[low, y]
    shares = []
    seg_share.wait()
    counts = []
    for number in range(1, 4):
        below = (seg_all[:, :, :, 0:2, :] < number).astype(F32)
        below = jnp.sum(below.reshape(16, 2, 128), axis=0)
        below = jnp.sum(below, axis=-1, keepdims=True)
        counts.append(jnp.where(low == 0, below[0:1], below[1:2]))
    bases = [0, 512, 1536, 3072]
    for n in range(4):
        for k in range(2):
            there = seg_all[n // 2, (n % 2) * 2 + k, core]
            there = jnp.where(low == 0, there[0:1], there[1:2])
            found = jnp.zeros((1, 128), F32)
            for number in range(1, 4):
                found = jnp.where(there == number, counts[number - 1], found)
            first_query = (n * 4 + k * 2 + core) * 128
            fill_distance(
                first_query, dist, bases[n], n + 1, slice(k * 128, k * 128 + 128), found
            )
    next(wo_steps)
    for index, (copy, source) in enumerate(kv_copies):
        copy.wait_recv()
        if index == 2:
            view = kvq.at[low, :, core, 0:128, :]
            shares.append(net.copy(view, view, at.sibling))
        if index > 2:
            view = kvq.at[source[0], source[1], core, 0:128, :]
            shares.append(net.copy(view, view, at.sibling))
    for copy, _ in kv_copies:
        copy.wait_send()
    wu_steps = gather_plane(net, at, wu)
    next(wu_steps)
    next(wd_steps)
    for copy in shares:
        copy.wait()

    slope = slope_of(at)
    for n in range(4):
        queries = pad_heads(kvq.at[:, :, core], n, 128, True)
        top = jnp.full((1, 256), -3.0e38, F32)
        for block in range(n + 1):
            rows = slice(block * KEYS, block * KEYS + KEYS)
            value = masked_scores(
                key_block(kvq, block), queries,
                dist[bases[n] + block * KEYS : bases[n] + block * KEYS + KEYS, :], slope,
            )
            score[rows, :] = value
            top = jnp.maximum(top, jnp.max(value, axis=0, keepdims=True))
        summed = jnp.zeros((1, 256), F32)
        for block in range(n + 1):
            rows = slice(block * KEYS, block * KEYS + KEYS)
            value = jnp.exp(score[rows, :] - top)
            score[rows, :] = value
            summed = summed + column_sum(value)
        scale = 1.0 / summed
        mixed = jnp.zeros((128, 256), F32)
        for block in range(n + 1):
            rows = slice(block * KEYS, block * KEYS + KEYS)
            probs = score[rows, :] * scale
            dist[bases[n] + block * KEYS : bases[n] + block * KEYS + KEYS, :] = probs
            mixed = mixed + dot(key_block(kvq, block), probs.astype(BF16), 0, 0)
        for k in range(2):
            lanes = slice(k * 128, k * 128 + 128)
            o_send[n // 2, (n % 2) * 2 + k] = mixed[64:128, lanes].astype(BF16)
    copies = chips.swap(net, o_send, o_all.at[low, y])
    o_all[low, y] = o_send[low, y]
    next(wo_steps)

    def half(h):
        return slice(h * 32, h * 32 + 32)

    def scatter_half(index, h):
        return Scatter(net, lambda j: part.at[index, j, half(h), :], slots.at[index, h], at.z_ring)

    def scatter(index, value):
        part[index] = value.astype(BF16).reshape(4, 64, 1024)
        return [scatter_half(index, 0), scatter_half(index, 1)]

    def owned(index, h):
        extra = slots[index, h, 0].astype(F32) + slots[index, h, 1].astype(F32)
        return part[index, z, half(h), :].astype(F32) + (extra + slots[index, h, 2].astype(F32))

    def gather(buffer, h):
        return Gather(net, lambda j: buffer.at[j, half(h), :], at.z_ring)

    def put_sums(to, sums):
        for i in range(8):
            for j, value in enumerate(sums):
                to[x, i : i + 1, j * 128 : j * 128 + 128] = value[:, i * 128 : i * 128 + 128]

    def put_grad(to, first, width, left, right):
        for i in range(4):
            value = dot(left(i), right, 0, 0).astype(BF16)
            to[i, :, :, :, first : first + width] = value.reshape(4, 2, 32, width)

    next(wu_steps)
    for copy, _ in copies:
        copy.wait()
    mixed = join_tiles(o_all, 0)

    def swap_rows(src, dst):
        dst[z] = src[z]
        return net.copies(
            [
                (src.at[turn(z, step)], dst.at[z], device)
                for step, device in zip(TO, at.z_ring[1])
            ],
            dst.at[0:3],
        )

    o_out[...] = mixed.reshape(4, 64, 256)
    copies = swap_rows(o_out, o_in)
    next(wd_steps)
    run(wo_steps)
    for copy in copies:
        copy.wait()
    added = ob_ref[...]
    for j in range(4):
        added = added + dot(o_in[j], wo[j].reshape(1024, 256), 1, 1)
    x1, units, rates, gathers = [], [], [], []
    for h in range(2):
        x1.append(x_ref[z, half(h), :].astype(F32) + added[half(h), :])
        unit, rate = norm_parts(x1[h])
        gathered[0, z, half(h), :] = (unit * gain2_ref[...] + shift2_ref[...]).astype(BF16)
        gathers.append(gather(gathered.at[0], h))
        units.append(unit)
        rates.append(rate)
        if h == 0:
            next(wu_steps)
    upstream = [dy_ref[z, half(h), :].astype(F32) for h in range(2)]
    dy_sum = column_sum(upstream[0]) + column_sum(upstream[1])
    run(wd_steps)
    down = wd[...].reshape(1024, 1024)
    dg[...] = dot(dy_ref[...].reshape(256, 1024), down, 1, 0).reshape(4, 64, 1024)
    run(wu_steps)
    up = wu[...].reshape(1024, 1024)
    back = []
    for h in range(2):
        gathers[h].finish()
        h2 = gathered[0, :, half(h), :].reshape(128, 1024)
        for i in range(2):
            cols = slice(i * 512, i * 512 + 512)
            u = dot(h2, wu[:, :, :, :, cols].reshape(1024, 512), 1, 0) + ub_ref[:, cols]
            tanh = jnp.tanh(0.7978845608028654 * (u + 0.044715 * u * u * u))
            g_ref[:, half(h), cols] = (0.5 * u * (1.0 + tanh)).astype(BF16).reshape(4, 32, 512)
            turned = 0.5 * u * (1.0 - tanh * tanh) * 0.7978845608028654 * (1.0 + 3 * 0.044715 * u * u)
            turned = (0.5 * (1.0 + tanh) + turned).reshape(4, 32, 512)
            du_ref[:, half(h), cols] = (dg[:, half(h), cols] * turned).astype(BF16)
        value = dot(du_ref[:, half(h), :].reshape(128, 1024), up, 1, 1).astype(BF16)
        part[2, :, half(h), :] = value.reshape(4, 32, 1024)
        back.append(scatter_half(2, h))
    du = du_ref[...].reshape(256, 1024)
    g = g_ref[...].reshape(256, 1024)
    put_grad(
        dwd_part, 0, 1024, lambda i: dy_ref[:, :, i * 256 : i * 256 + 256].reshape(256, 256), g
    )

    def put_d(rows, value):
        dud_ref[rows, 1024:2048] = value

    def put_u(rows, value):
        dud_ref[rows, 0:768] = value

    dwd_steps = scatter_plane(net, at, dwd_part, other_d, total_d, wide_d, thin_d, put_d)
    next(dwd_steps)
    def h2_columns(i):
        return gathered[0, :, :, i * 256 : i * 256 + 256].reshape(256, 256)

    put_grad(dwu_part, 0, 768, h2_columns, du[:, 0:768])
    dwu_steps = scatter_plane(net, at, dwu_part, other_u, total_u, wide_u, thin_u, put_u)
    put_grad(dwo_part, 0, 256, h2_columns, du[:, 768:1024])
    dx1, dh2, gathers = [], [], []
    for h in range(2):
        back[h].finish()
        dh2.append(owned(2, h))
        dx1.append(upstream[h] + norm_back(dh2[h], units[h], rates[h], gain2_ref[...]))
        gathered[1, z, half(h), :] = dx1[h].astype(BF16)
        if h == 0:
            next(dwd_steps)
            next(dwu_steps)
    for j in range(4):
        do_out[j] = dot(gathered[1, z], wo[j].reshape(1024, 256), 1, 0).astype(BF16)
    copies = swap_rows(do_out, do_in)
    gathers = [gather(gathered.at[1], 0), gather(gathered.at[1], 1)]
    early_sums = (
        column_sum(dx1[0]) + column_sum(dx1[1]),
        column_sum(dh2[0] * units[0]) + column_sum(dh2[1] * units[1]),
        column_sum(dh2[0]) + column_sum(dh2[1]),
        dy_sum,
        column_sum(du.astype(F32)),
    )
    put_sums(gx, early_sums)
    early = sum_small(net, at, gx, gy, gz, False)
    next(early)
    ffn = dot(g, down, 1, 1)
    for copy in copies:
        copy.wait()
    grads = do_in[...].reshape(256, 256).astype(F32).T.astype(BF16)
    for i in range(2):
        for j in range(4):
            do_send[i, j] = grads[j * 64 : j * 64 + 64, i * 128 : i * 128 + 128]
    copies = chips.swap(net, do_send, do_all.at[low, y])
    do_all[low, y] = do_send[low, y]
    front = scatter(1, ffn)
    def put_o(rows, value):
        dud_ref[rows, 768:1024] = value[:, 0:256]
        dwo_ref[rows, :] = value[:, 256:512]

    for copy, _ in copies:
        copy.wait()
    next(dwd_steps)
    next(dwu_steps)
    next(early)

    shared = []
    lane = lax.broadcasted_iota(jnp.int32, (1, 1, 1, 128), 3)
    scale = jnp.where(lane < 64, 0.125, 1.0).astype(F32)
    scale = scale.reshape(1, 1, 128)
    for n in (3, 2, 1, 0):
        queries = pad_heads(kvq.at[:, :, core], n, 128, True)
        grads = pad_heads(do_all, n, 0, False)
        right = jnp.concatenate([queries, grads], axis=1)
        inner = jnp.zeros((1, 256), F32)
        for block in range(n + 1):
            rows = slice(block * KEYS, block * KEYS + KEYS)
            probs = dist[bases[n] + block * KEYS : bases[n] + block * KEYS + KEYS, :]
            prob_grad = dot(key_block(kvq, block), grads, 1, 0)
            dp_ref[rows, :] = prob_grad
            inner = inner + column_sum(probs * prob_grad)
        query_grad = jnp.zeros((128, 256), F32)
        for block in range(n + 1):
            rows = slice(block * KEYS, block * KEYS + KEYS)
            probs = dist[bases[n] + block * KEYS : bases[n] + block * KEYS + KEYS, :]
            score_grad = (probs * (dp_ref[rows, :] - inner)).astype(BF16)
            both = jnp.concatenate([score_grad, probs.astype(BF16)], axis=1)
            i, j = block // 2, (block % 2) * 2
            value = dot(both, right, 1, 1).reshape(2, 2, 128, 128)
            if n < 3:
                value = value + sums_kv[i, j : j + 2]
            sums_kv[i, j : j + 2] = value
            query_grad = query_grad + dot(key_block(kvq, block), score_grad, 0, 0)
        query_grad = (query_grad * 0.125).astype(BF16)
        for k in range(2):
            lanes = slice(k * 128, k * 128 + 128)
            back_send[n // 2, (n % 2) * 2 + k, 128:192, :] = query_grad[0:64, lanes]
        i, chunk = n // 2, slice((n % 2) * 2, (n % 2) * 2 + 2)
        kv_out[i, chunk] = (sums_kv[i, chunk, 1 - core] * scale).astype(BF16)
        shared.append(net.copy(kv_out.at[i, chunk], kv_in.at[i, chunk], at.sibling))
        if n == 3:
            for steps in gathers:
                steps.finish()
            put_grad(
                dwo_part, 256, 256,
                lambda i: gathered[1, :, :, i * 256 : i * 256 + 256].reshape(256, 256), mixed,
            )
            dwo_steps = scatter_plane(net, at, dwo_part, other_o, total_o, wide_o, thin_o, put_o)
            next(dwo_steps)

    for copy in shared:
        copy.wait()
    back_send[:, :, 0:128, :] = (sums_kv[:, :, core] * scale + kv_in[...].astype(F32)).astype(BF16)
    kv_copies = chips.swap(net, back_send, own_all.at[low, y])
    own_all[low, y] = back_send[low, y]
    run(dwd_steps)
    outs = []
    for h in range(2):
        front[h].finish()
        bo_ref[z, half(h), :] = (x1[h] + owned(1, h) + db_ref[...]).astype(BF16)
        outs.append(gather(bo_ref, h))
    h1 = h1_ref[...]

    def left(i):
        return h1[:, i * 256 : i * 256 + 256]

    for copy, _ in kv_copies:
        copy.wait()
    next(dwo_steps)
    dq = join_tiles(own_all, 128)
    whole = []
    for i in range(2):
        tiles = [own_all[i, j, 0:128, :].astype(F32) for j in range(4)]
        keys = [tile[:, 0:64] for tile in tiles]
        values = [tile[:, 64:128] for tile in tiles]
        whole.append(jnp.concatenate(keys + values, axis=1))
    dkv = jnp.concatenate(whole, axis=0).astype(BF16)
    dqkv = jnp.concatenate([dq, dkv], axis=1)
    put_grad(dw1, 0, 768, left, dqkv)

    def put1(rows, value):
        dqkv_ref[rows, :] = value

    dw1_steps = scatter_plane(net, at, dw1, other1, total1, wide1, thin1, put1)
    next(dw1_steps)
    direct = dot(dqkv, w1[...].reshape(1024, 768), 1, 1)
    steps = scatter(3, direct)
    gain_sum, shift_sum = column_sum(direct * unit1[...]), column_sum(direct)
    query_sum, value_sum = column_sum(dq.astype(F32)), column_sum(dkv[:, 256:512].astype(F32))
    bias_sum = jnp.concatenate([query_sum, value_sum, jnp.zeros((1, 512), F32)], axis=1)
    put_sums(hx, (gain_sum, shift_sum, bias_sum))
    late = sum_small(net, at, hx, hy, hz, True)
    next(late)
    next(early)
    next(dwu_steps)
    next(dw1_steps)
    next(late)
    next(early)
    gathers = []
    for h in range(2):
        steps[h].finish()
        unit, rate = norm_parts(x_ref[z, half(h), :].astype(F32))
        grad = dx1[h] + norm_back(owned(3, h), unit, rate, gain1_ref[...])
        dxin_ref[z, half(h), :] = grad.astype(BF16)
        gathers.append(gather(dxin_ref, h))
    next(late)
    next(dwo_steps)
    next(dw1_steps)
    run(dwu_steps)
    run(dwo_steps)
    run(dw1_steps)
    run(early)
    run(late)
    early_over = gz[0, :, 0:512] + gz[1, :, 0:512] + gz[2, :, 0:512] + gz[3, :, 0:512]
    late_over = hz[0, :, 0:256] + hz[1, :, 0:256] + hz[2, :, 0:256] + hz[3, :, 0:256]
    for i in range(8):
        lanes = slice(i * 128, i * 128 + 128)
        for j in range(2):
            sums_ref[j : j + 1, lanes] = late_over[i : i + 1, j * 128 : j * 128 + 128]
        for j in range(4):
            sums_ref[j + 2 : j + 3, lanes] = early_over[i : i + 1, j * 128 : j * 128 + 128]
        sums_ref[6:7, lanes] = gz[z, i : i + 1, 512:640]
        sums_ref[7:8, lanes] = hz[z, i : i + 1, 256:384]
    for steps in outs + gathers:
        steps.finish()


def write_kernel(
    bo_ref, dxin_ref, dqkv_ref, dwo_ref, dud_ref, sums_ref,
    block_ref, input_ref, g1_ref, s1_ref, dwq_ref, qb_ref, dwk_ref, dwv_ref, vb_ref, out_ref,
    ob_ref, g2_ref, s2_ref, dwu_ref, ub_ref, dwd_ref, db_ref,
):
    block_ref[...] = bo_ref[...].astype(F32)
    input_ref[...] = dxin_ref[...].astype(F32)
    dwq_ref[...] = dqkv_ref[:, 0:256]
    dwk_ref[...] = dqkv_ref[:, 256:512]
    dwv_ref[...] = dqkv_ref[:, 512:768]
    out_ref[...] = dwo_ref[...]
    dwu_ref[...] = dud_ref[:, 0:1024]
    dwd_ref[...] = dud_ref[:, 1024:2048]
    for index, ref in enumerate((g1_ref, s1_ref, ob_ref, g2_ref, s2_ref, db_ref, ub_ref)):
        ref[...] = sums_ref[index : index + 1, :]
    qb_ref[...] = sums_ref[7:8, 0:256]
    vb_ref[...] = sums_ref[7:8, 256:512]


def on_device(
    block_input, first_gain, first_shift, query_weight, query_bias, key_weight, value_weight, value_bias,
    output_weight, output_bias, second_gain, second_shift, up_weight, up_bias, down_weight, down_bias,
    segments, out_cotangent,
):
    vmem = pl.BlockSpec(memory_space=pltpu.VMEM)

    def row(value):
        return value.reshape(1, -1)

    def shapes(*pairs):
        return [jax.ShapeDtypeStruct(shape, kind) for shape, kind in pairs]

    results = pl.pallas_call(
        layer_kernel,
        out_shape=shapes(
            ((4, 64, 1024), BF16),
            ((4, 64, 1024), BF16),
            ((32, 768), F32),
            ((32, 256), F32),
            ((32, 2048), F32),
            ((8, 1024), F32),
        ),
        in_specs=[vmem] * 18,
        out_specs=[vmem] * 6,
        scratch_shapes=[
            pltpu.VMEM((4, 4, 2, 32, 768), BF16),
            pltpu.VMEM((4, 4, 4, 2, 32, 256), BF16),
            pltpu.VMEM((4, 4, 2, 32, 1024), BF16),
            pltpu.VMEM((4, 4, 2, 32, 1024), BF16),
            pltpu.VMEM((2, 4, 2, 8, 128), jnp.int32),
            pltpu.VMEM((256, 1024), BF16),
            pltpu.VMEM((256, 1024), F32),
            pltpu.VMEM((2, 4, 192, 128), BF16),
            pltpu.VMEM((2, 4, 2, 192, 128), BF16),
            *[pltpu.VMEM((2, 4, 64, 128), BF16)] * 4,
            pltpu.VMEM((2, 4, 2, 128, 128), F32),
            *[pltpu.VMEM((2, 4, 128, 128), BF16)] * 2,
            *[pltpu.VMEM((2, 4, 192, 128), BF16)] * 2,
            pltpu.VMEM((5120, 256), F32),
            pltpu.VMEM((2048, 256), F32),
            pltpu.VMEM((2048, 256), F32),
            *[pltpu.VMEM((4, 64, 256), BF16)] * 4,
            pltpu.VMEM((4, 4, 64, 1024), BF16),
            pltpu.VMEM((4, 2, 3, 32, 1024), BF16),
            pltpu.VMEM((2, 4, 64, 1024), BF16),
            pltpu.VMEM((4, 64, 1024), F32),
            pltpu.VMEM((4, 64, 1024), BF16),
            pltpu.VMEM((4, 64, 1024), BF16),
            pltpu.VMEM((4, 8, 640), F32),
            pltpu.VMEM((4, 2, 8, 640), F32),
            pltpu.VMEM((4, 8, 640), F32),
            pltpu.VMEM((4, 8, 384), F32),
            pltpu.VMEM((4, 2, 8, 384), F32),
            pltpu.VMEM((4, 8, 384), F32),
            *plane_scratch(768),
            *plane_scratch(512),
            *plane_scratch(768),
            *plane_scratch(1024),
            pltpu.SemaphoreType.DMA((SENDS,)),
            pltpu.SemaphoreType.DMA((COPIES,)),
        ],
        compiler_params=pltpu.CompilerParams(
            collective_id=1, has_side_effects=True, vmem_limit_bytes=VMEM_BYTES
        ),
        cost_estimate=pl.CostEstimate(
            flops=10_000_000_000, bytes_accessed=16_000_000, transcendentals=0
        ),
        name="layer",
    )(
        block_input.reshape(4, 64, 1024), out_cotangent.reshape(4, 64, 1024), segments.reshape(2, 128),
        row(first_gain), row(first_shift), query_weight, row(query_bias), key_weight, value_weight,
        row(value_bias), output_weight, row(output_bias), row(second_gain), row(second_shift), up_weight,
        row(up_bias), down_weight, row(down_bias),
    )
    wide, narrow = ((1, 1024), F32), ((1, 256), F32)
    square, tall, tokens = ((32, 256), F32), ((32, 1024), F32), ((4, 64, 1024), F32)
    pairs = (
        tokens, tokens, wide, wide, square, narrow, square, square, narrow, square, wide, wide, wide,
        tall, wide, tall, wide,
    )

    def cut(*block):
        return pl.BlockSpec(block, lambda i: (i,) + (0,) * (len(block) - 1))

    def whole(*block):
        return pl.BlockSpec(block, lambda i: (0,) * len(block))

    outs = pl.pallas_call(
        write_kernel,
        out_shape=shapes(*pairs),
        grid=(2,),
        in_specs=[
            cut(2, 64, 1024), cut(2, 64, 1024), cut(16, 768), cut(16, 256), cut(16, 2048), whole(8, 1024),
        ],
        out_specs=[
            whole(*pair[0]) if pair[0][0] == 1 else cut(pair[0][0] // 2, *pair[0][1:]) for pair in pairs
        ],
        name="write",
    )(*results)
    ends = {0: (2, 1, 128, 1024), 1: (2, 1, 128, 1024)}
    flat = (2, 3, 5, 8, 10, 11, 12, 14, 16)
    return tuple(
        out.reshape(ends[i]) if i in ends else (out.reshape(-1) if i in flat else out)
        for i, out in enumerate(outs)
    )


def solution(mesh):
    tokens = P(None, "seq", "ctx", None)
    matrix = P(("seq", "ctx"), "head")
    return jax.shard_map(
        on_device,
        mesh=mesh,
        in_specs=(
            tokens, P(), P(), matrix, P("head"), matrix, matrix, P("head"), matrix, P(), P(), P(),
            matrix, P("head"), matrix, P(), P(None, "seq", "ctx"), tokens,
        ),
        out_specs=(
            tokens, tokens, P(), P(), matrix, P("head"), matrix, matrix, P("head"), matrix, P(), P(),
            P(), matrix, P("head"), matrix, P(),
        ),
        check_vma=False,
    )
```
